32 devices in a mesh: cases: 2 (over x), bus: 16 (over z, y, core).
Axes of the slice: x: 2, y: 2, z: 4, core: 2. Of those that a mesh axis runs over, the one named last changes fastest.
Arguments:
- ptdf: bfloat16 [20480, 10240], P('bus'), may hold values from -0.078125 to 0.078125
- line_limit: float32 [20480], P('bus'), may hold values from 1 to 8
- gen_cost: float32 [12288], P('bus'), may hold values from 0.1 to 2
- gen_max: float32 [12288], P('bus'), may hold values from 0.5 to 4
- gen_owner: int32 [12288, 1], P('bus'), may hold values from 0 to 15; in each aligned block of 768 rows (0 to 767, 768 to 1535, ...) at most 144 rows name the same one
- gen_local: int32 [12288], P('bus'), may hold values from 0 to 639
- availability: float32 [24576, 128], P(('cases', 'bus')), parts along dimension 0, may hold values from 0 to 1
- demand: float32 [20480, 128], P(('cases', 'bus')), parts along dimension 0, may hold values from 0.5 to 2.5
- dispatch: float32 [24576, 128], P(('cases', 'bus')), parts along dimension 0, may hold values from 0 to 2
- balance_price: float32 [256], P('cases'), parts along dimension 0, may hold values from -6 to 6
- line_price: float32 [40960, 128], P(('cases', 'bus')), parts along dimension 0, may hold values from -4 to 4
Outputs:
- dispatch_out: float32 [24576, 128], P(('cases', 'bus')), parts along dimension 0
- balance_out: float32 [256], P('cases'), parts along dimension 0
- line_out: float32 [40960, 128], P(('cases', 'bus')), parts along dimension 0
The draws below stay inside these ranges and needn't reach their ends.
There are 2 independent parts, one for each index of `cases`. The reference program is written for one: setup_inputs(seed, part) draws one part's arguments, and reference() takes and returns one part's arrays. A program takes and returns all parts, laid end to end along the dimension named above; an argument that names none is the same for every part. Nothing has to cross between parts.
Inputs may be any that keep to these rules, and one draw needn't show every extreme that they name: `gen_owner`: among the 768 generators of one device (aligned blocks of rows), no owner is named more than 144 times, a bound that some block reaches.
All inputs are finite; a program needn't handle non-finite values.
Results may differ from the reference program's by a relative error of at most 0.0036.
Values may be sent and summed in bfloat16 or wider, within the bound.
No kernel may reach another device: no remote copies, remote signals or barrier semaphores. Data moves between devices by JAX's collectives and lax.ppermute only.
A program may use at most 128 MiB of HBM per device.

```python
import math
import jax
import jax.numpy as jnp
import numpy as np
from jax import lax

BUSES = 10240
LINES = 20480
HOURS = 128
GEN_DEV = 768
ITERS = 2
GENS = 12288
BUS_DEV = 640
CAP = 144
N_BUS = 16


def place_ends(result, stream_key, least, largest):
    spot = [jax.random.randint(jax.random.fold_in(stream_key, axis), (), 0, length) for axis, length in enumerate(result.shape)]
    longest = result.shape.index(max(result.shape))
    neighbour = spot[:longest] + [(spot[longest] + 1) % result.shape[longest]] + spot[longest + 1:]
    return result.at[tuple(spot)].set(least).at[tuple(neighbour)].set(largest)


def raised(values, own_key, source, target, parts, factor):
    def block_of(dim):
        return (jnp.arange(values.shape[dim]) // (values.shape[dim] // parts)).reshape((-1,) + (1,) * (values.ndim - 1 - dim))

    near = jax.random.permutation(own_key, parts)[block_of(target)]
    other_side = (block_of(target) + parts // 2) % parts
    return jnp.where((block_of(source) == near) | (block_of(source) == other_side), factor * values, values)


def levels(stream_key, extent, pieces, least, largest):
    def one(axis_at, shards_of):
        heights = jax.random.uniform(jax.random.fold_in(jax.random.fold_in(stream_key, 6), axis_at), (shards_of,), jnp.float32, least / len(pieces), largest / len(pieces))
        return jnp.repeat(jnp.exp(heights), extent[axis_at] // shards_of).reshape((-1,) + (1,) * (len(extent) - axis_at - 1))

    level = one(*pieces[0])
    for cut in pieces[1:]:
        level = level * one(*cut)
    return level


def assign_block(key, own, number, rows, amount, top, most, lean):
    sequence = jax.random.permutation(key, amount)
    packed, usual = shares(amount, rows * top, most, lean, True), shares(amount, rows * top, most, lean, False)
    places = jnp.arange(amount)

    def named(tallies, rotation):
        used = int((tallies > 0).sum())
        fixed = max(1, used // 4)
        passed = fixed + (places - fixed + rotation * (used - fixed)) % max(1, amount - fixed)
        return jnp.zeros((amount,), jnp.int32).at[sequence[jnp.where(places < fixed, places, passed)]].set(jnp.asarray(tallies, jnp.int32))

    tallies = jnp.where(number % 4 == 0, named(packed, number // 4), named(usual, number - number // 4 - 1))
    mixed = jax.random.permutation(jax.random.fold_in(own, 3), amount)
    donor, taker = mixed[0:amount // 2 * 2:2], mixed[1:amount // 2 * 2:2]
    room = jnp.minimum(tallies[donor] - 1, most - tallies[taker]) // 2
    room = jnp.where((donor == sequence[0]) | (taker == sequence[0]) | (tallies[taker] == 0), 0, jnp.maximum(room, 0))
    passed = jax.random.randint(jax.random.fold_in(own, 4), (amount // 2,), 0, 1 << 20) % (room + 1)
    tallies = tallies.at[donor].add(-passed).at[taker].add(passed)
    items = jnp.searchsorted(jnp.cumsum(tallies), jnp.arange(rows * top), side="right").astype(jnp.int32)
    listing = items.reshape(top, rows).T
    listing = listing[jax.random.permutation(jax.random.fold_in(own, 1), rows)]
    rotation = jax.random.randint(jax.random.fold_in(own, 2), (rows, 1), 0, top)
    return jnp.take_along_axis(listing, (jnp.arange(top)[None, :] + rotation) % top, axis=1)


def shares(count, total, bound, skew, full):
    weights = [(1 << 20) // math.isqrt(standing ** skew) + 1 for standing in range(1, count + 1)]
    largest = bound if full else min(bound, max(-(-total // count), total * weights[0] // sum(weights)))
    least = 1 if total - largest >= count - 1 else 0
    counts, rest = [largest] + [least] * (count - 1), total - largest - least * (count - 1)
    while rest > 0:
        candidates = [i for i in range(1, count) if counts[i] < largest] or [i for i in range(1, count) if counts[i] < bound]
        whole, left = sum([weights[i] for i in candidates]), rest
        for i in candidates:
            addition = min(bound - counts[i], max(1, left * weights[i] // whole), rest)
            counts[i] = counts[i] + addition
            rest = rest - addition
    return np.array(counts)


def normal_values(rng, dims, scale, most, pieces=(), kind=jnp.bfloat16):
    result = scale * jax.random.normal(rng, dims, jnp.float32)
    if pieces:
        result = result * levels(rng, dims, pieces, -0.22, 0.18)
    return jnp.clip(result, -most, most).astype(kind)


def heavy_noise(rng, extent, scale, most, cuts, heavy, held_as=jnp.bfloat16):
    entries = scale * jax.random.normal(rng, extent, jnp.float32)
    if cuts:
        entries = entries * levels(rng, extent, cuts, -0.22, 0.18)
    return jnp.clip(raised(entries, jax.random.fold_in(rng, 3), *heavy), -most, most).astype(held_as)


def setup_inputs(seed: int = 0, part: int = 0) -> dict:
    key_list = jax.random.split(jax.random.key(seed), 12)
    own_keys = jax.random.split(jax.random.fold_in(key_list[11], part), 12)
    ptdf = heavy_noise(key_list[0], (LINES, BUSES), BUSES ** -0.5, 0.078125, ((0, 16),), (0, 1, 16, 2.0))
    line_limit = jnp.clip(jnp.exp(math.log(8.0) - 2.0794415 * jax.random.uniform(key_list[1], (LINES,), jnp.float32) ** levels(key_list[1], (LINES,), ((0, 16),), -0.2, 0.2)), 1.0, 8.0)
    gen_cost = jnp.clip(jnp.exp(math.log(2.0) - 2.9957323 * jax.random.uniform(key_list[2], (GENS,), jnp.float32) ** levels(key_list[2], (GENS,), ((0, 16),), -0.2, 0.2)), 0.1, 2.0)
    gen_max = jnp.clip(jnp.exp(math.log(4.0) - 2.0794415 * jax.random.uniform(key_list[3], (GENS,), jnp.float32) ** levels(key_list[3], (GENS,), ((0, 16),), -0.2, 0.2)), 0.5, 4.0)
    gen_owner_keys = jax.random.split(jax.random.fold_in(key_list[4], 1), GENS // GEN_DEV)
    gen_owner_turns = jax.random.permutation(jax.random.fold_in(key_list[4], 3), GENS // GEN_DEV)
    gen_owner = jax.vmap(lambda own, number: assign_block(jax.random.fold_in(key_list[4], 2), own, number, GEN_DEV, N_BUS, 1, CAP, 2))(gen_owner_keys, gen_owner_turns).reshape((GENS, 1))
    gen_local = place_ends(jax.random.randint(key_list[5], (GENS,), 0, BUS_DEV), jax.random.fold_in(key_list[5], 1), 0, BUS_DEV - 1).astype(jnp.int32)
    availability = jnp.clip(1.0 * jax.random.uniform(own_keys[6], (GENS, HOURS), jnp.float32) ** levels(own_keys[6], (GENS, HOURS), ((0, 16),), -0.2, 0.2), 0.0, 1.0)
    demand = jnp.clip(0.5 + 2.0 * jax.random.uniform(own_keys[7], (BUSES, HOURS), jnp.float32) ** levels(own_keys[7], (BUSES, HOURS), ((0, 16),), -0.2, 0.2), 0.5, 2.5)
    dispatch = jnp.clip(2.0 * jax.random.uniform(own_keys[8], (GENS, HOURS), jnp.float32) ** levels(own_keys[8], (GENS, HOURS), ((0, 16),), -0.2, 0.2), 0.0, 2.0)
    balance_price = normal_values(own_keys[9], (HOURS,), 1.0, 6.0, (), jnp.float32)
    line_price = normal_values(own_keys[10], (LINES, HOURS), 0.5, 4.0, ((0, 16),), jnp.float32)
    return dict(ptdf=ptdf, line_limit=line_limit, gen_cost=gen_cost, gen_max=gen_max, gen_owner=gen_owner, gen_local=gen_local, availability=availability, demand=demand, dispatch=dispatch, balance_price=balance_price, line_price=line_price)


tau_step = 0.2
sigma_step = 0.15


def reference(ptdf, line_limit, gen_cost, gen_max, gen_owner, gen_local, availability, demand, dispatch, balance_price, line_price):
    bus_count = BUSES // N_BUS
    gen_bus = (gen_owner[:, 0] * bus_count + gen_local).astype(jnp.int32)
    upper = gen_max[:, None] * availability
    limit = line_limit[:, None]
    for iteration in range(ITERS):
        line_half = line_price.astype(jnp.bfloat16)
        shadow = lax.dot_general(ptdf, line_half, (((0,), (0,)), ((), ())), preferred_element_type=jnp.float32)
        price = shadow[gen_bus] + balance_price[None, :]
        updated = jnp.clip(dispatch - tau_step * (gen_cost[:, None] + price), 0.0, upper)
        extra = 2.0 * updated - dispatch
        injection = jax.ops.segment_sum(extra, gen_bus, num_segments=BUSES) - demand
        balance = jnp.sum(injection, axis=0)
        balance_price = balance_price + sigma_step * balance / BUSES
        flow = jnp.dot(ptdf, injection.astype(jnp.bfloat16), preferred_element_type=jnp.float32)
        shifted = line_price + sigma_step * flow
        line_price = shifted - sigma_step * jnp.clip(shifted / sigma_step, -limit, limit)
        dispatch = updated
    return (dispatch, balance_price, line_price)
```

```python
import functools

import jax
import jax.numpy as jnp
from jax import lax
from jax.experimental import pallas as pl
from jax.experimental.pallas import tpu as pltpu
from jax.sharding import PartitionSpec as P

ITERS = 2

tau_step = 0.2
sigma_step = 0.15

META = 16
F32 = jnp.float32
BF16 = jnp.bfloat16
NT = (((1,), (1,)), ((), ()))
NN = (((1,), (0,)), ((), ()))


def dot(a, b, dims=NN):
    return lax.dot_general(a, b, dims, preferred_element_type=F32)


def halves(x):
    hi = x.astype(BF16)
    lo = (x - hi.astype(F32)).astype(BF16)
    return hi, lo


def thirds(x):
    hi = x.astype(BF16)
    rest = x - hi.astype(F32)
    mid = rest.astype(BF16)
    low = (rest - mid.astype(F32)).astype(BF16)
    return hi, mid, low


def pack_kernel(cap, owner_ref, local_ref, cost_ref, dispatch_ref, max_ref, avail_ref, out_ref, rank_ref, pay_ref, meta_ref):
    step = pl.program_id(0)
    gens = dispatch_ref.shape[0]
    hours = dispatch_ref.shape[1]

    @pl.when(step == 0)
    def _():
        owner = owner_ref[...]
        out_hits = lax.broadcasted_iota(jnp.int32, (rank_ref.shape[0], gens), 0)
        hits = (out_hits == owner).astype(F32)
        before = (
            lax.broadcasted_iota(jnp.int32, (gens, gens), 0) < lax.broadcasted_iota(jnp.int32, (gens, gens), 1)
        ).astype(F32)
        count = dot(hits.astype(BF16), before.astype(BF16))
        rank = jnp.sum(count * hits, axis=0, keepdims=True).astype(jnp.int32)
        rank_ref[...] = jnp.broadcast_to(owner * cap + rank, rank_ref.shape)
        pay_ref[:, :hours] = dispatch_ref[...].astype(BF16)
        pay_ref[:, hours:] = (max_ref[...] * avail_ref[...]).astype(BF16)
        local = local_ref[...]
        cost = cost_ref[...]
        hi, mid, low = thirds(cost)
        row = lax.broadcasted_iota(jnp.int32, (META, gens), 0)
        parts = [
            (local // 128 + 1).astype(F32),
            (local % 128).astype(F32),
            hi.astype(F32),
            mid.astype(F32),
            low.astype(F32),
        ]
        meta = jnp.zeros((META, gens), F32)
        for i, part in enumerate(parts):
            meta = jnp.where(row == i, part, meta)
        meta_ref[...] = meta.astype(BF16)

    slot = rank_ref[0:1, :] - step * cap
    pick = (lax.broadcasted_iota(jnp.int32, (cap, gens), 0) == slot).astype(F32).astype(BF16)
    out_ref[0, :cap, :] = dot(pick, pay_ref[...]).astype(BF16)
    out_ref[0, cap:, :] = jnp.zeros((META, 2 * hours), BF16)
    out_ref[0, cap:, :cap] = dot(meta_ref[...], pick, NT).astype(BF16)


def pack(devices, cap, owner, local_bus, cost, dispatch, gen_max, availability):
    gens, hours = dispatch.shape
    full = lambda *shape: pl.BlockSpec(shape, lambda i: (0,) * len(shape))
    return pl.pallas_call(
        functools.partial(pack_kernel, cap),
        grid=(devices,),
        out_shape=jax.ShapeDtypeStruct((devices, cap + META, 2 * hours), BF16),
        in_specs=[
            full(1, gens),
            full(1, gens),
            full(1, gens),
            full(gens, hours),
            full(gens, 1),
            full(gens, hours),
        ],
        out_specs=pl.BlockSpec((1, cap + META, 2 * hours), lambda i: (i, 0, 0)),
        scratch_shapes=[
            pltpu.VMEM((devices, gens), jnp.int32),
            pltpu.VMEM((gens, 2 * hours), BF16),
            pltpu.VMEM((META, gens), BF16),
        ],
        compiler_params=pltpu.CompilerParams(vmem_limit_bytes=48 << 20),
        cost_estimate=pl.CostEstimate(flops=4 * devices * cap * gens * hours, bytes_accessed=3 << 20, transcendentals=0),
        name="pack_generators",
    )(owner, local_bus, cost, dispatch, gen_max, availability)


def unpack_kernel(devices, cap, block, owner_ref, back_ref, dispatch_ref, max_ref, avail_ref, out_ref):
    gens = owner_ref.shape[0]
    owner = owner_ref[...]
    hits = (lax.broadcasted_iota(jnp.int32, (gens, devices), 1) == owner).astype(F32)
    before = (
        lax.broadcasted_iota(jnp.int32, (gens, gens), 1) < lax.broadcasted_iota(jnp.int32, (gens, gens), 0)
    ).astype(F32)
    count = dot(before.astype(BF16), hits.astype(BF16))
    rank = jnp.sum(count * hits, axis=1, keepdims=True).astype(jnp.int32)
    slot = owner * cap + rank
    out_ref[...] = jnp.zeros(out_ref.shape, F32)

    def body(step, carry):
        start = pl.multiple_of(step * block, block)
        pick = (lax.broadcasted_iota(jnp.int32, (gens, block), 1) == slot - start).astype(F32).astype(BF16)
        out_ref[...] += dot(pick, back_ref[pl.ds(start, block), :])
        return carry

    lax.fori_loop(0, back_ref.shape[0] // block, body, 0)
    change = out_ref[...]
    dispatch = dispatch_ref[...]
    upper = max_ref[...] * avail_ref[...]
    sent = dispatch.astype(BF16).astype(F32)
    to_upper = (upper.astype(BF16).astype(F32) - sent).astype(BF16).astype(F32)
    moved = jnp.minimum(jnp.maximum(dispatch + change, 0.0), upper)
    moved = jnp.where(change == to_upper, upper, moved)
    out_ref[...] = jnp.where(change == -sent, 0.0, moved)


def unpack(devices, cap, owner_column, back, dispatch, gen_max, availability):
    gens = owner_column.shape[0]
    hours = back.shape[2]
    slots = devices * cap
    block = 256 if slots % 256 == 0 else 128 if slots % 128 == 0 else 16
    return pl.pallas_call(
        functools.partial(unpack_kernel, devices, cap, block),
        out_shape=jax.ShapeDtypeStruct((gens, hours), F32),
        compiler_params=pltpu.CompilerParams(vmem_limit_bytes=48 << 20),
        cost_estimate=pl.CostEstimate(flops=2 * slots * gens * hours, bytes_accessed=1 << 20, transcendentals=0),
        name="unpack_dispatch",
    )(owner_column, back.reshape(slots, hours), dispatch, gen_max, availability)


def update_kernel(cap, first, last, parts, *refs):
    price_refs = refs[:parts]
    balance_ref, demand_ref, recv_ref, prev_ref, upd_ref, inj_ref, shadow_ref, acc_ref, extra_ref = refs[parts:]
    step = pl.program_id(0)
    buses, hours = demand_ref.shape

    @pl.when(step == 0)
    def _():
        shadow = price_refs[0][...].astype(F32)
        for ref in price_refs[1:]:
            shadow = shadow + ref[...].astype(F32)
        hi, lo = halves(shadow)
        shadow_ref[:hours, :] = hi
        shadow_ref[hours:, :] = lo
        acc_ref[...] = jnp.zeros(acc_ref.shape, F32)
        extra_ref[...] = jnp.zeros(extra_ref.shape, BF16)

    meta = recv_ref[0, cap:, :]
    meta32 = meta[:, : extra_ref.shape[0]].astype(F32)
    bus_row = ((meta32[0:1] - 1.0) * 128.0 + meta32[1:2]).astype(jnp.int32)
    eye = (
        lax.broadcasted_iota(jnp.int32, (cap, 2 * hours), 0) == lax.broadcasted_iota(jnp.int32, (cap, 2 * hours), 1)
    ).astype(F32)
    columns = dot(eye.astype(BF16), meta, NT)
    bus_column = ((columns[:, 0:1] - 1.0) * 128.0 + columns[:, 1:2]).astype(jnp.int32)
    cost = (columns[:, 2:3] + columns[:, 3:4]) + columns[:, 4:5]
    at_bus = (lax.broadcasted_iota(jnp.int32, (cap, buses), 1) == bus_column).astype(F32).astype(BF16)
    both = dot(at_bus, shadow_ref[...], NT)
    price = both[:, :hours] + both[:, hours:] + balance_ref[...]
    if first:
        dispatch = recv_ref[0, :cap, :hours].astype(F32)
    else:
        dispatch = prev_ref[0]
    upper = recv_ref[0, :cap, hours:].astype(F32)
    updated = jnp.minimum(jnp.maximum(dispatch - tau_step * (cost + price), 0.0), upper)
    if last:
        upd_ref[0] = (updated - recv_ref[0, :cap, :hours].astype(F32)).astype(BF16)
    else:
        upd_ref[0] = updated
    extra = 2.0 * updated - dispatch
    hi, lo = halves(extra)
    extra_ref[:cap, :hours] = hi
    extra_ref[:cap, hours:] = lo
    at_row = lax.broadcasted_iota(jnp.int32, (buses, extra_ref.shape[0]), 0)
    to_bus = (at_row == bus_row).astype(F32).astype(BF16)
    acc_ref[...] += dot(to_bus, extra_ref[...])

    @pl.when(step == pl.num_programs(0) - 1)
    def _():
        injection = acc_ref[:, :hours] + acc_ref[:, hours:] - demand_ref[...]
        inj_ref[:buses, :] = injection.astype(BF16)
        hi, mid, low = thirds(jnp.sum(injection, axis=0, keepdims=True))
        row = lax.broadcasted_iota(jnp.int32, (META, hours), 0)
        tail = jnp.where(row == 0, hi.astype(F32), 0.0)
        tail = jnp.where(row == 1, mid.astype(F32), tail)
        tail = jnp.where(row == 2, low.astype(F32), tail)
        inj_ref[buses:, :] = tail.astype(BF16)


def update(cap, first, last, prices, balance_price, demand, recv, previous):
    devices = recv.shape[0]
    buses, hours = demand.shape
    full = lambda *shape: pl.BlockSpec(shape, lambda i: (0,) * len(shape))
    slots = lambda width: pl.BlockSpec((1, cap, width), lambda i: (i, 0, 0))
    if first:
        previous, prev_spec = balance_price, full(1, hours)
    else:
        prev_spec = slots(hours)
    return pl.pallas_call(
        functools.partial(update_kernel, cap, first, last, len(prices)),
        grid=(devices,),
        out_shape=(
            jax.ShapeDtypeStruct((devices, cap, hours), BF16 if last else F32),
            jax.ShapeDtypeStruct((buses + META, hours), BF16),
        ),
        in_specs=[full(hours, buses)] * len(prices)
        + [
            full(1, hours),
            full(buses, hours),
            pl.BlockSpec((1, cap + META, 2 * hours), lambda i: (i, 0, 0)),
            prev_spec,
        ],
        out_specs=(slots(hours), full(buses + META, hours)),
        scratch_shapes=[
            pltpu.VMEM((2 * hours, buses), BF16),
            pltpu.VMEM((buses, 2 * hours), F32),
            pltpu.VMEM((-(-cap // 128) * 128, 2 * hours), BF16),
        ],
        compiler_params=pltpu.CompilerParams(vmem_limit_bytes=48 << 20),
        cost_estimate=pl.CostEstimate(flops=8 * devices * cap * buses * hours, bytes_accessed=4 << 20, transcendentals=0),
        name="update_generators",
    )(*prices, balance_price, demand, recv, previous)


def shadow_kernel(place_ref, line_ref, ptdf_ref, keep_ref, send_ref):
    step = pl.program_id(0)
    part = dot(line_ref[...], ptdf_ref[...])

    @pl.when(step == 0)
    def _():
        send_ref[1] = part.astype(BF16)

    @pl.when(step == 1)
    def _():
        keep_ref[1] = part

    @pl.when(step == 2)
    def _():
        send_ref[0] = part.astype(BF16)

    @pl.when(step == 3)
    def _():
        keep_ref[0] = part


def shadow_chunk(chunk, place, line_t, ptdf, buses):
    hours, lines = line_t.shape
    return pl.pallas_call(
        shadow_kernel,
        grid_spec=pltpu.PrefetchScalarGridSpec(
            num_scalar_prefetch=1,
            grid=(4,),
            in_specs=[
                pl.BlockSpec((hours, lines), lambda i, place: (0, 0)),
                pl.BlockSpec((lines, buses), lambda i, place: (0, place[0] ^ (4 * chunk + 3 - i))),
            ],
            out_specs=(
                pl.BlockSpec((2, hours, buses), lambda i, place: (0, 0, 0)),
                pl.BlockSpec((2, hours, buses), lambda i, place: (0, 0, 0)),
            ),
        ),
        out_shape=(
            jax.ShapeDtypeStruct((2, hours, buses), F32),
            jax.ShapeDtypeStruct((2, hours, buses), BF16),
        ),
        compiler_params=pltpu.CompilerParams(vmem_limit_bytes=48 << 20),
        cost_estimate=pl.CostEstimate(
            flops=8 * hours * lines * buses, bytes_accessed=8 * lines * buses, transcendentals=0
        ),
        name="shadow_chunk",
    )(place, line_t, ptdf)


def flow_kernel(start, end, place_ref, ptdf_ref, b0, b1, b2, b3, acc_ref, sum_ref, *rest):
    step = pl.program_id(0)
    if end:
        limit_ref, line_ref, out_ref, half_ref, sum_out, inj_ref = rest
    else:
        out_ref, sum_out, inj_ref = rest
    buses = inj_ref.shape[0] // 4

    @pl.when(step == 0)
    def _():
        total = jnp.zeros(sum_ref.shape, F32) if start else sum_ref[...]
        for rel, ref in enumerate((b0, b1, b2, b3)):
            offset = pl.multiple_of(((place_ref[0] ^ rel) & 3) * buses, META)
            inj_ref[pl.ds(offset, buses), :] = ref[:buses, :]
            tail = ref[buses:, :].astype(F32)
            total = total + jnp.sum(tail, axis=0, keepdims=True)
        sum_out[...] = total

    flow = dot(ptdf_ref[...], inj_ref[...])
    if not start:
        flow = flow + acc_ref[...]
    if end:
        shifted = line_ref[...] + sigma_step * flow
        limit = limit_ref[...]
        line = shifted - sigma_step * jnp.minimum(jnp.maximum(shifted / sigma_step, -limit), limit)
        out_ref[...] = line
        half_ref[...] = line.astype(BF16)
    else:
        out_ref[...] = flow


def flow_chunk(chunk, place, ptdf, blocks, acc, total, limit=None, line=None):
    lines = ptdf.shape[0]
    rows, hours = blocks[0].shape
    buses = rows - META
    start, end = acc is None, limit is not None
    tile = lines // 4
    tiled = lambda width: pl.BlockSpec((tile, width), lambda i, place: (i, 0))
    full = lambda *shape: pl.BlockSpec(shape, lambda i, place: (0,) * len(shape))
    if start:
        acc, acc_spec = total, full(1, hours)
    else:
        acc_spec = tiled(hours)
    operands = [ptdf, *blocks, acc, total]
    in_specs = [pl.BlockSpec((tile, 4 * buses), lambda i, place: (i, (place[0] >> 2) ^ chunk))]
    in_specs += [full(rows, hours)] * 4 + [acc_spec, full(1, hours)]
    out_shape = [jax.ShapeDtypeStruct((lines, hours), F32)]
    out_specs = [tiled(hours)]
    if end:
        operands += [limit, line]
        in_specs += [tiled(1), tiled(hours)]
        out_shape += [jax.ShapeDtypeStruct((lines, hours), BF16)]
        out_specs += [tiled(hours)]
    out_shape += [jax.ShapeDtypeStruct((1, hours), F32)]
    out_specs += [full(1, hours)]
    return pl.pallas_call(
        functools.partial(flow_kernel, start, end),
        grid_spec=pltpu.PrefetchScalarGridSpec(
            num_scalar_prefetch=1,
            grid=(4,),
            in_specs=in_specs,
            out_specs=tuple(out_specs),
            scratch_shapes=[pltpu.VMEM((4 * buses, hours), BF16)],
        ),
        out_shape=tuple(out_shape),
        compiler_params=pltpu.CompilerParams(vmem_limit_bytes=48 << 20),
        cost_estimate=pl.CostEstimate(
            flops=8 * hours * lines * buses, bytes_accessed=8 * lines * buses, transcendentals=0
        ),
        name="flow_chunk",
    )(place, *operands)


def swap(x, devices, mask):
    return lax.ppermute(x, "bus", [(i, i ^ mask) for i in range(devices)])


def local(
    ptdf,
    line_limit,
    gen_cost,
    gen_max,
    gen_owner,
    gen_local,
    availability,
    demand,
    dispatch,
    balance_price,
    line_price,
):
    devices = lax.axis_size("bus")
    place = lax.axis_index("bus").astype(jnp.int32).reshape(1)
    buses = demand.shape[0]
    all_buses = buses * devices
    gens, hours = dispatch.shape
    cap = -(-max(2, 3 * gens // devices) // 16) * 16
    staged = devices == 16 and buses % 128 == 0

    outgoing = pack(
        devices,
        cap,
        gen_owner.reshape(1, gens),
        gen_local.reshape(1, gens),
        gen_cost.reshape(1, gens),
        dispatch,
        gen_max.reshape(gens, 1),
        availability,
    )
    recv = lax.all_to_all(outgoing, "bus", split_axis=0, concat_axis=0, tiled=True)
    limit = line_limit.reshape(-1, 1)
    balance_row = balance_price.reshape(1, hours)
    line_half = line_price.astype(BF16)
    held = None
    for iteration in range(ITERS):
        last = iteration == ITERS - 1
        if staged:
            line_t = line_half.T
            prices = []
            for chunk in (3, 2, 1, 0):
                keep, send = shadow_chunk(chunk, place, line_t, ptdf, buses)
                got = swap(send, devices, 1)
                across = (keep[1] + got[1].astype(F32)).astype(BF16)
                crossed = swap(across, devices, 2)
                part = keep[0] + got[0].astype(F32) + crossed.astype(F32)
                if chunk:
                    part = swap(part.astype(BF16), devices, 4 * chunk)
                prices.append(part)
        else:
            shadow = lax.dot_general(ptdf, line_half, (((0,), (0,)), ((), ())), preferred_element_type=F32)
            prices = [lax.psum_scatter(shadow, "bus", scatter_dimension=0, tiled=True).T]
        held, block = update(cap, iteration == 0, last, prices, balance_row, demand, recv, held)
        if last:
            back = lax.all_to_all(held, "bus", split_axis=0, concat_axis=0, tiled=True)
        if staged:
            acc, total = None, balance_row
            for chunk in range(4):
                near = swap(block, devices, 4 * chunk) if chunk else block
                far = swap(near, devices, 2)
                blocks = [near, swap(near, devices, 1), far, swap(far, devices, 1)]
                if chunk < 3:
                    acc, total = flow_chunk(chunk, place, ptdf, blocks, acc, total)
                else:
                    line_price, line_half, total = flow_chunk(
                        chunk, place, ptdf, blocks, acc, total, limit, line_price
                    )
            balance = total
        else:
            every = lax.all_gather(block, "bus", axis=0, tiled=False)
            balance = jnp.sum(every[:, buses:].astype(F32), axis=(0, 1)).reshape(1, hours)
            flow = jnp.dot(ptdf, every[:, :buses].reshape(all_buses, hours), preferred_element_type=F32)
            shifted = line_price + sigma_step * flow
            line_price = shifted - sigma_step * jnp.clip(shifted / sigma_step, -limit, limit)
            line_half = line_price.astype(BF16)
        balance_row = balance_row + sigma_step * balance / all_buses
    dispatch = unpack(devices, cap, gen_owner, back, dispatch, gen_max.reshape(gens, 1), availability)
    return (dispatch, balance_row.reshape(hours), line_price)


def solution(mesh):
    return jax.shard_map(
        local,
        mesh=mesh,
        in_specs=(
            P("bus", None),
            P("bus"),
            P("bus"),
            P("bus"),
            P("bus", None),
            P("bus"),
            P(("cases", "bus"), None),
            P(("cases", "bus"), None),
            P(("cases", "bus"), None),
            P("cases"),
            P(("cases", "bus"), None),
        ),
        out_specs=(P(("cases", "bus"), None), P("cases"), P(("cases", "bus"), None)),
        check_vma=False,
    )
```

```python
import functools

import jax
import jax.numpy as jnp
from jax import lax
from jax.experimental import pallas as pl
from jax.experimental.pallas import tpu as pltpu
from jax.sharding import PartitionSpec as P

ITERS = 2

tau_step = 0.2
sigma_step = 0.15

GROUP = 4
LIMIT = 48 << 20
COST = 3
META = 16
F32 = jnp.float32
BF16 = jnp.bfloat16
NT = (((1,), (1,)), ((), ()))
NN = (((1,), (0,)), ((), ()))


def dot(a, b, dims=NN):
    return lax.dot_general(a, b, dims, preferred_element_type=F32)


def halves(x):
    hi = x.astype(BF16)
    lo = (x - hi.astype(F32)).astype(BF16)
    return hi, lo


def thirds(x):
    hi = x.astype(BF16)
    rest = x - hi.astype(F32)
    mid = rest.astype(BF16)
    low = (rest - mid.astype(F32)).astype(BF16)
    return hi, mid, low


def as_row(ref):
    return jnp.concatenate([ref[i : i + 1, :] for i in range(ref.shape[0])], axis=1)


def pack_kernel(cap, owner_ref, local_ref, cost_ref, dispatch_ref, max_ref, avail_ref, out_ref, slot_ref, pay_ref, meta_ref):
    step = pl.program_id(0)
    gens, hours = dispatch_ref.shape
    group = out_ref.shape[0]

    @pl.when(step == 0)
    def _():
        owner = as_row(owner_ref)
        hits = (lax.broadcasted_iota(jnp.int32, (slot_ref.shape[0], gens), 0) == owner).astype(F32)
        before = (
            lax.broadcasted_iota(jnp.int32, (gens, gens), 0) < lax.broadcasted_iota(jnp.int32, (gens, gens), 1)
        ).astype(F32)
        count = dot(hits.astype(BF16), before.astype(BF16))
        rank = jnp.sum(count * hits, axis=0, keepdims=True).astype(jnp.int32)
        slot_ref[...] = jnp.broadcast_to(owner * cap + rank, slot_ref.shape)
        pay_ref[:, :hours] = dispatch_ref[...].astype(BF16)
        lanes = max_ref.shape[1]
        eye = (
            lax.broadcasted_iota(jnp.int32, (lanes, lanes), 0) == lax.broadcasted_iota(jnp.int32, (lanes, lanes), 1)
        ).astype(F32)
        for i in range(gens // lanes):
            rows = slice(i * lanes, (i + 1) * lanes)
            most = jnp.sum(eye * max_ref[i : i + 1, :], axis=1, keepdims=True)
            pay_ref[rows, hours:] = (most * avail_ref[rows, :]).astype(BF16)
        local = as_row(local_ref)
        hi, mid, low = thirds(as_row(cost_ref))
        row = lax.broadcasted_iota(jnp.int32, (META, gens), 0)
        parts = [
            (lax.shift_right_logical(local, 7) + 1).astype(F32),
            (local & 127).astype(F32),
            hi.astype(F32),
            mid.astype(F32),
            low.astype(F32),
        ]
        meta = jnp.zeros((META, gens), F32)
        for i, part in enumerate(parts):
            meta = jnp.where(row == i, part, meta)
        meta_ref[...] = meta.astype(BF16)

    slot = slot_ref[0:1, :] - step * (group * cap)
    place = lax.broadcasted_iota(jnp.int32, (cap, gens), 0)
    picks = [(place == slot - i * cap).astype(F32).astype(BF16) for i in range(group)]
    moved = dot(jnp.concatenate(picks, axis=0), pay_ref[...]).astype(BF16)
    for i in range(group):
        out_ref[i, :cap, :] = moved[i * cap : (i + 1) * cap]
        out_ref[i, cap:, :] = jnp.zeros((META, 2 * hours), BF16)
        out_ref[i, cap:, :cap] = dot(meta_ref[...], picks[i], NT).astype(BF16)


def pack(devices, cap, owner, local_bus, cost, dispatch, gen_max, availability):
    gens, hours = dispatch.shape
    full = lambda *shape: pl.BlockSpec(shape, lambda i: (0,) * len(shape))
    folded = (gens // 128, 128)
    return pl.pallas_call(
        functools.partial(pack_kernel, cap),
        grid=(devices // GROUP,),
        out_shape=jax.ShapeDtypeStruct((devices, cap + META, 2 * hours), BF16),
        in_specs=[
            full(*folded),
            full(*folded),
            full(*folded),
            full(gens, hours),
            full(*folded),
            full(gens, hours),
        ],
        out_specs=pl.BlockSpec((GROUP, cap + META, 2 * hours), lambda i: (i, 0, 0)),
        scratch_shapes=[
            pltpu.VMEM((devices, gens), jnp.int32),
            pltpu.VMEM((gens, 2 * hours), BF16),
            pltpu.VMEM((META, gens), BF16),
        ],
        compiler_params=pltpu.CompilerParams(vmem_limit_bytes=LIMIT),
        cost_estimate=pl.CostEstimate(flops=4 * devices * cap * gens * hours, bytes_accessed=3 << 20, transcendentals=0),
        name="pack_generators",
    )(
        owner.reshape(folded),
        local_bus.reshape(folded),
        cost.reshape(folded),
        dispatch,
        gen_max.reshape(folded),
        availability,
    )


def unpack_kernel(devices, cap, block, owner_ref, back_ref, dispatch_ref, max_ref, avail_ref, out_ref):
    gens = owner_ref.shape[0]
    owner = owner_ref[...]
    hits = (lax.broadcasted_iota(jnp.int32, (gens, devices), 1) == owner).astype(F32)
    before = (
        lax.broadcasted_iota(jnp.int32, (gens, gens), 1) < lax.broadcasted_iota(jnp.int32, (gens, gens), 0)
    ).astype(F32)
    count = dot(before.astype(BF16), hits.astype(BF16))
    rank = jnp.sum(count * hits, axis=1, keepdims=True).astype(jnp.int32)
    slot = owner * cap + rank
    out_ref[...] = jnp.zeros(out_ref.shape, F32)

    def body(step, carry):
        start = pl.multiple_of(step * block, block)
        pick = (lax.broadcasted_iota(jnp.int32, (gens, block), 1) == slot - start).astype(F32).astype(BF16)
        out_ref[...] += dot(pick, back_ref[pl.ds(start, block), :])
        return carry

    lax.fori_loop(0, back_ref.shape[0] // block, body, 0)
    change = out_ref[...]
    dispatch = dispatch_ref[...]
    upper = max_ref[...] * avail_ref[...]
    sent = dispatch.astype(BF16).astype(F32)
    to_upper = (upper.astype(BF16).astype(F32) - sent).astype(BF16).astype(F32)
    moved = jnp.minimum(jnp.maximum(dispatch + change, 0.0), upper)
    moved = jnp.where(change == to_upper, upper, moved)
    out_ref[...] = jnp.where(change == -sent, 0.0, moved)


def unpack(devices, cap, owner_column, back, dispatch, gen_max, availability):
    gens = owner_column.shape[0]
    hours = back.shape[2]
    slots = devices * cap
    block = 256 if slots % 256 == 0 else 128 if slots % 128 == 0 else 16
    return pl.pallas_call(
        functools.partial(unpack_kernel, devices, cap, block),
        out_shape=jax.ShapeDtypeStruct((gens, hours), F32),
        compiler_params=pltpu.CompilerParams(vmem_limit_bytes=LIMIT),
        cost_estimate=pl.CostEstimate(flops=2 * slots * gens * hours, bytes_accessed=1 << 20, transcendentals=0),
        name="unpack_dispatch",
    )(owner_column, back.reshape(slots, hours), dispatch, gen_max, availability)


def update_kernel(cap, first, last, parts, *refs):
    price_refs = refs[:parts]
    balance_ref, demand_ref, recv_ref, prev_ref, upd_ref, inj_ref, shadow_ref, acc_ref, extra_ref = refs[parts:]
    step = pl.program_id(0)
    buses, hours = demand_ref.shape

    @pl.when(step == 0)
    def _():
        shadow = price_refs[0][...].astype(F32)
        for ref in price_refs[1:]:
            shadow = shadow + ref[...].astype(F32)
        hi, lo = halves(shadow)
        shadow_ref[:hours, :] = hi
        shadow_ref[hours:, :] = lo
        acc_ref[...] = jnp.zeros(acc_ref.shape, F32)
        extra_ref[...] = jnp.zeros(extra_ref.shape, BF16)

    group = recv_ref.shape[0]
    pad = extra_ref.shape[0] // group
    wide = 2 * hours
    meta = recv_ref[:, cap:, :].reshape(group * META, wide)
    eye = (
        lax.broadcasted_iota(jnp.int32, (cap, wide), 0) == lax.broadcasted_iota(jnp.int32, (cap, wide), 1)
    ).astype(F32)
    columns = dot(eye.astype(BF16), meta, NT)
    buses_at = lax.broadcasted_iota(jnp.int32, (cap, buses), 1)
    picks = []
    for i in range(group):
        at = i * META
        bus_column = ((columns[:, at : at + 1] - 1.0) * 128.0 + columns[:, at + 1 : at + 2]).astype(jnp.int32)
        picks.append((buses_at == bus_column).astype(F32).astype(BF16))
    both = dot(jnp.concatenate(picks, axis=0), shadow_ref[...], NT)
    for i in range(group):
        at = i * META
        cost = (columns[:, at + 2 : at + 3] + columns[:, at + 3 : at + 4]) + columns[:, at + 4 : at + 5]
        rows = slice(i * cap, (i + 1) * cap)
        price = both[rows, :hours] + both[rows, hours:] + balance_ref[...]
        sent = recv_ref[i, :cap, :hours].astype(F32)
        dispatch = sent if first else prev_ref[i]
        upper = recv_ref[i, :cap, hours:].astype(F32)
        updated = jnp.minimum(jnp.maximum(dispatch - tau_step * (cost + price), 0.0), upper)
        if last:
            upd_ref[i] = (updated - sent).astype(BF16)
        else:
            upd_ref[i] = updated
        hi, lo = halves(2.0 * updated - dispatch)
        extra_ref[i * pad : i * pad + cap, :hours] = hi
        extra_ref[i * pad : i * pad + cap, hours:] = lo
    at_row = lax.broadcasted_iota(jnp.int32, (buses, pad), 0)
    picks = []
    for i in range(group):
        row = recv_ref[i, cap:, :pad].astype(F32)
        bus_row = ((row[0:1] - 1.0) * 128.0 + row[1:2]).astype(jnp.int32)
        picks.append((at_row == bus_row).astype(F32).astype(BF16))
    acc_ref[...] += dot(jnp.concatenate(picks, axis=1), extra_ref[...])

    @pl.when(step == pl.num_programs(0) - 1)
    def _():
        injection = acc_ref[:, :hours] + acc_ref[:, hours:] - demand_ref[...]
        inj_ref[:buses, :] = injection.astype(BF16)
        hi, mid, low = thirds(jnp.sum(injection, axis=0, keepdims=True))
        row = lax.broadcasted_iota(jnp.int32, (META, hours), 0)
        tail = jnp.where(row == 0, hi.astype(F32), 0.0)
        tail = jnp.where(row == 1, mid.astype(F32), tail)
        tail = jnp.where(row == 2, low.astype(F32), tail)
        inj_ref[buses:, :] = tail.astype(BF16)


def update(cap, first, last, prices, balance_price, demand, recv, previous):
    devices = recv.shape[0]
    buses, hours = demand.shape
    full = lambda *shape: pl.BlockSpec(shape, lambda i: (0,) * len(shape))
    slots = lambda width: pl.BlockSpec((GROUP, cap, width), lambda i: (i, 0, 0))
    if first:
        previous, prev_spec = balance_price, full(1, hours)
    else:
        prev_spec = slots(hours)
    return pl.pallas_call(
        functools.partial(update_kernel, cap, first, last, len(prices)),
        grid=(devices // GROUP,),
        out_shape=(
            jax.ShapeDtypeStruct((devices, cap, hours), BF16 if last else F32),
            jax.ShapeDtypeStruct((buses + META, hours), BF16),
        ),
        in_specs=[full(hours, buses)] * len(prices)
        + [
            full(1, hours),
            full(buses, hours),
            pl.BlockSpec((GROUP, cap + META, 2 * hours), lambda i: (i, 0, 0)),
            prev_spec,
        ],
        out_specs=(slots(hours), full(buses + META, hours)),
        scratch_shapes=[
            pltpu.VMEM((2 * hours, buses), BF16),
            pltpu.VMEM((buses, 2 * hours), F32),
            pltpu.VMEM((GROUP * (-(-cap // 128) * 128), 2 * hours), BF16),
        ],
        compiler_params=pltpu.CompilerParams(vmem_limit_bytes=LIMIT),
        cost_estimate=pl.CostEstimate(flops=8 * devices * cap * buses * hours, bytes_accessed=4 << 20, transcendentals=0),
        name="update_generators",
    )(*prices, balance_price, demand, recv, previous)


def shadow_kernel(place_ref, line_ref, ptdf_ref, keep_ref, send_ref):
    step = pl.program_id(0)
    part = dot(line_ref[...], ptdf_ref[...])

    @pl.when(step == 0)
    def _():
        send_ref[1] = part.astype(BF16)

    @pl.when(step == 1)
    def _():
        keep_ref[1] = part

    @pl.when(step == 2)
    def _():
        send_ref[0] = part.astype(BF16)

    @pl.when(step == 3)
    def _():
        keep_ref[0] = part


def shadow_chunk(chunk, place, line_t, ptdf, buses):
    hours, lines = line_t.shape
    return pl.pallas_call(
        shadow_kernel,
        grid_spec=pltpu.PrefetchScalarGridSpec(
            num_scalar_prefetch=1,
            grid=(4,),
            in_specs=[
                pl.BlockSpec((hours, lines), lambda i, place: (0, 0)),
                pl.BlockSpec((lines, buses), lambda i, place: (0, place[0] ^ (4 * chunk + 3 - i))),
            ],
            out_specs=(
                pl.BlockSpec((2, hours, buses), lambda i, place: (0, 0, 0)),
                pl.BlockSpec((2, hours, buses), lambda i, place: (0, 0, 0)),
            ),
        ),
        out_shape=(
            jax.ShapeDtypeStruct((2, hours, buses), F32),
            jax.ShapeDtypeStruct((2, hours, buses), BF16),
        ),
        compiler_params=pltpu.CompilerParams(vmem_limit_bytes=LIMIT),
        cost_estimate=pl.CostEstimate(
            flops=COST * 8 * hours * lines * buses, bytes_accessed=8 * lines * buses, transcendentals=0
        ),
        name="shadow_chunk",
    )(place, line_t, ptdf)


def flow_kernel(start, end, place_ref, ptdf_ref, b0, b1, b2, b3, acc_ref, sum_ref, *rest):
    step = pl.program_id(0)
    if end:
        limit_ref, line_ref, out_ref, half_ref, sum_out, inj_ref = rest
    else:
        out_ref, sum_out, inj_ref = rest
    buses = inj_ref.shape[0] // 4

    @pl.when(step == 0)
    def _():
        total = jnp.zeros(sum_ref.shape, F32) if start else sum_ref[...]
        for rel, ref in enumerate((b0, b1, b2, b3)):
            offset = pl.multiple_of(((place_ref[0] ^ rel) & 3) * buses, META)
            inj_ref[pl.ds(offset, buses), :] = ref[:buses, :]
            tail = ref[buses:, :].astype(F32)
            total = total + jnp.sum(tail, axis=0, keepdims=True)
        sum_out[...] = total

    depth = ptdf_ref.shape[1]
    rows = pl.ds(pl.multiple_of(step * depth, depth), depth)
    part = dot(ptdf_ref[...], inj_ref[rows, :])

    @pl.when(step == 0)
    def _():
        out_ref[...] = part if start else acc_ref[...] + part

    @pl.when(step > 0)
    def _():
        out_ref[...] += part

    if end:

        @pl.when(step == pl.num_programs(0) - 1)
        def _():
            shifted = line_ref[...] + sigma_step * out_ref[...]
            limit = limit_ref[...]
            line = shifted - sigma_step * jnp.minimum(jnp.maximum(shifted / sigma_step, -limit), limit)
            out_ref[...] = line
            half_ref[...] = line.astype(BF16)


def flow_chunk(chunk, place, ptdf, blocks, acc, total, limit=None, line=None):
    lines = ptdf.shape[0]
    rows, hours = blocks[0].shape
    buses = rows - META
    start, end = acc is None, limit is not None
    steps = 5
    depth = 4 * buses // steps
    full = lambda *shape: pl.BlockSpec(shape, lambda i, place: (0,) * len(shape))
    if start:
        acc, acc_spec = total, full(1, hours)
    else:
        acc_spec = full(lines, hours)
    operands = [ptdf, *blocks, acc, total]
    in_specs = [pl.BlockSpec((lines, depth), lambda i, place: (0, ((place[0] >> 2) ^ chunk) * steps + i))]
    in_specs += [full(rows, hours)] * 4 + [acc_spec, full(1, hours)]
    out_shape = [jax.ShapeDtypeStruct((lines, hours), F32)]
    out_specs = [full(lines, hours)]
    if end:
        operands += [limit, line]
        in_specs += [full(lines, 1), full(lines, hours)]
        out_shape += [jax.ShapeDtypeStruct((lines, hours), BF16)]
        out_specs += [full(lines, hours)]
    out_shape += [jax.ShapeDtypeStruct((1, hours), F32)]
    out_specs += [full(1, hours)]
    return pl.pallas_call(
        functools.partial(flow_kernel, start, end),
        grid_spec=pltpu.PrefetchScalarGridSpec(
            num_scalar_prefetch=1,
            grid=(steps,),
            in_specs=in_specs,
            out_specs=tuple(out_specs),
            scratch_shapes=[pltpu.VMEM((4 * buses, hours), BF16)],
        ),
        out_shape=tuple(out_shape),
        compiler_params=pltpu.CompilerParams(vmem_limit_bytes=LIMIT),
        cost_estimate=pl.CostEstimate(
            flops=COST * 8 * hours * lines * buses, bytes_accessed=8 * lines * buses, transcendentals=0
        ),
        name="flow_chunk",
    )(place, *operands)


def swap(x, devices, mask):
    return lax.ppermute(x, "bus", [(i, i ^ mask) for i in range(devices)])


def local(
    ptdf,
    line_limit,
    gen_cost,
    gen_max,
    gen_owner,
    gen_local,
    availability,
    demand,
    dispatch,
    balance_price,
    line_price,
):
    devices = lax.axis_size("bus")
    place = lax.axis_index("bus").astype(jnp.int32).reshape(1)
    buses = demand.shape[0]
    all_buses = buses * devices
    gens, hours = dispatch.shape
    cap = -(-max(2, 3 * gens // devices) // 16) * 16
    staged = devices == 16 and buses % 128 == 0

    outgoing = pack(
        devices,
        cap,
        gen_owner,
        gen_local,
        gen_cost,
        dispatch,
        gen_max,
        availability,
    )
    limit = line_limit.reshape(-1, 1)
    balance_row = balance_price.reshape(1, hours)
    line_half = line_price.astype(BF16)
    if staged:
        line_half, outgoing = lax.optimization_barrier((line_half, outgoing))
    recv = lax.all_to_all(outgoing, "bus", split_axis=0, concat_axis=0, tiled=True)
    held = None
    for iteration in range(ITERS):
        last = iteration == ITERS - 1
        if staged:
            line_t = line_half.T
            keeps, gots, crossed, parts = {}, {}, {}, {}

            def across(chunk):
                both = (keeps[chunk][1] + gots[chunk][1].astype(F32)).astype(BF16)
                crossed[chunk] = swap(both, devices, 2)
                return both

            def settle(chunk):
                part = keeps[chunk][0] + gots[chunk][0].astype(F32) + crossed[chunk].astype(F32)
                if chunk == 2:
                    part = part + parts[3].astype(F32)
                if chunk:
                    part = part.astype(BF16)
                    parts[chunk] = swap(part, devices, 8 if chunk == 2 else 4)
                else:
                    parts[chunk] = part
                return part

            def product(chunk, line_t):
                keeps[chunk], send = shadow_chunk(chunk, place, line_t, ptdf, buses)
                gots[chunk] = swap(send, devices, 1)

            product(3, line_t)
            product(2, line_t)
            line_t, _ = lax.optimization_barrier((line_t, across(3)))
            product(1, line_t)
            line_t, _, _ = lax.optimization_barrier((line_t, across(2), settle(3)))
            product(0, line_t)
            across(1)
            settle(2)
            across(0)
            settle(1)
            settle(0)
            prices = [parts[0], parts[1], parts[2]]
        else:
            shadow = lax.dot_general(ptdf, line_half, (((0,), (0,)), ((), ())), preferred_element_type=F32)
            prices = [lax.psum_scatter(shadow, "bus", scatter_dimension=0, tiled=True).T]
        held, block = update(cap, iteration == 0, last, prices, balance_row, demand, recv, held)
        if staged:
            near, far, cross, far_cross = {0: block}, {}, {}, {}

            def spread(chunk):
                far[chunk] = swap(near[chunk], devices, 2)
                cross[chunk] = swap(near[chunk], devices, 1)

            def settle_far(chunk):
                far_cross[chunk] = swap(far[chunk], devices, 1)

            def blocks(chunk):
                return [near[chunk], cross[chunk], far[chunk], far_cross[chunk]]

            near[2] = swap(block, devices, 8)
            near[1] = swap(block, devices, 4)
            spread(0)
            near[3] = swap(near[2], devices, 4)
            spread(1)
            spread(2)
            settle_far(0)
            near[1], near[2], row = lax.optimization_barrier((near[1], near[2], balance_row))
            acc, total = flow_chunk(0, place, ptdf, blocks(0), None, row)
            near[3], acc = lax.optimization_barrier((near[3], acc))
            spread(3)
            if last:
                held, _ = lax.optimization_barrier((held, near[3]))
                back = lax.all_to_all(held, "bus", split_axis=0, concat_axis=0, tiled=True)
            settle_far(1)
            acc, total = flow_chunk(1, place, ptdf, blocks(1), acc, total)
            settle_far(2)
            acc, total = flow_chunk(2, place, ptdf, blocks(2), acc, total)
            settle_far(3)
            line_price, line_half, total = flow_chunk(
                3, place, ptdf, blocks(3), acc, total, limit, line_price
            )
            balance = total
        else:
            if last:
                back = lax.all_to_all(held, "bus", split_axis=0, concat_axis=0, tiled=True)
            every = lax.all_gather(block, "bus", axis=0, tiled=False)
            balance = jnp.sum(every[:, buses:].astype(F32), axis=(0, 1)).reshape(1, hours)
            flow = jnp.dot(ptdf, every[:, :buses].reshape(all_buses, hours), preferred_element_type=F32)
            shifted = line_price + sigma_step * flow
            line_price = shifted - sigma_step * jnp.clip(shifted / sigma_step, -limit, limit)
            line_half = line_price.astype(BF16)
        balance_row = balance_row + sigma_step * balance / all_buses
    dispatch = unpack(devices, cap, gen_owner, back, dispatch, gen_max.reshape(gens, 1), availability)
    return (dispatch, balance_row.reshape(hours), line_price)


def solution(mesh):
    return jax.shard_map(
        local,
        mesh=mesh,
        in_specs=(
            P("bus", None),
            P("bus"),
            P("bus"),
            P("bus"),
            P("bus", None),
            P("bus"),
            P(("cases", "bus"), None),
            P(("cases", "bus"), None),
            P(("cases", "bus"), None),
            P("cases"),
            P(("cases", "bus"), None),
        ),
        out_specs=(P(("cases", "bus"), None), P("cases"), P(("cases", "bus"), None)),
        check_vma=False,
    )
```

```python
import functools

import jax
import jax.numpy as jnp
from jax import lax
from jax.experimental import pallas as pl
from jax.experimental.pallas import tpu as pltpu
from jax.sharding import PartitionSpec as P

ITERS = 2

tau_step = 0.2
sigma_step = 0.15

GROUP = 4
LIMIT = 48 << 20
COST = 3
META = 16
F32 = jnp.float32
BF16 = jnp.bfloat16
NT = (((1,), (1,)), ((), ()))
NN = (((1,), (0,)), ((), ()))


def dot(a, b, dims=NN):
    return lax.dot_general(a, b, dims, preferred_element_type=F32)


def halves(x):
    hi = x.astype(BF16)
    lo = (x - hi.astype(F32)).astype(BF16)
    return hi, lo


def thirds(x):
    hi = x.astype(BF16)
    rest = x - hi.astype(F32)
    mid = rest.astype(BF16)
    low = (rest - mid.astype(F32)).astype(BF16)
    return hi, mid, low


def as_row(ref):
    return jnp.concatenate([ref[i : i + 1, :] for i in range(ref.shape[0])], axis=1)


def pack_kernel(cap, owner_ref, local_ref, cost_ref, dispatch_ref, max_ref, avail_ref, out_ref, slot_ref, pay_ref, meta_ref):
    step = pl.program_id(0)
    gens, hours = dispatch_ref.shape
    group = out_ref.shape[0]

    @pl.when(step == 0)
    def _():
        owner = as_row(owner_ref)
        hits = (lax.broadcasted_iota(jnp.int32, (slot_ref.shape[0], gens), 0) == owner).astype(F32)
        before = (
            lax.broadcasted_iota(jnp.int32, (gens, gens), 0) < lax.broadcasted_iota(jnp.int32, (gens, gens), 1)
        ).astype(F32)
        count = dot(hits.astype(BF16), before.astype(BF16))
        rank = jnp.sum(count * hits, axis=0, keepdims=True).astype(jnp.int32)
        slot_ref[...] = jnp.broadcast_to(owner * cap + rank, slot_ref.shape)
        pay_ref[:, :hours] = dispatch_ref[...].astype(BF16)
        lanes = max_ref.shape[1]
        eye = (
            lax.broadcasted_iota(jnp.int32, (lanes, lanes), 0) == lax.broadcasted_iota(jnp.int32, (lanes, lanes), 1)
        ).astype(F32)
        for i in range(gens // lanes):
            rows = slice(i * lanes, (i + 1) * lanes)
            most = jnp.sum(eye * max_ref[i : i + 1, :], axis=1, keepdims=True)
            pay_ref[rows, hours:] = (most * avail_ref[rows, :]).astype(BF16)
        local = as_row(local_ref)
        hi, mid, low = thirds(as_row(cost_ref))
        row = lax.broadcasted_iota(jnp.int32, (META, gens), 0)
        parts = [
            (lax.shift_right_logical(local, 7) + 1).astype(F32),
            (local & 127).astype(F32),
            hi.astype(F32),
            mid.astype(F32),
            low.astype(F32),
        ]
        meta = jnp.zeros((META, gens), F32)
        for i, part in enumerate(parts):
            meta = jnp.where(row == i, part, meta)
        meta_ref[...] = meta.astype(BF16)

    slot = slot_ref[0:1, :] - step * (group * cap)
    place = lax.broadcasted_iota(jnp.int32, (cap, gens), 0)
    picks = [(place == slot - i * cap).astype(F32).astype(BF16) for i in range(group)]
    moved = dot(jnp.concatenate(picks, axis=0), pay_ref[...]).astype(BF16)
    for i in range(group):
        out_ref[i, :cap, :] = moved[i * cap : (i + 1) * cap]
        out_ref[i, cap:, :] = jnp.zeros((META, 2 * hours), BF16)
        out_ref[i, cap:, :cap] = dot(meta_ref[...], picks[i], NT).astype(BF16)


def pack(devices, cap, owner, local_bus, cost, dispatch, gen_max, availability):
    gens, hours = dispatch.shape
    full = lambda *shape: pl.BlockSpec(shape, lambda i: (0,) * len(shape))
    folded = (gens // 128, 128)
    return pl.pallas_call(
        functools.partial(pack_kernel, cap),
        grid=(devices // GROUP,),
        out_shape=jax.ShapeDtypeStruct((devices, cap + META, 2 * hours), BF16),
        in_specs=[
            full(*folded),
            full(*folded),
            full(*folded),
            full(gens, hours),
            full(*folded),
            full(gens, hours),
        ],
        out_specs=pl.BlockSpec((GROUP, cap + META, 2 * hours), lambda i: (i, 0, 0)),
        scratch_shapes=[
            pltpu.VMEM((devices, gens), jnp.int32),
            pltpu.VMEM((gens, 2 * hours), BF16),
            pltpu.VMEM((META, gens), BF16),
        ],
        compiler_params=pltpu.CompilerParams(vmem_limit_bytes=LIMIT),
        cost_estimate=pl.CostEstimate(flops=4 * devices * cap * gens * hours, bytes_accessed=3 << 20, transcendentals=0),
        name="pack_generators",
    )(
        owner.reshape(folded),
        local_bus.reshape(folded),
        cost.reshape(folded),
        dispatch,
        gen_max.reshape(folded),
        availability,
    )


def slot_kernel(devices, cap, owner_ref, slot_ref):
    gens = owner_ref.shape[0]
    owner = owner_ref[...]
    hits = (lax.broadcasted_iota(jnp.int32, (gens, devices), 1) == owner).astype(F32)
    before = (
        lax.broadcasted_iota(jnp.int32, (gens, gens), 1) < lax.broadcasted_iota(jnp.int32, (gens, gens), 0)
    ).astype(F32)
    count = dot(before.astype(BF16), hits.astype(BF16))
    rank = jnp.sum(count * hits, axis=1, keepdims=True).astype(jnp.int32)
    slot_ref[...] = owner * cap + rank


def slot_column(devices, cap, owner_column):
    return pl.pallas_call(
        functools.partial(slot_kernel, devices, cap),
        out_shape=jax.ShapeDtypeStruct(owner_column.shape, jnp.int32),
        compiler_params=pltpu.CompilerParams(vmem_limit_bytes=LIMIT),
        name="slot_column",
    )(owner_column)


def unpack_kernel(block, slot_ref, back_ref, dispatch_ref, max_ref, avail_ref, out_ref):
    gens = slot_ref.shape[0]
    slot = slot_ref[...]
    at = lax.broadcasted_iota(jnp.int32, (gens, block), 1)
    change = None
    for start in range(0, back_ref.shape[0], block):
        pick = (at == slot - start).astype(F32).astype(BF16)
        part = dot(pick, back_ref[start : start + block, :])
        change = part if change is None else change + part
    dispatch = dispatch_ref[...]
    upper = max_ref[...] * avail_ref[...]
    sent = dispatch.astype(BF16).astype(F32)
    to_upper = (upper.astype(BF16).astype(F32) - sent).astype(BF16).astype(F32)
    moved = jnp.minimum(jnp.maximum(dispatch + change, 0.0), upper)
    moved = jnp.where(change == to_upper, upper, moved)
    out_ref[...] = jnp.where(change == -sent, 0.0, moved)


def unpack(slot, back, dispatch, gen_max, availability):
    gens = slot.shape[0]
    devices, cap, hours = back.shape
    slots = devices * cap
    block = next(size for size in (768, 256, 128, 16) if slots % size == 0)
    return pl.pallas_call(
        functools.partial(unpack_kernel, block),
        out_shape=jax.ShapeDtypeStruct((gens, hours), F32),
        compiler_params=pltpu.CompilerParams(vmem_limit_bytes=LIMIT),
        cost_estimate=pl.CostEstimate(flops=2 * slots * gens * hours, bytes_accessed=1 << 20, transcendentals=0),
        name="unpack_dispatch",
    )(slot, back.reshape(slots, hours), dispatch, gen_max, availability)


def update_kernel(cap, first, last, parts, *refs):
    price_refs = refs[:parts]
    balance_ref, demand_ref, recv_ref, prev_ref, upd_ref, inj_ref, shadow_ref, acc_ref, extra_ref = refs[parts:]
    step = pl.program_id(0)
    buses, hours = demand_ref.shape

    @pl.when(step == 0)
    def _():
        shadow = price_refs[0][...].astype(F32)
        for ref in price_refs[1:]:
            shadow = shadow + ref[...].astype(F32)
        hi, lo = halves(shadow)
        shadow_ref[:hours, :] = hi
        shadow_ref[hours:, :] = lo
        acc_ref[...] = jnp.zeros(acc_ref.shape, F32)
        extra_ref[...] = jnp.zeros(extra_ref.shape, BF16)

    group = recv_ref.shape[0]
    pad = extra_ref.shape[0] // group
    wide = 2 * hours
    meta = recv_ref[:, cap:, :].reshape(group * META, wide)
    eye = (
        lax.broadcasted_iota(jnp.int32, (cap, wide), 0) == lax.broadcasted_iota(jnp.int32, (cap, wide), 1)
    ).astype(F32)
    columns = dot(eye.astype(BF16), meta, NT)
    buses_at = lax.broadcasted_iota(jnp.int32, (cap, buses), 1)
    picks = []
    for i in range(group):
        at = i * META
        bus_column = ((columns[:, at : at + 1] - 1.0) * 128.0 + columns[:, at + 1 : at + 2]).astype(jnp.int32)
        picks.append((buses_at == bus_column).astype(F32).astype(BF16))
    both = dot(jnp.concatenate(picks, axis=0), shadow_ref[...], NT)
    for i in range(group):
        at = i * META
        cost = (columns[:, at + 2 : at + 3] + columns[:, at + 3 : at + 4]) + columns[:, at + 4 : at + 5]
        rows = slice(i * cap, (i + 1) * cap)
        price = both[rows, :hours] + both[rows, hours:] + balance_ref[...]
        sent = recv_ref[i, :cap, :hours].astype(F32)
        dispatch = sent if first else prev_ref[i]
        upper = recv_ref[i, :cap, hours:].astype(F32)
        updated = jnp.minimum(jnp.maximum(dispatch - tau_step * (cost + price), 0.0), upper)
        if last:
            upd_ref[i] = (updated - sent).astype(BF16)
        else:
            upd_ref[i] = updated
        hi, lo = halves(2.0 * updated - dispatch)
        extra_ref[i * pad : i * pad + cap, :hours] = hi
        extra_ref[i * pad : i * pad + cap, hours:] = lo
    at_row = lax.broadcasted_iota(jnp.int32, (buses, pad), 0)
    picks = []
    for i in range(group):
        row = recv_ref[i, cap:, :pad].astype(F32)
        bus_row = ((row[0:1] - 1.0) * 128.0 + row[1:2]).astype(jnp.int32)
        picks.append((at_row == bus_row).astype(F32).astype(BF16))
    acc_ref[...] += dot(jnp.concatenate(picks, axis=1), extra_ref[...])

    @pl.when(step == pl.num_programs(0) - 1)
    def _():
        injection = acc_ref[:, :hours] + acc_ref[:, hours:] - demand_ref[...]
        inj_ref[:buses, :] = injection.astype(BF16)
        hi, mid, low = thirds(jnp.sum(injection, axis=0, keepdims=True))
        row = lax.broadcasted_iota(jnp.int32, (META, hours), 0)
        tail = jnp.where(row == 0, hi.astype(F32), 0.0)
        tail = jnp.where(row == 1, mid.astype(F32), tail)
        tail = jnp.where(row == 2, low.astype(F32), tail)
        inj_ref[buses:, :] = tail.astype(BF16)


def update(cap, first, last, prices, balance_price, demand, recv, previous):
    devices = recv.shape[0]
    buses, hours = demand.shape
    full = lambda *shape: pl.BlockSpec(shape, lambda i: (0,) * len(shape))
    slots = lambda width: pl.BlockSpec((GROUP, cap, width), lambda i: (i, 0, 0))
    if first:
        previous, prev_spec = balance_price, full(1, hours)
    else:
        prev_spec = slots(hours)
    return pl.pallas_call(
        functools.partial(update_kernel, cap, first, last, len(prices)),
        grid=(devices // GROUP,),
        out_shape=(
            jax.ShapeDtypeStruct((devices, cap, hours), BF16 if last else F32),
            jax.ShapeDtypeStruct((buses + META, hours), BF16),
        ),
        in_specs=[full(hours, buses)] * len(prices)
        + [
            full(1, hours),
            full(buses, hours),
            pl.BlockSpec((GROUP, cap + META, 2 * hours), lambda i: (i, 0, 0)),
            prev_spec,
        ],
        out_specs=(slots(hours), full(buses + META, hours)),
        scratch_shapes=[
            pltpu.VMEM((2 * hours, buses), BF16),
            pltpu.VMEM((buses, 2 * hours), F32),
            pltpu.VMEM((GROUP * (-(-cap // 128) * 128), 2 * hours), BF16),
        ],
        compiler_params=pltpu.CompilerParams(vmem_limit_bytes=LIMIT),
        cost_estimate=pl.CostEstimate(flops=8 * devices * cap * buses * hours, bytes_accessed=4 << 20, transcendentals=0),
        name="update_generators",
    )(*prices, balance_price, demand, recv, previous)


def shadow_kernel(place_ref, line_ref, *refs):
    ptdf_refs, (keep_ref, send_ref) = refs[:-2], refs[-2:]
    step = pl.program_id(0)
    depth = ptdf_refs[0].shape[0]
    part = dot(line_ref[:, :depth], ptdf_refs[0][...])
    for i, ref in enumerate(ptdf_refs[1:], 1):
        part = part + dot(line_ref[:, i * depth : (i + 1) * depth], ref[...])

    @pl.when(step == 0)
    def _():
        send_ref[1] = part.astype(BF16)

    @pl.when(step == 1)
    def _():
        keep_ref[1] = part

    @pl.when(step == 2)
    def _():
        send_ref[0] = part.astype(BF16)

    @pl.when(step == 3)
    def _():
        keep_ref[0] = part


def shadow_chunk(chunk, place, line_t, ptdf, buses):
    hours, lines = line_t.shape
    pieces = 5
    return pl.pallas_call(
        shadow_kernel,
        grid_spec=pltpu.PrefetchScalarGridSpec(
            num_scalar_prefetch=1,
            grid=(4,),
            in_specs=[
                pl.BlockSpec((hours, lines), lambda i, place: (0, 0)),
            ]
            + [
                pl.BlockSpec((lines // pieces, buses), lambda i, place, p=p: (p, place[0] ^ (4 * chunk + 3 - i)))
                for p in range(pieces)
            ],
            out_specs=(
                pl.BlockSpec((2, hours, buses), lambda i, place: (0, 0, 0)),
                pl.BlockSpec((2, hours, buses), lambda i, place: (0, 0, 0)),
            ),
        ),
        out_shape=(
            jax.ShapeDtypeStruct((2, hours, buses), F32),
            jax.ShapeDtypeStruct((2, hours, buses), BF16),
        ),
        compiler_params=pltpu.CompilerParams(vmem_limit_bytes=LIMIT),
        cost_estimate=pl.CostEstimate(
            flops=COST * 8 * hours * lines * buses, bytes_accessed=8 * lines * buses, transcendentals=0
        ),
        name="shadow_chunk",
    )(place, line_t, *[ptdf] * pieces)


def flow_kernel(start, end, pieces, place_ref, *refs):
    ptdf_refs = refs[:pieces]
    b0, b1, b2, b3, acc_ref, sum_ref, *rest = refs[pieces:]
    step = pl.program_id(0)
    if end:
        limit_ref, line_ref, out_ref, half_ref, sum_out, inj_ref = rest
    else:
        out_ref, sum_out, inj_ref = rest
    buses = inj_ref.shape[0] // 4

    @pl.when(step == 0)
    def _():
        total = jnp.zeros(sum_ref.shape, F32) if start else sum_ref[...]
        for rel, ref in enumerate((b0, b1, b2, b3)):
            offset = pl.multiple_of(((place_ref[0] ^ rel) & 3) * buses, META)
            inj_ref[pl.ds(offset, buses), :] = ref[:buses, :]
            tail = ref[buses:, :].astype(F32)
            total = total + jnp.sum(tail, axis=0, keepdims=True)
        sum_out[...] = total

    tile, depth = ptdf_refs[0].shape
    inj = inj_ref[pl.ds(pl.multiple_of(step * depth, depth), depth), :]
    parts = [dot(ref[...], inj) for ref in ptdf_refs]

    @pl.when(step == 0)
    def _():
        for i, part in enumerate(parts):
            rows = slice(i * tile, (i + 1) * tile)
            out_ref[rows, :] = part if start else acc_ref[rows, :] + part

    @pl.when(step > 0)
    def _():
        for i, part in enumerate(parts):
            out_ref[i * tile : (i + 1) * tile, :] += part

    if end:

        @pl.when(step == pl.num_programs(0) - 1)
        def _():
            shifted = line_ref[...] + sigma_step * out_ref[...]
            limit = limit_ref[...]
            line = shifted - sigma_step * jnp.minimum(jnp.maximum(shifted / sigma_step, -limit), limit)
            out_ref[...] = line
            half_ref[...] = line.astype(BF16)


def flow_chunk(chunk, place, ptdf, blocks, acc, total, limit=None, line=None):
    lines = ptdf.shape[0]
    rows, hours = blocks[0].shape
    buses = rows - META
    start, end = acc is None, limit is not None
    steps, pieces = 5, 4
    depth = 4 * buses // steps
    full = lambda *shape: pl.BlockSpec(shape, lambda i, place: (0,) * len(shape))
    if start:
        acc, acc_spec = total, full(1, hours)
    else:
        acc_spec = full(lines, hours)
    operands = [ptdf] * pieces + [*blocks, acc, total]
    in_specs = [
        pl.BlockSpec((lines // pieces, depth), lambda i, place, p=p: (p, ((place[0] >> 2) ^ chunk) * steps + i))
        for p in range(pieces)
    ]
    in_specs += [full(rows, hours)] * 4 + [acc_spec, full(1, hours)]
    out_shape = [jax.ShapeDtypeStruct((lines, hours), F32)]
    out_specs = [full(lines, hours)]
    if end:
        operands += [limit, line]
        in_specs += [full(lines, 1), full(lines, hours)]
        out_shape += [jax.ShapeDtypeStruct((lines, hours), BF16)]
        out_specs += [full(lines, hours)]
    out_shape += [jax.ShapeDtypeStruct((1, hours), F32)]
    out_specs += [full(1, hours)]
    return pl.pallas_call(
        functools.partial(flow_kernel, start, end, pieces),
        grid_spec=pltpu.PrefetchScalarGridSpec(
            num_scalar_prefetch=1,
            grid=(steps,),
            in_specs=in_specs,
            out_specs=tuple(out_specs),
            scratch_shapes=[pltpu.VMEM((4 * buses, hours), BF16)],
        ),
        out_shape=tuple(out_shape),
        compiler_params=pltpu.CompilerParams(vmem_limit_bytes=LIMIT),
        cost_estimate=pl.CostEstimate(
            flops=COST * 8 * hours * lines * buses, bytes_accessed=8 * lines * buses, transcendentals=0
        ),
        name="flow_chunk",
    )(place, *operands)


def swap(x, devices, mask):
    return lax.ppermute(x, "bus", [(i, i ^ mask) for i in range(devices)])


def local(
    ptdf,
    line_limit,
    gen_cost,
    gen_max,
    gen_owner,
    gen_local,
    availability,
    demand,
    dispatch,
    balance_price,
    line_price,
):
    devices = lax.axis_size("bus")
    place = lax.axis_index("bus").astype(jnp.int32).reshape(1)
    buses = demand.shape[0]
    all_buses = buses * devices
    gens, hours = dispatch.shape
    cap = -(-max(2, 3 * gens // devices) // 16) * 16
    staged = devices == 16 and buses % 128 == 0

    outgoing = pack(
        devices,
        cap,
        gen_owner,
        gen_local,
        gen_cost,
        dispatch,
        gen_max,
        availability,
    )
    limit = line_limit.reshape(-1, 1)
    balance_row = balance_price.reshape(1, hours)
    line_half = line_price.astype(BF16)
    recv = lax.all_to_all(outgoing, "bus", split_axis=0, concat_axis=0, tiled=True)
    slot = None if staged else slot_column(devices, cap, gen_owner)
    held = None
    for iteration in range(ITERS):
        last = iteration == ITERS - 1
        if staged:
            line_t = line_half.T
            keeps, gots, crossed, parts = {}, {}, {}, {}

            def across(chunk):
                both = (keeps[chunk][1] + gots[chunk][1].astype(F32)).astype(BF16)
                crossed[chunk] = swap(both, devices, 2)
                return both

            def settle(chunk):
                part = keeps[chunk][0] + gots[chunk][0].astype(F32) + crossed[chunk].astype(F32)
                if chunk == 2:
                    part = part + parts[3].astype(F32)
                if chunk:
                    part = part.astype(BF16)
                    parts[chunk] = swap(part, devices, 8 if chunk == 2 else 4)
                else:
                    parts[chunk] = part
                return part

            def product(chunk, line_t):
                keeps[chunk], send = shadow_chunk(chunk, place, line_t, ptdf, buses)
                gots[chunk] = swap(send, devices, 1)

            product(3, line_t)
            if iteration == 0:
                line_t, _ = lax.optimization_barrier((line_t, outgoing))
            product(2, line_t)
            line_t, _ = lax.optimization_barrier((line_t, across(3)))
            product(1, line_t)
            line_t, _, _ = lax.optimization_barrier((line_t, across(2), settle(3)))
            product(0, line_t)
            across(1)
            settle(2)
            across(0)
            settle(1)
            settle(0)
            prices = [parts[0], parts[1], parts[2]]
        else:
            shadow = lax.dot_general(ptdf, line_half, (((0,), (0,)), ((), ())), preferred_element_type=F32)
            prices = [lax.psum_scatter(shadow, "bus", scatter_dimension=0, tiled=True).T]
        held, block = update(cap, iteration == 0, last, prices, balance_row, demand, recv, held)
        if staged:
            near, far, cross, far_cross = {0: block}, {}, {}, {}

            def spread(chunk):
                far[chunk] = swap(near[chunk], devices, 2)
                cross[chunk] = swap(near[chunk], devices, 1)

            def settle_far(chunk):
                far_cross[chunk] = swap(far[chunk], devices, 1)

            def blocks(chunk):
                return [near[chunk], cross[chunk], far[chunk], far_cross[chunk]]

            near[2] = swap(block, devices, 8)
            near[1] = swap(block, devices, 4)
            spread(0)
            near[3] = swap(near[2], devices, 4)
            spread(1)
            spread(2)
            settle_far(0)
            near[1], near[2], row = lax.optimization_barrier((near[1], near[2], balance_row))
            acc, total = flow_chunk(0, place, ptdf, blocks(0), None, row)
            if iteration == 0:
                owner, acc = lax.optimization_barrier((gen_owner, acc))
                slot = slot_column(devices, cap, owner)
            near[3], acc = lax.optimization_barrier((near[3], acc))
            spread(3)
            if last:
                held, _ = lax.optimization_barrier((held, near[3]))
                back = lax.all_to_all(held, "bus", split_axis=0, concat_axis=0, tiled=True)
            settle_far(1)
            acc, total = flow_chunk(1, place, ptdf, blocks(1), acc, total)
            settle_far(2)
            far[3], acc = lax.optimization_barrier((far[3], acc))
            acc, total = flow_chunk(2, place, ptdf, blocks(2), acc, total)
            settle_far(3)
            line_price, line_half, total = flow_chunk(
                3, place, ptdf, blocks(3), acc, total, limit, line_price
            )
            balance = total
        else:
            if last:
                back = lax.all_to_all(held, "bus", split_axis=0, concat_axis=0, tiled=True)
            every = lax.all_gather(block, "bus", axis=0, tiled=False)
            balance = jnp.sum(every[:, buses:].astype(F32), axis=(0, 1)).reshape(1, hours)
            flow = jnp.dot(ptdf, every[:, :buses].reshape(all_buses, hours), preferred_element_type=F32)
            shifted = line_price + sigma_step * flow
            line_price = shifted - sigma_step * jnp.clip(shifted / sigma_step, -limit, limit)
            line_half = line_price.astype(BF16)
        balance_row = balance_row + sigma_step * balance / all_buses
    dispatch = unpack(slot, back, dispatch, gen_max.reshape(gens, 1), availability)
    return (dispatch, balance_row.reshape(hours), line_price)


def solution(mesh):
    return jax.shard_map(
        local,
        mesh=mesh,
        in_specs=(
            P("bus", None),
            P("bus"),
            P("bus"),
            P("bus"),
            P("bus", None),
            P("bus"),
            P(("cases", "bus"), None),
            P(("cases", "bus"), None),
            P(("cases", "bus"), None),
            P("cases"),
            P(("cases", "bus"), None),
        ),
        out_specs=(P(("cases", "bus"), None), P("cases"), P(("cases", "bus"), None)),
        check_vma=False,
    )
```

```python
import functools

import jax
import jax.numpy as jnp
from jax import lax
from jax.experimental import pallas as pl
from jax.experimental.pallas import tpu as pltpu
from jax.sharding import PartitionSpec as P

ITERS = 2

tau_step = 0.2
sigma_step = 0.15

GROUP = 4
LIMIT = 16 << 20
COST = 3
META = 16
F32 = jnp.float32
BF16 = jnp.bfloat16
NT = (((1,), (1,)), ((), ()))
NN = (((1,), (0,)), ((), ()))


def dot(a, b, dims=NN):
    return lax.dot_general(a, b, dims, preferred_element_type=F32)


def halves(x):
    hi = x.astype(BF16)
    lo = (x - hi.astype(F32)).astype(BF16)
    return hi, lo


def thirds(x):
    hi = x.astype(BF16)
    rest = x - hi.astype(F32)
    mid = rest.astype(BF16)
    low = (rest - mid.astype(F32)).astype(BF16)
    return hi, mid, low


def as_row(ref):
    return jnp.concatenate([ref[i : i + 1, :] for i in range(ref.shape[0])], axis=1)


def pack_kernel(cap, owner_ref, local_ref, cost_ref, dispatch_ref, max_ref, avail_ref, out_ref, slot_ref, pay_ref, meta_ref):
    step = pl.program_id(0)
    gens, hours = dispatch_ref.shape
    group = out_ref.shape[0]

    @pl.when(step == 0)
    def _():
        owner = as_row(owner_ref)
        hits = (lax.broadcasted_iota(jnp.int32, (slot_ref.shape[0], gens), 0) == owner).astype(F32)
        before = (
            lax.broadcasted_iota(jnp.int32, (gens, gens), 0) < lax.broadcasted_iota(jnp.int32, (gens, gens), 1)
        ).astype(F32)
        count = dot(hits.astype(BF16), before.astype(BF16))
        rank = jnp.sum(count * hits, axis=0, keepdims=True).astype(jnp.int32)
        slot_ref[...] = jnp.broadcast_to(owner * cap + rank, slot_ref.shape)
        pay_ref[:, :hours] = dispatch_ref[...].astype(BF16)
        lanes = max_ref.shape[1]
        eye = (
            lax.broadcasted_iota(jnp.int32, (lanes, lanes), 0) == lax.broadcasted_iota(jnp.int32, (lanes, lanes), 1)
        ).astype(F32)
        for i in range(gens // lanes):
            rows = slice(i * lanes, (i + 1) * lanes)
            most = jnp.sum(eye * max_ref[i : i + 1, :], axis=1, keepdims=True)
            pay_ref[rows, hours:] = (most * avail_ref[rows, :]).astype(BF16)
        local = as_row(local_ref)
        hi, mid, low = thirds(as_row(cost_ref))
        row = lax.broadcasted_iota(jnp.int32, (META, gens), 0)
        parts = [
            (lax.shift_right_logical(local, 7) + 1).astype(F32),
            (local & 127).astype(F32),
            hi.astype(F32),
            mid.astype(F32),
            low.astype(F32),
        ]
        meta = jnp.zeros((META, gens), F32)
        for i, part in enumerate(parts):
            meta = jnp.where(row == i, part, meta)
        meta_ref[...] = meta.astype(BF16)

    slot = slot_ref[0:1, :] - step * (group * cap)
    place = lax.broadcasted_iota(jnp.int32, (cap, gens), 0)
    picks = [(place == slot - i * cap).astype(F32).astype(BF16) for i in range(group)]
    moved = dot(jnp.concatenate(picks, axis=0), pay_ref[...]).astype(BF16)
    for i in range(group):
        out_ref[i, :cap, :] = moved[i * cap : (i + 1) * cap]
        out_ref[i, cap:, :] = jnp.zeros((META, 2 * hours), BF16)
        out_ref[i, cap:, :cap] = dot(meta_ref[...], picks[i], NT).astype(BF16)


def pack(devices, cap, owner, local_bus, cost, dispatch, gen_max, availability):
    gens, hours = dispatch.shape
    full = lambda *shape: pl.BlockSpec(shape, lambda i: (0,) * len(shape))
    folded = (gens // 128, 128)
    return pl.pallas_call(
        functools.partial(pack_kernel, cap),
        grid=(devices // GROUP,),
        out_shape=jax.ShapeDtypeStruct((devices, cap + META, 2 * hours), BF16),
        in_specs=[
            full(*folded),
            full(*folded),
            full(*folded),
            full(gens, hours),
            full(*folded),
            full(gens, hours),
        ],
        out_specs=pl.BlockSpec((GROUP, cap + META, 2 * hours), lambda i: (i, 0, 0)),
        scratch_shapes=[
            pltpu.VMEM((devices, gens), jnp.int32),
            pltpu.VMEM((gens, 2 * hours), BF16),
            pltpu.VMEM((META, gens), BF16),
        ],
        compiler_params=pltpu.CompilerParams(vmem_limit_bytes=LIMIT),
        cost_estimate=pl.CostEstimate(flops=4 * devices * cap * gens * hours, bytes_accessed=3 << 20, transcendentals=0),
        name="pack_generators",
    )(
        owner.reshape(folded),
        local_bus.reshape(folded),
        cost.reshape(folded),
        dispatch,
        gen_max.reshape(folded),
        availability,
    )


def slot_kernel(devices, cap, owner_ref, slot_ref):
    gens = owner_ref.shape[0]
    owner = owner_ref[...]
    hits = (lax.broadcasted_iota(jnp.int32, (gens, devices), 1) == owner).astype(F32)
    before = (
        lax.broadcasted_iota(jnp.int32, (gens, gens), 1) < lax.broadcasted_iota(jnp.int32, (gens, gens), 0)
    ).astype(F32)
    count = dot(before.astype(BF16), hits.astype(BF16))
    rank = jnp.sum(count * hits, axis=1, keepdims=True).astype(jnp.int32)
    slot_ref[...] = owner * cap + rank


def slot_column(devices, cap, owner_column):
    return pl.pallas_call(
        functools.partial(slot_kernel, devices, cap),
        out_shape=jax.ShapeDtypeStruct(owner_column.shape, jnp.int32),
        compiler_params=pltpu.CompilerParams(vmem_limit_bytes=LIMIT),
        name="slot_column",
    )(owner_column)


def unpack_kernel(block, slot_ref, back_ref, dispatch_ref, max_ref, avail_ref, out_ref):
    gens = slot_ref.shape[0]
    slot = slot_ref[...]
    at = lax.broadcasted_iota(jnp.int32, (gens, block), 1)
    change = None
    for start in range(0, back_ref.shape[0], block):
        pick = (at == slot - start).astype(F32).astype(BF16)
        part = dot(pick, back_ref[start : start + block, :])
        change = part if change is None else change + part
    dispatch = dispatch_ref[...]
    upper = max_ref[...] * avail_ref[...]
    sent = dispatch.astype(BF16).astype(F32)
    to_upper = (upper.astype(BF16).astype(F32) - sent).astype(BF16).astype(F32)
    moved = jnp.minimum(jnp.maximum(dispatch + change, 0.0), upper)
    moved = jnp.where(change == to_upper, upper, moved)
    out_ref[...] = jnp.where(change == -sent, 0.0, moved)


def unpack(slot, back, dispatch, gen_max, availability):
    gens = slot.shape[0]
    devices, cap, hours = back.shape
    slots = devices * cap
    block = next(size for size in (768, 256, 128, 16) if slots % size == 0)
    return pl.pallas_call(
        functools.partial(unpack_kernel, block),
        out_shape=jax.ShapeDtypeStruct((gens, hours), F32),
        compiler_params=pltpu.CompilerParams(vmem_limit_bytes=LIMIT),
        cost_estimate=pl.CostEstimate(flops=2 * slots * gens * hours, bytes_accessed=1 << 20, transcendentals=0),
        name="unpack_dispatch",
    )(slot, back.reshape(slots, hours), dispatch, gen_max, availability)


def update_kernel(cap, first, last, parts, *refs):
    price_refs = refs[:parts]
    balance_ref, demand_ref, recv_ref, prev_ref, upd_ref, inj_ref, shadow_ref, acc_ref, extra_ref = refs[parts:]
    step = pl.program_id(0)
    buses, hours = demand_ref.shape

    @pl.when(step == 0)
    def _():
        shadow = price_refs[0][...].astype(F32)
        for ref in price_refs[1:]:
            shadow = shadow + ref[...].astype(F32)
        hi, lo = halves(shadow)
        shadow_ref[:hours, :] = hi
        shadow_ref[hours:, :] = lo
        acc_ref[...] = jnp.zeros(acc_ref.shape, F32)
        extra_ref[...] = jnp.zeros(extra_ref.shape, BF16)

    group = recv_ref.shape[0]
    pad = extra_ref.shape[0] // group
    wide = 2 * hours
    meta = recv_ref[:, cap:, :].reshape(group * META, wide)
    eye = (
        lax.broadcasted_iota(jnp.int32, (cap, wide), 0) == lax.broadcasted_iota(jnp.int32, (cap, wide), 1)
    ).astype(F32)
    columns = dot(eye.astype(BF16), meta, NT)
    buses_at = lax.broadcasted_iota(jnp.int32, (cap, buses), 1)
    picks = []
    for i in range(group):
        at = i * META
        bus_column = ((columns[:, at : at + 1] - 1.0) * 128.0 + columns[:, at + 1 : at + 2]).astype(jnp.int32)
        picks.append((buses_at == bus_column).astype(F32).astype(BF16))
    both = dot(jnp.concatenate(picks, axis=0), shadow_ref[...], NT)
    for i in range(group):
        at = i * META
        cost = (columns[:, at + 2 : at + 3] + columns[:, at + 3 : at + 4]) + columns[:, at + 4 : at + 5]
        rows = slice(i * cap, (i + 1) * cap)
        price = both[rows, :hours] + both[rows, hours:] + balance_ref[...]
        sent = recv_ref[i, :cap, :hours].astype(F32)
        dispatch = sent if first else prev_ref[i]
        upper = recv_ref[i, :cap, hours:].astype(F32)
        updated = jnp.minimum(jnp.maximum(dispatch - tau_step * (cost + price), 0.0), upper)
        if last:
            upd_ref[i] = (updated - sent).astype(BF16)
        else:
            upd_ref[i] = updated
        hi, lo = halves(2.0 * updated - dispatch)
        extra_ref[i * pad : i * pad + cap, :hours] = hi
        extra_ref[i * pad : i * pad + cap, hours:] = lo
    at_row = lax.broadcasted_iota(jnp.int32, (buses, pad), 0)
    picks = []
    for i in range(group):
        row = recv_ref[i, cap:, :pad].astype(F32)
        bus_row = ((row[0:1] - 1.0) * 128.0 + row[1:2]).astype(jnp.int32)
        picks.append((at_row == bus_row).astype(F32).astype(BF16))
    acc_ref[...] += dot(jnp.concatenate(picks, axis=1), extra_ref[...])

    @pl.when(step == pl.num_programs(0) - 1)
    def _():
        injection = acc_ref[:, :hours] + acc_ref[:, hours:] - demand_ref[...]
        inj_ref[:buses, :] = injection.astype(BF16)
        hi, mid, low = thirds(jnp.sum(injection, axis=0, keepdims=True))
        row = lax.broadcasted_iota(jnp.int32, (META, hours), 0)
        tail = jnp.where(row == 0, hi.astype(F32), 0.0)
        tail = jnp.where(row == 1, mid.astype(F32), tail)
        tail = jnp.where(row == 2, low.astype(F32), tail)
        inj_ref[buses:, :] = tail.astype(BF16)


def update(cap, first, last, prices, balance_price, demand, recv, previous):
    devices = recv.shape[0]
    buses, hours = demand.shape
    full = lambda *shape: pl.BlockSpec(shape, lambda i: (0,) * len(shape))
    slots = lambda width: pl.BlockSpec((GROUP, cap, width), lambda i: (i, 0, 0))
    if first:
        previous, prev_spec = balance_price, full(1, hours)
    else:
        prev_spec = slots(hours)
    return pl.pallas_call(
        functools.partial(update_kernel, cap, first, last, len(prices)),
        grid=(devices // GROUP,),
        out_shape=(
            jax.ShapeDtypeStruct((devices, cap, hours), BF16 if last else F32),
            jax.ShapeDtypeStruct((buses + META, hours), BF16),
        ),
        in_specs=[full(hours, buses)] * len(prices)
        + [
            full(1, hours),
            full(buses, hours),
            pl.BlockSpec((GROUP, cap + META, 2 * hours), lambda i: (i, 0, 0)),
            prev_spec,
        ],
        out_specs=(slots(hours), full(buses + META, hours)),
        scratch_shapes=[
            pltpu.VMEM((2 * hours, buses), BF16),
            pltpu.VMEM((buses, 2 * hours), F32),
            pltpu.VMEM((GROUP * (-(-cap // 128) * 128), 2 * hours), BF16),
        ],
        compiler_params=pltpu.CompilerParams(vmem_limit_bytes=LIMIT),
        cost_estimate=pl.CostEstimate(flops=8 * devices * cap * buses * hours, bytes_accessed=4 << 20, transcendentals=0),
        name="update_generators",
    )(*prices, balance_price, demand, recv, previous)


def shadow_kernel(chunk, fetch, place_ref, line_ref, ptdf_ref, keep_ref, send_ref, *rest):
    buses = keep_ref.shape[2]
    columns = [slice(rel * buses, (rel + 1) * buses) for rel in range(4)]
    if fetch:
        held_ref, sems = rest
        copies = []
        for rel in range(4):
            start = pl.multiple_of((place_ref[0] ^ (4 * chunk + rel)) * buses, 128)
            copies.append(
                pltpu.make_async_copy(
                    ptdf_ref.at[:, pl.ds(start, buses)], held_ref.at[:, pl.ds(rel * buses, buses)], sems.at[rel]
                )
            )
        for rel in (3, 2, 1, 0):
            copies[rel].start()
    else:
        held_ref = ptdf_ref

    def part(rel):
        if fetch:
            copies[rel].wait()
        return dot(line_ref[...], held_ref[:, columns[rel]])

    send_ref[1] = part(3).astype(BF16)
    keep_ref[1] = part(2)
    send_ref[0] = part(1).astype(BF16)
    keep_ref[0] = part(0)


def shadow_chunk(chunk, fetch, place, line_t, ptdf, buses):
    hours, lines = line_t.shape
    vmem = pl.BlockSpec(memory_space=pltpu.VMEM)
    out_shape = [
        jax.ShapeDtypeStruct((2, hours, buses), F32),
        jax.ShapeDtypeStruct((2, hours, buses), BF16),
    ]
    if fetch:
        out_shape.append(pltpu.VMEM((lines, 4 * buses), BF16))
    return pl.pallas_call(
        functools.partial(shadow_kernel, chunk, fetch),
        in_specs=[pl.BlockSpec(memory_space=pltpu.SMEM), vmem, pl.BlockSpec(memory_space=pltpu.MemorySpace.HBM) if fetch else vmem],
        out_specs=tuple([vmem] * len(out_shape)),
        out_shape=tuple(out_shape),
        scratch_shapes=[pltpu.SemaphoreType.DMA((4,))] if fetch else [],
        compiler_params=pltpu.CompilerParams(vmem_limit_bytes=LIMIT),
        cost_estimate=pl.CostEstimate(
            flops=COST * 8 * hours * lines * buses, bytes_accessed=8 * lines * buses, transcendentals=0
        ),
        name="shadow_chunk",
    )(place, line_t, pltpu.with_memory_space_constraint(ptdf, pltpu.MemorySpace.HBM) if fetch else ptdf)


def flow_kernel(start, end, ptdf_ref, b0, b1, b2, b3, acc_ref, sum_ref, *rest):
    if end:
        limit_ref, line_ref, out_ref, half_ref, sum_out, inj_ref = rest
    else:
        out_ref, sum_out, inj_ref = rest
    buses = inj_ref.shape[0] // 4
    total = jnp.zeros(sum_ref.shape, F32) if start else sum_ref[...]
    for rel, ref in enumerate((b0, b1, b2, b3)):
        inj_ref[rel * buses : (rel + 1) * buses, :] = ref[:buses, :]
        tail = ref[buses:, :].astype(F32)
        total = total + jnp.sum(tail, axis=0, keepdims=True)
    sum_out[...] = total
    tile = ptdf_ref.shape[0] // 4

    def body(i, carry):
        rows = pl.ds(pl.multiple_of(i * tile, tile), tile)
        flow = dot(ptdf_ref[rows, :], inj_ref[...])
        if not start:
            flow = flow + acc_ref[rows, :]
        if end:
            shifted = line_ref[rows, :] + sigma_step * flow
            limit = limit_ref[rows, :]
            line = shifted - sigma_step * jnp.minimum(jnp.maximum(shifted / sigma_step, -limit), limit)
            out_ref[rows, :] = line
            half_ref[rows, :] = line.astype(BF16)
        else:
            out_ref[rows, :] = flow
        return carry

    lax.fori_loop(0, 4, body, 0)


def flow_chunk(ptdf, blocks, acc, total, limit=None, line=None):
    lines = ptdf.shape[0]
    rows, hours = blocks[0].shape
    buses = rows - META
    start, end = acc is None, limit is not None
    operands = [ptdf, *blocks, total if start else acc, total]
    out_shape = [jax.ShapeDtypeStruct((lines, hours), F32)]
    if end:
        operands += [limit, line]
        out_shape += [jax.ShapeDtypeStruct((lines, hours), BF16)]
    out_shape += [jax.ShapeDtypeStruct((1, hours), F32)]
    in_specs = [pl.BlockSpec(memory_space=pltpu.VMEM)] * len(operands)
    return pl.pallas_call(
        functools.partial(flow_kernel, start, end),
        in_specs=in_specs,
        out_shape=tuple(out_shape),
        scratch_shapes=[pltpu.VMEM((4 * buses, hours), BF16)],
        compiler_params=pltpu.CompilerParams(vmem_limit_bytes=LIMIT),
        cost_estimate=pl.CostEstimate(
            flops=COST * 8 * hours * lines * buses, bytes_accessed=8 * lines * buses, transcendentals=0
        ),
        name="flow_chunk",
    )(*operands)


def swap(x, devices, mask):
    return lax.ppermute(x, "bus", [(i, i ^ mask) for i in range(devices)])


def local(
    ptdf,
    line_limit,
    gen_cost,
    gen_max,
    gen_owner,
    gen_local,
    availability,
    demand,
    dispatch,
    balance_price,
    line_price,
):
    devices = lax.axis_size("bus")
    place = lax.axis_index("bus").astype(jnp.int32).reshape(1)
    buses = demand.shape[0]
    all_buses = buses * devices
    gens, hours = dispatch.shape
    cap = -(-max(2, 3 * gens // devices) // 16) * 16
    staged = devices == 16 and buses % 128 == 0

    outgoing = pack(
        devices,
        cap,
        gen_owner,
        gen_local,
        gen_cost,
        dispatch,
        gen_max,
        availability,
    )
    limit = line_limit.reshape(-1, 1)
    balance_row = balance_price.reshape(1, hours)
    line_half = line_price.astype(BF16)
    recv = lax.all_to_all(outgoing, "bus", split_axis=0, concat_axis=0, tiled=True)
    slot = None if staged else slot_column(devices, cap, gen_owner)
    held, resident = None, {}
    for iteration in range(ITERS):
        last = iteration == ITERS - 1
        if staged:
            line_t = line_half.T
            keeps, gots, crossed, parts = {}, {}, {}, {}

            def across(chunk):
                both = (keeps[chunk][1] + gots[chunk][1].astype(F32)).astype(BF16)
                crossed[chunk] = swap(both, devices, 2)
                return both

            def settle(chunk):
                part = keeps[chunk][0] + gots[chunk][0].astype(F32) + crossed[chunk].astype(F32)
                if chunk == 2:
                    part = part + parts[3].astype(F32)
                if chunk:
                    part = part.astype(BF16)
                    parts[chunk] = swap(part, devices, 8 if chunk == 2 else 4)
                else:
                    parts[chunk] = part
                return part

            def product(chunk, line_t):
                if chunk in resident:
                    keeps[chunk], send = shadow_chunk(chunk, False, place, line_t, resident[chunk], buses)
                else:
                    keeps[chunk], send, resident[chunk] = shadow_chunk(chunk, True, place, line_t, ptdf, buses)
                gots[chunk] = swap(send, devices, 1)

            product(3, line_t)
            if iteration == 0:
                line_t, _ = lax.optimization_barrier((line_t, outgoing))
            product(2, line_t)
            line_t, _ = lax.optimization_barrier((line_t, across(3)))
            product(1, line_t)
            line_t, _, _ = lax.optimization_barrier((line_t, across(2), settle(3)))
            product(0, line_t)
            across(1)
            settle(2)
            across(0)
            settle(1)
            settle(0)
            prices = [parts[0], parts[1], parts[2]]
        else:
            shadow = lax.dot_general(ptdf, line_half, (((0,), (0,)), ((), ())), preferred_element_type=F32)
            prices = [lax.psum_scatter(shadow, "bus", scatter_dimension=0, tiled=True).T]
        held, block = update(cap, iteration == 0, last, prices, balance_row, demand, recv, held)
        if staged:
            near, far, cross, far_cross = {0: block}, {}, {}, {}

            def spread(chunk):
                far[chunk] = swap(near[chunk], devices, 2)
                cross[chunk] = swap(near[chunk], devices, 1)

            def settle_far(chunk):
                far_cross[chunk] = swap(far[chunk], devices, 1)

            def blocks(chunk):
                return [near[chunk], cross[chunk], far[chunk], far_cross[chunk]]

            near[2] = swap(block, devices, 8)
            near[1] = swap(block, devices, 4)
            spread(0)
            near[3] = swap(near[2], devices, 4)
            spread(1)
            spread(2)
            settle_far(0)
            near[1], near[2], row = lax.optimization_barrier((near[1], near[2], balance_row))
            acc, total = flow_chunk(resident[0], blocks(0), None, row)
            if iteration == 0:
                owner, acc = lax.optimization_barrier((gen_owner, acc))
                slot = slot_column(devices, cap, owner)
            near[3], acc = lax.optimization_barrier((near[3], acc))
            spread(3)
            if last:
                held, _ = lax.optimization_barrier((held, near[3]))
                back = lax.all_to_all(held, "bus", split_axis=0, concat_axis=0, tiled=True)
            settle_far(1)
            acc, total = flow_chunk(resident[1], blocks(1), acc, total)
            settle_far(2)
            far[3], acc = lax.optimization_barrier((far[3], acc))
            acc, total = flow_chunk(resident[2], blocks(2), acc, total)
            settle_far(3)
            line_price, line_half, total = flow_chunk(
                resident[3], blocks(3), acc, total, limit, line_price
            )
            balance = total
        else:
            if last:
                back = lax.all_to_all(held, "bus", split_axis=0, concat_axis=0, tiled=True)
            every = lax.all_gather(block, "bus", axis=0, tiled=False)
            balance = jnp.sum(every[:, buses:].astype(F32), axis=(0, 1)).reshape(1, hours)
            flow = jnp.dot(ptdf, every[:, :buses].reshape(all_buses, hours), preferred_element_type=F32)
            shifted = line_price + sigma_step * flow
            line_price = shifted - sigma_step * jnp.clip(shifted / sigma_step, -limit, limit)
            line_half = line_price.astype(BF16)
        balance_row = balance_row + sigma_step * balance / all_buses
    dispatch = unpack(slot, back, dispatch, gen_max.reshape(gens, 1), availability)
    return (dispatch, balance_row.reshape(hours), line_price)


def solution(mesh):
    return jax.shard_map(
        local,
        mesh=mesh,
        in_specs=(
            P("bus", None),
            P("bus"),
            P("bus"),
            P("bus"),
            P("bus", None),
            P("bus"),
            P(("cases", "bus"), None),
            P(("cases", "bus"), None),
            P(("cases", "bus"), None),
            P("cases"),
            P(("cases", "bus"), None),
        ),
        out_specs=(P(("cases", "bus"), None), P("cases"), P(("cases", "bus"), None)),
        check_vma=False,
    )
```

```python
import functools

import jax
import jax.numpy as jnp
from jax import lax
from jax.experimental import pallas as pl
from jax.experimental.pallas import tpu as pltpu
from jax.sharding import PartitionSpec as P

ITERS = 2

tau_step = 0.2
sigma_step = 0.15

GROUP = 4
LIMIT = 12 << 20
COST = 3
META = 16
F32 = jnp.float32
BF16 = jnp.bfloat16
NT = (((1,), (1,)), ((), ()))
NN = (((1,), (0,)), ((), ()))


def dot(a, b, dims=NN):
    return lax.dot_general(a, b, dims, preferred_element_type=F32)


def halves(x):
    hi = x.astype(BF16)
    lo = (x - hi.astype(F32)).astype(BF16)
    return hi, lo


def thirds(x):
    hi = x.astype(BF16)
    rest = x - hi.astype(F32)
    mid = rest.astype(BF16)
    low = (rest - mid.astype(F32)).astype(BF16)
    return hi, mid, low


def as_row(ref):
    return jnp.concatenate([ref[i : i + 1, :] for i in range(ref.shape[0])], axis=1)


def pack_kernel(
    cap, devices, owner_ref, local_ref, cost_ref, dispatch_ref, max_ref, avail_ref, out_ref, slot_ref, pay_ref, meta_ref
):
    step = pl.program_id(0)
    gens, hours = dispatch_ref.shape
    group = out_ref.shape[0]

    @pl.when(step == 0)
    def _():
        owner = owner_ref[...]
        hits = (lax.broadcasted_iota(jnp.int32, (devices, gens), 0) == owner).astype(F32)
        before = (
            lax.broadcasted_iota(jnp.int32, (gens, gens), 0) < lax.broadcasted_iota(jnp.int32, (gens, gens), 1)
        ).astype(F32)
        count = dot(hits.astype(BF16), before.astype(BF16))
        rank = jnp.sum(count * hits, axis=0, keepdims=True).astype(jnp.int32)
        slot_ref[...] = owner * cap + rank
        pay_ref[:, :hours] = dispatch_ref[...].astype(BF16)
        lanes = max_ref.shape[1]
        eye = (
            lax.broadcasted_iota(jnp.int32, (lanes, lanes), 0) == lax.broadcasted_iota(jnp.int32, (lanes, lanes), 1)
        ).astype(F32)
        for i in range(gens // lanes):
            rows = slice(i * lanes, (i + 1) * lanes)
            most = jnp.sum(eye * max_ref[i : i + 1, :], axis=1, keepdims=True)
            pay_ref[rows, hours:] = (most * avail_ref[rows, :]).astype(BF16)
        local = as_row(local_ref)
        hi, mid, low = thirds(as_row(cost_ref))
        row = lax.broadcasted_iota(jnp.int32, (META, gens), 0)
        parts = [
            (lax.shift_right_logical(local, 7) + 1).astype(F32),
            (local & 127).astype(F32),
            hi.astype(F32),
            mid.astype(F32),
            low.astype(F32),
        ]
        meta = jnp.zeros((META, gens), F32)
        for i, part in enumerate(parts):
            meta = jnp.where(row == i, part, meta)
        meta_ref[...] = meta.astype(BF16)

    slot = slot_ref[...] - step * (group * cap)
    place = lax.broadcasted_iota(jnp.int32, (cap, gens), 0)
    picks = [(place == slot - i * cap).astype(F32).astype(BF16) for i in range(group)]
    moved = dot(jnp.concatenate(picks, axis=0), pay_ref[...]).astype(BF16)
    for i in range(group):
        out_ref[i, :cap, :] = moved[i * cap : (i + 1) * cap]
        out_ref[i, cap:, :] = jnp.zeros((META, 2 * hours), BF16)
        out_ref[i, cap:, :cap] = dot(meta_ref[...], picks[i], NT).astype(BF16)


def pack(devices, cap, owner, local_bus, cost, dispatch, gen_max, availability):
    gens, hours = dispatch.shape
    full = lambda *shape: pl.BlockSpec(shape, lambda i: (0,) * len(shape))
    folded = (gens // 128, 128)
    return pl.pallas_call(
        functools.partial(pack_kernel, cap, devices),
        grid=(devices // GROUP,),
        out_shape=(
            jax.ShapeDtypeStruct((devices, cap + META, 2 * hours), BF16),
            jax.ShapeDtypeStruct((1, gens), jnp.int32),
        ),
        in_specs=[
            full(1, gens),
            full(*folded),
            full(*folded),
            full(gens, hours),
            full(*folded),
            full(gens, hours),
        ],
        out_specs=(pl.BlockSpec((GROUP, cap + META, 2 * hours), lambda i: (i, 0, 0)), full(1, gens)),
        scratch_shapes=[
            pltpu.VMEM((gens, 2 * hours), BF16),
            pltpu.VMEM((META, gens), BF16),
        ],
        compiler_params=pltpu.CompilerParams(vmem_limit_bytes=LIMIT),
        cost_estimate=pl.CostEstimate(flops=4 * devices * cap * gens * hours, bytes_accessed=3 << 20, transcendentals=0),
        name="pack_generators",
    )(
        owner.reshape(1, gens),
        local_bus.reshape(folded),
        cost.reshape(folded),
        dispatch,
        gen_max.reshape(folded),
        availability,
    )


def unpack_kernel(block, slot_ref, back_ref, dispatch_ref, max_ref, avail_ref, out_ref):
    gens = slot_ref.shape[1]
    slot = jnp.broadcast_to(slot_ref[...].astype(F32), (128, gens)).T[:, 0:1].astype(jnp.int32)
    at = lax.broadcasted_iota(jnp.int32, (gens, block), 1)
    change = None
    for start in range(0, back_ref.shape[0], block):
        pick = (at == slot - start).astype(F32).astype(BF16)
        part = dot(pick, back_ref[start : start + block, :])
        change = part if change is None else change + part
    dispatch = dispatch_ref[...]
    upper = max_ref[...] * avail_ref[...]
    sent = dispatch.astype(BF16).astype(F32)
    to_upper = (upper.astype(BF16).astype(F32) - sent).astype(BF16).astype(F32)
    moved = jnp.minimum(jnp.maximum(dispatch + change, 0.0), upper)
    moved = jnp.where(change == to_upper, upper, moved)
    out_ref[...] = jnp.where(change == -sent, 0.0, moved)


def unpack(slot, back, dispatch, gen_max, availability):
    gens = slot.shape[1]
    devices, cap, hours = back.shape
    slots = devices * cap
    block = next(size for size in (768, 256, 128, 16) if slots % size == 0)
    return pl.pallas_call(
        functools.partial(unpack_kernel, block),
        out_shape=jax.ShapeDtypeStruct((gens, hours), F32),
        compiler_params=pltpu.CompilerParams(vmem_limit_bytes=LIMIT),
        cost_estimate=pl.CostEstimate(flops=2 * slots * gens * hours, bytes_accessed=1 << 20, transcendentals=0),
        name="unpack_dispatch",
    )(slot, back.reshape(slots, hours), dispatch, gen_max, availability)


def update_kernel(cap, first, last, parts, *refs):
    price_refs = refs[:parts]
    balance_ref, demand_ref, recv_ref, prev_ref, upd_ref, inj_ref, shadow_ref, acc_ref, extra_ref = refs[parts:]
    step = pl.program_id(0)
    buses, hours = demand_ref.shape

    @pl.when(step == 0)
    def _():
        shadow = price_refs[0][...].astype(F32)
        for ref in price_refs[1:]:
            shadow = shadow + ref[...].astype(F32)
        hi, lo = halves(shadow)
        shadow_ref[:hours, :] = hi
        shadow_ref[hours:, :] = lo
        acc_ref[...] = jnp.zeros(acc_ref.shape, F32)
        extra_ref[...] = jnp.zeros(extra_ref.shape, BF16)

    group = recv_ref.shape[0]
    pad = extra_ref.shape[0] // group
    wide = 2 * hours
    meta = recv_ref[:, cap:, :].reshape(group * META, wide)
    eye = (
        lax.broadcasted_iota(jnp.int32, (cap, wide), 0) == lax.broadcasted_iota(jnp.int32, (cap, wide), 1)
    ).astype(F32)
    columns = dot(eye.astype(BF16), meta, NT)
    buses_at = lax.broadcasted_iota(jnp.int32, (cap, buses), 1)
    picks = []
    for i in range(group):
        at = i * META
        bus_column = ((columns[:, at : at + 1] - 1.0) * 128.0 + columns[:, at + 1 : at + 2]).astype(jnp.int32)
        picks.append((buses_at == bus_column).astype(F32).astype(BF16))
    both = dot(jnp.concatenate(picks, axis=0), shadow_ref[...], NT)
    for i in range(group):
        at = i * META
        cost = (columns[:, at + 2 : at + 3] + columns[:, at + 3 : at + 4]) + columns[:, at + 4 : at + 5]
        rows = slice(i * cap, (i + 1) * cap)
        price = both[rows, :hours] + both[rows, hours:] + balance_ref[...]
        sent = recv_ref[i, :cap, :hours].astype(F32)
        dispatch = sent if first else prev_ref[i]
        upper = recv_ref[i, :cap, hours:].astype(F32)
        updated = jnp.minimum(jnp.maximum(dispatch - tau_step * (cost + price), 0.0), upper)
        if last:
            upd_ref[i] = (updated - sent).astype(BF16)
        else:
            upd_ref[i] = updated
        hi, lo = halves(2.0 * updated - dispatch)
        extra_ref[i * pad : i * pad + cap, :hours] = hi
        extra_ref[i * pad : i * pad + cap, hours:] = lo
    at_row = lax.broadcasted_iota(jnp.int32, (buses, pad), 0)
    picks = []
    for i in range(group):
        row = recv_ref[i, cap:, :pad].astype(F32)
        bus_row = ((row[0:1] - 1.0) * 128.0 + row[1:2]).astype(jnp.int32)
        picks.append((at_row == bus_row).astype(F32).astype(BF16))
    acc_ref[...] += dot(jnp.concatenate(picks, axis=1), extra_ref[...])

    @pl.when(step == pl.num_programs(0) - 1)
    def _():
        injection = acc_ref[:, :hours] + acc_ref[:, hours:] - demand_ref[...]
        inj_ref[:buses, :] = injection.astype(BF16)
        hi, mid, low = thirds(jnp.sum(injection, axis=0, keepdims=True))
        row = lax.broadcasted_iota(jnp.int32, (META, hours), 0)
        tail = jnp.where(row == 0, hi.astype(F32), 0.0)
        tail = jnp.where(row == 1, mid.astype(F32), tail)
        tail = jnp.where(row == 2, low.astype(F32), tail)
        inj_ref[buses:, :] = tail.astype(BF16)


def update(cap, first, last, prices, balance_price, demand, recv, previous):
    devices = recv.shape[0]
    buses, hours = demand.shape
    full = lambda *shape: pl.BlockSpec(shape, lambda i: (0,) * len(shape))
    slots = lambda width: pl.BlockSpec((GROUP, cap, width), lambda i: (i, 0, 0))
    if first:
        previous, prev_spec = balance_price, full(1, hours)
    else:
        prev_spec = slots(hours)
    return pl.pallas_call(
        functools.partial(update_kernel, cap, first, last, len(prices)),
        grid=(devices // GROUP,),
        out_shape=(
            jax.ShapeDtypeStruct((devices, cap, hours), BF16 if last else F32),
            jax.ShapeDtypeStruct((buses + META, hours), BF16),
        ),
        in_specs=[full(hours, buses)] * len(prices)
        + [
            full(1, hours),
            full(buses, hours),
            pl.BlockSpec((GROUP, cap + META, 2 * hours), lambda i: (i, 0, 0)),
            prev_spec,
        ],
        out_specs=(slots(hours), full(buses + META, hours)),
        scratch_shapes=[
            pltpu.VMEM((2 * hours, buses), BF16),
            pltpu.VMEM((buses, 2 * hours), F32),
            pltpu.VMEM((GROUP * (-(-cap // 128) * 128), 2 * hours), BF16),
        ],
        compiler_params=pltpu.CompilerParams(vmem_limit_bytes=LIMIT),
        cost_estimate=pl.CostEstimate(flops=8 * devices * cap * buses * hours, bytes_accessed=4 << 20, transcendentals=0),
        name="update_generators",
    )(*prices, balance_price, demand, recv, previous)


def shadow_kernel(chunk, fetch, turn, place_ref, line_ref, ptdf_ref, keep_ref, send_ref, *rest):
    buses = keep_ref.shape[2]
    columns = [slice(rel * buses, (rel + 1) * buses) for rel in range(4)]
    if turn:
        *rest, line_t_ref, sems = rest
        rest = [*rest, sems]
    if fetch:
        held_ref, sems = rest
        copies = []
        for rel in range(4):
            start = pl.multiple_of((place_ref[0] ^ (4 * chunk + rel)) * buses, 128)
            copies.append(
                pltpu.make_async_copy(
                    ptdf_ref.at[:, pl.ds(start, buses)], held_ref.at[:, pl.ds(rel * buses, buses)], sems.at[rel]
                )
            )
        for rel in (3, 2, 1, 0):
            copies[rel].start()
    else:
        held_ref = ptdf_ref
    if turn:
        line_t_ref[...] = line_ref[...].T.astype(BF16)
        line_ref = line_t_ref

    def part(rel):
        if fetch:
            copies[rel].wait()
        return dot(line_ref[...], held_ref[:, columns[rel]])

    send_ref[1] = part(3).astype(BF16)
    keep_ref[1] = part(2)
    send_ref[0] = part(1).astype(BF16)
    keep_ref[0] = part(0)


def shadow_chunk(chunk, fetch, place, line, ptdf, buses):
    turn = line.dtype == F32
    lines, hours = line.shape if turn else line.shape[::-1]
    vmem = pl.BlockSpec(memory_space=pltpu.VMEM)
    out_shape = [
        jax.ShapeDtypeStruct((2, hours, buses), F32),
        jax.ShapeDtypeStruct((2, hours, buses), BF16),
    ]
    if fetch:
        out_shape.append(pltpu.VMEM((lines, 4 * buses), BF16))
    if turn:
        out_shape.append(jax.ShapeDtypeStruct((hours, lines), BF16))
    return pl.pallas_call(
        functools.partial(shadow_kernel, chunk, fetch, turn),
        in_specs=[pl.BlockSpec(memory_space=pltpu.SMEM), vmem, pl.BlockSpec(memory_space=pltpu.MemorySpace.HBM) if fetch else vmem],
        out_specs=tuple([vmem] * len(out_shape)),
        out_shape=tuple(out_shape),
        scratch_shapes=[pltpu.SemaphoreType.DMA((4,))] if fetch else [],
        compiler_params=pltpu.CompilerParams(vmem_limit_bytes=LIMIT),
        cost_estimate=pl.CostEstimate(
            flops=COST * 8 * hours * lines * buses, bytes_accessed=8 * lines * buses, transcendentals=0
        ),
        name="shadow_chunk",
    )(place, line, pltpu.with_memory_space_constraint(ptdf, pltpu.MemorySpace.HBM) if fetch else ptdf)


def flow_kernel(start, end, ptdf_ref, b0, b1, b2, b3, acc_ref, sum_ref, *rest):
    if end:
        limit_ref, line_ref, out_ref, half_ref, sum_out, inj_ref = rest
    else:
        out_ref, sum_out, inj_ref = rest
    buses = inj_ref.shape[0] // 4
    total = jnp.zeros(sum_ref.shape, F32) if start else sum_ref[...]
    for rel, ref in enumerate((b0, b1, b2, b3)):
        inj_ref[rel * buses : (rel + 1) * buses, :] = ref[:buses, :]
        tail = ref[buses:, :].astype(F32)
        total = total + jnp.sum(tail, axis=0, keepdims=True)
    sum_out[...] = total
    tile = ptdf_ref.shape[0] // 4

    def body(i, carry):
        rows = pl.ds(pl.multiple_of(i * tile, tile), tile)
        flow = dot(ptdf_ref[rows, :], inj_ref[...])
        if not start:
            flow = flow + acc_ref[rows, :]
        if end:
            shifted = line_ref[rows, :] + sigma_step * flow
            limit = limit_ref[rows, :]
            line = shifted - sigma_step * jnp.minimum(jnp.maximum(shifted / sigma_step, -limit), limit)
            out_ref[rows, :] = line
        else:
            out_ref[rows, :] = flow
        return carry

    lax.fori_loop(0, 4, body, 0)
    if end:
        half_ref[...] = out_ref[...].T.astype(BF16)


def flow_chunk(ptdf, blocks, acc, total, limit=None, line=None):
    lines = ptdf.shape[0]
    rows, hours = blocks[0].shape
    buses = rows - META
    start, end = acc is None, limit is not None
    operands = [ptdf, *blocks, total if start else acc, total]
    out_shape = [jax.ShapeDtypeStruct((lines, hours), F32)]
    if end:
        operands += [limit, line]
        out_shape += [jax.ShapeDtypeStruct((hours, lines), BF16)]
    out_shape += [jax.ShapeDtypeStruct((1, hours), F32)]
    in_specs = [pl.BlockSpec(memory_space=pltpu.VMEM)] * len(operands)
    return pl.pallas_call(
        functools.partial(flow_kernel, start, end),
        in_specs=in_specs,
        out_shape=tuple(out_shape),
        scratch_shapes=[pltpu.VMEM((4 * buses, hours), BF16)],
        compiler_params=pltpu.CompilerParams(vmem_limit_bytes=LIMIT),
        cost_estimate=pl.CostEstimate(
            flops=COST * 8 * hours * lines * buses, bytes_accessed=8 * lines * buses, transcendentals=0
        ),
        name="flow_chunk",
    )(*operands)


def swap(x, devices, mask):
    return lax.ppermute(x, "bus", [(i, i ^ mask) for i in range(devices)])


def local(
    ptdf,
    line_limit,
    gen_cost,
    gen_max,
    gen_owner,
    gen_local,
    availability,
    demand,
    dispatch,
    balance_price,
    line_price,
):
    devices = lax.axis_size("bus")
    place = lax.axis_index("bus").astype(jnp.int32).reshape(1)
    buses = demand.shape[0]
    all_buses = buses * devices
    gens, hours = dispatch.shape
    cap = -(-max(2, 3 * gens // devices) // 16) * 16
    staged = devices == 16 and buses % 128 == 0

    outgoing, slot = pack(
        devices,
        cap,
        gen_owner,
        gen_local,
        gen_cost,
        dispatch,
        gen_max,
        availability,
    )
    limit = line_limit.reshape(-1, 1)
    balance_row = balance_price.reshape(1, hours)
    line_half = line_price if staged else line_price.astype(BF16)
    recv = lax.all_to_all(outgoing, "bus", split_axis=0, concat_axis=0, tiled=True)
    held, resident = None, {}
    for iteration in range(ITERS):
        last = iteration == ITERS - 1
        if staged:
            line_t = line_half
            keeps, gots, crossed, parts = {}, {}, {}, {}

            def across(chunk):
                both = (keeps[chunk][1] + gots[chunk][1].astype(F32)).astype(BF16)
                crossed[chunk] = swap(both, devices, 2)
                return both

            def settle(chunk):
                part = keeps[chunk][0] + gots[chunk][0].astype(F32) + crossed[chunk].astype(F32)
                if chunk == 2:
                    part = part + parts[3].astype(F32)
                if chunk:
                    part = part.astype(BF16)
                    parts[chunk] = swap(part, devices, 8 if chunk == 2 else 4)
                else:
                    parts[chunk] = part
                return part

            def product(chunk, line_t):
                if chunk in resident:
                    keeps[chunk], send = shadow_chunk(chunk, False, place, line_t, resident[chunk], buses)
                else:
                    keeps[chunk], send, resident[chunk], *turned = shadow_chunk(
                        chunk, True, place, line_t, ptdf, buses
                    )
                    line_t = turned[0] if turned else line_t
                gots[chunk] = swap(send, devices, 1)
                return line_t

            line_t = product(3, line_t)
            if iteration == 0:
                line_t, _ = lax.optimization_barrier((line_t, outgoing))
            product(2, line_t)
            line_t, _ = lax.optimization_barrier((line_t, across(3)))
            product(1, line_t)
            line_t, _, _ = lax.optimization_barrier((line_t, across(2), settle(3)))
            product(0, line_t)
            across(1)
            settle(2)
            across(0)
            settle(1)
            settle(0)
            prices = [parts[0], parts[1], parts[2]]
        else:
            shadow = lax.dot_general(ptdf, line_half, (((0,), (0,)), ((), ())), preferred_element_type=F32)
            prices = [lax.psum_scatter(shadow, "bus", scatter_dimension=0, tiled=True).T]
        held, block = update(cap, iteration == 0, last, prices, balance_row, demand, recv, held)
        if staged:
            near, far, cross, far_cross = {0: block}, {}, {}, {}

            def spread(chunk):
                far[chunk] = swap(near[chunk], devices, 2)
                cross[chunk] = swap(near[chunk], devices, 1)

            def settle_far(chunk):
                far_cross[chunk] = swap(far[chunk], devices, 1)

            def blocks(chunk):
                return [near[chunk], cross[chunk], far[chunk], far_cross[chunk]]

            near[2] = swap(block, devices, 8)
            near[1] = swap(block, devices, 4)
            spread(0)
            near[3] = swap(near[2], devices, 4)
            spread(1)
            spread(2)
            settle_far(0)
            near[1], near[2], row = lax.optimization_barrier((near[1], near[2], balance_row))
            acc, total = flow_chunk(resident[0], blocks(0), None, row)
            near[3], acc = lax.optimization_barrier((near[3], acc))
            spread(3)
            if last:
                held, _ = lax.optimization_barrier((held, near[3]))
                back = lax.all_to_all(held, "bus", split_axis=0, concat_axis=0, tiled=True)
            settle_far(1)
            acc, total = flow_chunk(resident[1], blocks(1), acc, total)
            settle_far(2)
            far[3], acc = lax.optimization_barrier((far[3], acc))
            acc, total = flow_chunk(resident[2], blocks(2), acc, total)
            settle_far(3)
            line_price, line_half, total = flow_chunk(
                resident[3], blocks(3), acc, total, limit, line_price
            )
            balance = total
        else:
            if last:
                back = lax.all_to_all(held, "bus", split_axis=0, concat_axis=0, tiled=True)
            every = lax.all_gather(block, "bus", axis=0, tiled=False)
            balance = jnp.sum(every[:, buses:].astype(F32), axis=(0, 1)).reshape(1, hours)
            flow = jnp.dot(ptdf, every[:, :buses].reshape(all_buses, hours), preferred_element_type=F32)
            shifted = line_price + sigma_step * flow
            line_price = shifted - sigma_step * jnp.clip(shifted / sigma_step, -limit, limit)
            line_half = line_price.astype(BF16)
        balance_row = balance_row + sigma_step * balance / all_buses
    dispatch = unpack(slot, back, dispatch, gen_max.reshape(gens, 1), availability)
    return (dispatch, balance_row.reshape(hours), line_price)


def solution(mesh):
    return jax.shard_map(
        local,
        mesh=mesh,
        in_specs=(
            P("bus", None),
            P("bus"),
            P("bus"),
            P("bus"),
            P("bus", None),
            P("bus"),
            P(("cases", "bus"), None),
            P(("cases", "bus"), None),
            P(("cases", "bus"), None),
            P("cases"),
            P(("cases", "bus"), None),
        ),
        out_specs=(P(("cases", "bus"), None), P("cases"), P(("cases", "bus"), None)),
        check_vma=False,
    )
```

```python
import functools

import jax
import jax.numpy as jnp
from jax import lax
from jax.experimental import pallas as pl
from jax.experimental.pallas import tpu as pltpu
from jax.sharding import PartitionSpec as P

ITERS = 2

tau_step = 0.2
sigma_step = 0.15

GROUP = 4
LIMIT = 16 << 20
COST = 3
META = 16
F32 = jnp.float32
BF16 = jnp.bfloat16
NT = (((1,), (1,)), ((), ()))
NN = (((1,), (0,)), ((), ()))


def dot(a, b, dims=NN):
    return lax.dot_general(a, b, dims, preferred_element_type=F32)


def halves(x):
    hi = x.astype(BF16)
    lo = (x - hi.astype(F32)).astype(BF16)
    return hi, lo


def thirds(x):
    hi = x.astype(BF16)
    rest = x - hi.astype(F32)
    mid = rest.astype(BF16)
    low = (rest - mid.astype(F32)).astype(BF16)
    return hi, mid, low


def as_row(ref):
    return jnp.concatenate([ref[i : i + 1, :] for i in range(ref.shape[0])], axis=1)


def pack_kernel(
    cap, devices, owner_ref, local_ref, cost_ref, dispatch_ref, max_ref, avail_ref, out_ref, slot_ref, pay_ref, meta_ref
):
    step = pl.program_id(0)
    gens, hours = dispatch_ref.shape
    group = out_ref.shape[0]

    @pl.when(step == 0)
    def _():
        owner = owner_ref[...]
        hits = (lax.broadcasted_iota(jnp.int32, (devices, gens), 0) == owner).astype(F32)
        before = (
            lax.broadcasted_iota(jnp.int32, (gens, gens), 0) < lax.broadcasted_iota(jnp.int32, (gens, gens), 1)
        ).astype(F32)
        count = dot(hits.astype(BF16), before.astype(BF16))
        rank = jnp.sum(count * hits, axis=0, keepdims=True).astype(jnp.int32)
        slot_ref[...] = owner * cap + rank
        pay_ref[:, :hours] = dispatch_ref[...].astype(BF16)
        lanes = max_ref.shape[1]
        eye = (
            lax.broadcasted_iota(jnp.int32, (lanes, lanes), 0) == lax.broadcasted_iota(jnp.int32, (lanes, lanes), 1)
        ).astype(F32)
        for i in range(gens // lanes):
            rows = slice(i * lanes, (i + 1) * lanes)
            most = jnp.sum(eye * max_ref[i : i + 1, :], axis=1, keepdims=True)
            pay_ref[rows, hours:] = (most * avail_ref[rows, :]).astype(BF16)
        local = as_row(local_ref)
        hi, mid, low = thirds(as_row(cost_ref))
        row = lax.broadcasted_iota(jnp.int32, (META, gens), 0)
        parts = [
            (lax.shift_right_logical(local, 7) + 1).astype(F32),
            (local & 127).astype(F32),
            hi.astype(F32),
            mid.astype(F32),
            low.astype(F32),
        ]
        meta = jnp.zeros((META, gens), F32)
        for i, part in enumerate(parts):
            meta = jnp.where(row == i, part, meta)
        meta_ref[...] = meta.astype(BF16)

    slot = slot_ref[...] - step * (group * cap)
    place = lax.broadcasted_iota(jnp.int32, (cap, gens), 0)
    picks = [(place == slot - i * cap).astype(F32).astype(BF16) for i in range(group)]
    moved = dot(jnp.concatenate(picks, axis=0), pay_ref[...]).astype(BF16)
    for i in range(group):
        out_ref[i, :cap, :] = moved[i * cap : (i + 1) * cap]
        out_ref[i, cap:, :] = jnp.zeros((META, 2 * hours), BF16)
        out_ref[i, cap:, :cap] = dot(meta_ref[...], picks[i], NT).astype(BF16)


def pack(devices, cap, owner, local_bus, cost, dispatch, gen_max, availability):
    gens, hours = dispatch.shape
    full = lambda *shape: pl.BlockSpec(shape, lambda i: (0,) * len(shape))
    folded = (gens // 128, 128)
    return pl.pallas_call(
        functools.partial(pack_kernel, cap, devices),
        grid=(devices // GROUP,),
        out_shape=(
            jax.ShapeDtypeStruct((devices, cap + META, 2 * hours), BF16),
            jax.ShapeDtypeStruct((1, gens), jnp.int32),
        ),
        in_specs=[
            full(1, gens),
            full(*folded),
            full(*folded),
            full(gens, hours),
            full(*folded),
            full(gens, hours),
        ],
        out_specs=(pl.BlockSpec((GROUP, cap + META, 2 * hours), lambda i: (i, 0, 0)), full(1, gens)),
        scratch_shapes=[
            pltpu.VMEM((gens, 2 * hours), BF16),
            pltpu.VMEM((META, gens), BF16),
        ],
        compiler_params=pltpu.CompilerParams(vmem_limit_bytes=LIMIT),
        cost_estimate=pl.CostEstimate(flops=4 * devices * cap * gens * hours, bytes_accessed=3 << 20, transcendentals=0),
        name="pack_generators",
    )(
        owner.reshape(1, gens),
        local_bus.reshape(folded),
        cost.reshape(folded),
        dispatch,
        gen_max.reshape(folded),
        availability,
    )


def unpack_kernel(block, slot_ref, back_ref, dispatch_ref, max_ref, avail_ref, out_ref):
    gens = slot_ref.shape[1]
    slot = jnp.broadcast_to(slot_ref[...].astype(F32), (128, gens)).T[:, 0:1].astype(jnp.int32)
    at = lax.broadcasted_iota(jnp.int32, (gens, block), 1)
    change = None
    for start in range(0, back_ref.shape[0], block):
        pick = (at == slot - start).astype(F32).astype(BF16)
        part = dot(pick, back_ref[start : start + block, :])
        change = part if change is None else change + part
    dispatch = dispatch_ref[...]
    upper = max_ref[...] * avail_ref[...]
    sent = dispatch.astype(BF16).astype(F32)
    to_upper = (upper.astype(BF16).astype(F32) - sent).astype(BF16).astype(F32)
    moved = jnp.minimum(jnp.maximum(dispatch + change, 0.0), upper)
    moved = jnp.where(change == to_upper, upper, moved)
    out_ref[...] = jnp.where(change == -sent, 0.0, moved)


def unpack(slot, back, dispatch, gen_max, availability):
    gens = slot.shape[1]
    devices, cap, hours = back.shape
    slots = devices * cap
    block = next(size for size in (768, 256, 128, 16) if slots % size == 0)
    return pl.pallas_call(
        functools.partial(unpack_kernel, block),
        out_shape=jax.ShapeDtypeStruct((gens, hours), F32),
        compiler_params=pltpu.CompilerParams(vmem_limit_bytes=LIMIT),
        cost_estimate=pl.CostEstimate(flops=2 * slots * gens * hours, bytes_accessed=1 << 20, transcendentals=0),
        name="unpack_dispatch",
    )(slot, back.reshape(slots, hours), dispatch, gen_max, availability)


def update_kernel(cap, first, last, parts, *refs):
    price_refs = refs[:parts]
    balance_ref, demand_ref, recv_ref, prev_ref, upd_ref, inj_ref, shadow_ref, acc_ref, extra_ref = refs[parts:]
    step = pl.program_id(0)
    buses, hours = demand_ref.shape

    @pl.when(step == 0)
    def _():
        shadow = price_refs[0][...].astype(F32)
        for ref in price_refs[1:]:
            shadow = shadow + ref[...].astype(F32)
        hi, lo = halves(shadow)
        shadow_ref[:hours, :] = hi
        shadow_ref[hours:, :] = lo
        acc_ref[...] = jnp.zeros(acc_ref.shape, F32)
        extra_ref[...] = jnp.zeros(extra_ref.shape, BF16)

    group = recv_ref.shape[0]
    pad = extra_ref.shape[0] // group
    wide = 2 * hours
    meta = recv_ref[:, cap:, :].reshape(group * META, wide)
    eye = (
        lax.broadcasted_iota(jnp.int32, (cap, wide), 0) == lax.broadcasted_iota(jnp.int32, (cap, wide), 1)
    ).astype(F32)
    columns = dot(eye.astype(BF16), meta, NT)
    buses_at = lax.broadcasted_iota(jnp.int32, (cap, buses), 1)
    picks = []
    for i in range(group):
        at = i * META
        bus_column = ((columns[:, at : at + 1] - 1.0) * 128.0 + columns[:, at + 1 : at + 2]).astype(jnp.int32)
        picks.append((buses_at == bus_column).astype(F32).astype(BF16))
    both = dot(jnp.concatenate(picks, axis=0), shadow_ref[...], NT)
    for i in range(group):
        at = i * META
        cost = (columns[:, at + 2 : at + 3] + columns[:, at + 3 : at + 4]) + columns[:, at + 4 : at + 5]
        rows = slice(i * cap, (i + 1) * cap)
        price = both[rows, :hours] + both[rows, hours:] + balance_ref[...]
        sent = recv_ref[i, :cap, :hours].astype(F32)
        dispatch = sent if first else prev_ref[i]
        upper = recv_ref[i, :cap, hours:].astype(F32)
        updated = jnp.minimum(jnp.maximum(dispatch - tau_step * (cost + price), 0.0), upper)
        if last:
            upd_ref[i] = (updated - sent).astype(BF16)
        else:
            upd_ref[i] = updated
        hi, lo = halves(2.0 * updated - dispatch)
        extra_ref[i * pad : i * pad + cap, :hours] = hi
        extra_ref[i * pad : i * pad + cap, hours:] = lo
    at_row = lax.broadcasted_iota(jnp.int32, (buses, pad), 0)
    picks = []
    for i in range(group):
        row = recv_ref[i, cap:, :pad].astype(F32)
        bus_row = ((row[0:1] - 1.0) * 128.0 + row[1:2]).astype(jnp.int32)
        picks.append((at_row == bus_row).astype(F32).astype(BF16))
    acc_ref[...] += dot(jnp.concatenate(picks, axis=1), extra_ref[...])

    @pl.when(step == pl.num_programs(0) - 1)
    def _():
        injection = acc_ref[:, :hours] + acc_ref[:, hours:] - demand_ref[...]
        inj_ref[:buses, :] = injection.astype(BF16)
        hi, mid, low = thirds(jnp.sum(injection, axis=0, keepdims=True))
        row = lax.broadcasted_iota(jnp.int32, (META, hours), 0)
        tail = jnp.where(row == 0, hi.astype(F32), 0.0)
        tail = jnp.where(row == 1, mid.astype(F32), tail)
        tail = jnp.where(row == 2, low.astype(F32), tail)
        inj_ref[buses:, :] = tail.astype(BF16)


def update(cap, first, last, prices, balance_price, demand, recv, previous):
    devices = recv.shape[0]
    buses, hours = demand.shape
    full = lambda *shape: pl.BlockSpec(shape, lambda i: (0,) * len(shape))
    slots = lambda width: pl.BlockSpec((GROUP, cap, width), lambda i: (i, 0, 0))
    if first:
        previous, prev_spec = balance_price, full(1, hours)
    else:
        prev_spec = slots(hours)
    return pl.pallas_call(
        functools.partial(update_kernel, cap, first, last, len(prices)),
        grid=(devices // GROUP,),
        out_shape=(
            jax.ShapeDtypeStruct((devices, cap, hours), BF16 if last else F32),
            jax.ShapeDtypeStruct((buses + META, hours), BF16),
        ),
        in_specs=[full(hours, buses)] * len(prices)
        + [
            full(1, hours),
            full(buses, hours),
            pl.BlockSpec((GROUP, cap + META, 2 * hours), lambda i: (i, 0, 0)),
            prev_spec,
        ],
        out_specs=(slots(hours), full(buses + META, hours)),
        scratch_shapes=[
            pltpu.VMEM((2 * hours, buses), BF16),
            pltpu.VMEM((buses, 2 * hours), F32),
            pltpu.VMEM((GROUP * (-(-cap // 128) * 128), 2 * hours), BF16),
        ],
        compiler_params=pltpu.CompilerParams(vmem_limit_bytes=LIMIT),
        cost_estimate=pl.CostEstimate(flops=8 * devices * cap * buses * hours, bytes_accessed=4 << 20, transcendentals=0),
        name="update_generators",
    )(*prices, balance_price, demand, recv, previous)


def shadow_kernel(chunk, stream, turn, place_ref, line_ref, ptdf_ref, keep_ref, send_ref, *rest):
    buses = keep_ref.shape[2]
    columns = [slice(rel * buses, (rel + 1) * buses) for rel in range(4)]
    if stream:
        if turn:
            line_t_ref, held_ref, sems, line_held_ref = rest
            line_copy = pltpu.make_async_copy(line_ref, line_held_ref, sems.at[4])
            line_copy.start()
        else:
            held_ref, sems = rest
        copies = []
        for rel in range(4):
            start = pl.multiple_of((place_ref[0] ^ (4 * chunk + rel)) * buses, 128)
            copies.append(
                pltpu.make_async_copy(
                    ptdf_ref.at[:, pl.ds(start, buses)], held_ref.at[:, columns[rel]], sems.at[rel]
                )
            )
        for rel in (3, 2, 1, 0):
            copies[rel].start()
        if turn:
            line_copy.wait()
            line_t_ref[...] = line_held_ref[...].T.astype(BF16)
            line_ref = line_t_ref
    else:
        held_ref = ptdf_ref

    def part(rel):
        if stream:
            copies[rel].wait()
        return dot(line_ref[...], held_ref[:, columns[rel]])

    send_ref[1] = part(3).astype(BF16)
    keep_ref[1] = part(2)
    send_ref[0] = part(1).astype(BF16)
    keep_ref[0] = part(0)


def in_hbm(x):
    return pltpu.with_memory_space_constraint(x, pltpu.MemorySpace.HBM)


HBM_SPEC = pl.BlockSpec(memory_space=pltpu.MemorySpace.HBM)
VMEM_SPEC = pl.BlockSpec(memory_space=pltpu.VMEM)
SMEM_SPEC = pl.BlockSpec(memory_space=pltpu.SMEM)


def chunk_cost(hours, lines, buses):
    return pl.CostEstimate(flops=COST * 8 * hours * lines * buses, bytes_accessed=8 * lines * buses, transcendentals=0)


def shadow_chunk(chunk, stream, place, line, ptdf, buses):
    turn = line.dtype == F32
    lines, hours = line.shape if turn else line.shape[::-1]
    out_shape = [
        jax.ShapeDtypeStruct((2, hours, buses), F32),
        jax.ShapeDtypeStruct((2, hours, buses), BF16),
    ]
    scratch = [pltpu.VMEM((lines, 4 * buses), BF16), pltpu.SemaphoreType.DMA((5,))] if stream else []
    if turn:
        out_shape.append(jax.ShapeDtypeStruct((hours, lines), BF16))
        scratch.append(pltpu.VMEM((lines, hours), F32))
    return pl.pallas_call(
        functools.partial(shadow_kernel, chunk, stream, turn),
        in_specs=[SMEM_SPEC, HBM_SPEC if turn else VMEM_SPEC, HBM_SPEC if stream else VMEM_SPEC],
        out_specs=tuple([VMEM_SPEC] * len(out_shape)),
        out_shape=tuple(out_shape),
        scratch_shapes=scratch,
        compiler_params=pltpu.CompilerParams(vmem_limit_bytes=LIMIT),
        cost_estimate=chunk_cost(hours, lines, buses),
        name="shadow_chunk",
    )(place, in_hbm(line) if turn else line, in_hbm(ptdf) if stream else ptdf)


TILES = 4


def flow_kernel(chunk, start, end, keep, place_ref, ptdf_ref, b0, b1, b2, b3, acc_ref, sum_ref, *rest):
    if end:
        limit_ref, line_ref, out_ref, half_ref, sum_out, *rest = rest
    else:
        out_ref, sum_out, *rest = rest
    held_ref, inj_ref, sems = rest
    buses = inj_ref.shape[0] // 4
    tile = held_ref.shape[0] // TILES
    copies = []
    for i in range(TILES):
        rows = pl.ds(i * tile, tile)
        for rel in range(4):
            first = pl.multiple_of((place_ref[0] ^ (4 * chunk + rel)) * buses, 128)
            copies.append(
                pltpu.make_async_copy(
                    ptdf_ref.at[rows, pl.ds(first, buses)],
                    held_ref.at[rows, pl.ds(rel * buses, buses)],
                    sems.at[i, rel],
                )
            )
            copies[-1].start()
    total = jnp.zeros(sum_ref.shape, F32) if start else sum_ref[...]
    for rel, ref in enumerate((b0, b1, b2, b3)):
        inj_ref[rel * buses : (rel + 1) * buses, :] = ref[:buses, :]
        tail = ref[buses:, :].astype(F32)
        total = total + jnp.sum(tail, axis=0, keepdims=True)
    sum_out[...] = total
    for i in range(TILES):
        rows = slice(i * tile, (i + 1) * tile)
        for copy in copies[4 * i : 4 * i + 4]:
            copy.wait()
        flow = dot(held_ref[rows, :], inj_ref[...])
        if not start:
            flow = flow + acc_ref[rows, :]
        if end:
            shifted = line_ref[rows, :] + sigma_step * flow
            limit = limit_ref[rows, :]
            line = shifted - sigma_step * jnp.minimum(jnp.maximum(shifted / sigma_step, -limit), limit)
            out_ref[rows, :] = line
        else:
            out_ref[rows, :] = flow
    if end:
        half_ref[...] = out_ref[...].T.astype(BF16)


def flow_chunk(chunk, keep, place, ptdf, blocks, acc, total, limit=None, line=None):
    lines = ptdf.shape[0]
    rows, hours = blocks[0].shape
    buses = rows - META
    start, end = acc is None, limit is not None
    operands = [*blocks, total if start else acc, total]
    out_shape = [jax.ShapeDtypeStruct((lines, hours), F32)]
    if end:
        operands += [limit, line]
        out_shape += [jax.ShapeDtypeStruct((hours, lines), BF16)]
    out_shape += [jax.ShapeDtypeStruct((1, hours), F32)]
    held = pltpu.VMEM((lines, 4 * buses), BF16)
    if keep:
        out_shape.append(held)
    return pl.pallas_call(
        functools.partial(flow_kernel, chunk, start, end, keep),
        in_specs=[SMEM_SPEC, HBM_SPEC] + [VMEM_SPEC] * len(operands),
        out_specs=tuple([VMEM_SPEC] * len(out_shape)),
        out_shape=tuple(out_shape),
        scratch_shapes=([] if keep else [held])
        + [pltpu.VMEM((4 * buses, hours), BF16), pltpu.SemaphoreType.DMA((TILES, 4))],
        compiler_params=pltpu.CompilerParams(vmem_limit_bytes=LIMIT),
        cost_estimate=chunk_cost(hours, lines, buses),
        name="flow_chunk",
    )(place, in_hbm(ptdf), *operands)


def swap(x, devices, mask):
    return lax.ppermute(x, "bus", [(i, i ^ mask) for i in range(devices)])


def local(
    ptdf,
    line_limit,
    gen_cost,
    gen_max,
    gen_owner,
    gen_local,
    availability,
    demand,
    dispatch,
    balance_price,
    line_price,
):
    devices = lax.axis_size("bus")
    place = lax.axis_index("bus").astype(jnp.int32).reshape(1)
    buses = demand.shape[0]
    all_buses = buses * devices
    gens, hours = dispatch.shape
    cap = -(-max(2, 3 * gens // devices) // 16) * 16
    staged = devices == 16 and buses % 128 == 0

    outgoing, slot = pack(
        devices,
        cap,
        gen_owner,
        gen_local,
        gen_cost,
        dispatch,
        gen_max,
        availability,
    )
    limit = line_limit.reshape(-1, 1)
    balance_row = balance_price.reshape(1, hours)
    line_half = line_price if staged else line_price.astype(BF16)
    recv = lax.all_to_all(outgoing, "bus", split_axis=0, concat_axis=0, tiled=True)
    held, resident = None, {}
    for iteration in range(ITERS):
        last = iteration == ITERS - 1
        if staged:
            line_t = line_half
            keeps, gots, crossed, parts = {}, {}, {}, {}

            def across(chunk):
                both = (keeps[chunk][1] + gots[chunk][1].astype(F32)).astype(BF16)
                crossed[chunk] = swap(both, devices, 2)
                return both

            def settle(chunk):
                part = keeps[chunk][0] + gots[chunk][0].astype(F32) + crossed[chunk].astype(F32)
                if chunk == 2:
                    part = part + parts[3].astype(F32)
                if chunk:
                    part = part.astype(BF16)
                    parts[chunk] = swap(part, devices, 8 if chunk == 2 else 4)
                else:
                    parts[chunk] = part
                return part

            def product(chunk, line_t):
                columns = resident.get(chunk, ptdf)
                keeps[chunk], send, *turned = shadow_chunk(
                    chunk, chunk not in resident, place, line_t, columns, buses
                )
                gots[chunk] = swap(send, devices, 1)
                return turned[0] if turned else line_t

            line_t = product(3, line_t)
            if iteration == 0:
                line_t, _ = lax.optimization_barrier((line_t, outgoing))
            product(2, line_t)
            line_t, _ = lax.optimization_barrier((line_t, across(3)))
            product(1, line_t)
            line_t, _, _ = lax.optimization_barrier((line_t, across(2), settle(3)))
            product(0, line_t)
            gots[1], crossed[2] = lax.optimization_barrier((gots[1], crossed[2]))
            parts[3], _, _ = lax.optimization_barrier((parts[3], across(1), across(0)))
            crossed[1], _ = lax.optimization_barrier((crossed[1], settle(2)))
            settle(1)
            settle(0)
            prices = [parts[0], parts[1], parts[2]]
        else:
            shadow = lax.dot_general(ptdf, line_half, (((0,), (0,)), ((), ())), preferred_element_type=F32)
            prices = [lax.psum_scatter(shadow, "bus", scatter_dimension=0, tiled=True).T]
        held, block = update(cap, iteration == 0, last, prices, balance_row, demand, recv, held)
        if staged:
            near, far, cross, far_cross = {0: block}, {}, {}, {}

            def spread(chunk):
                far[chunk] = swap(near[chunk], devices, 2)
                cross[chunk] = swap(near[chunk], devices, 1)

            def settle_far(chunk):
                far_cross[chunk] = swap(far[chunk], devices, 1)

            def blocks(chunk):
                return [near[chunk], cross[chunk], far[chunk], far_cross[chunk]]

            def flow(chunk, acc, total, *rest):
                acc, *given = flow_chunk(chunk, not last, place, ptdf, blocks(chunk), acc, total, *rest)
                if not last:
                    *given, resident[chunk] = given
                return (acc, *given)

            near[2] = swap(block, devices, 8)
            near[1] = swap(block, devices, 4)
            spread(0)
            near[1], near[2], far[0], cross[0], row = lax.optimization_barrier(
                (near[1], near[2], far[0], cross[0], balance_row)
            )
            near[3] = swap(near[2], devices, 4)
            spread(1)
            spread(2)
            settle_far(0)
            acc, total = flow(0, None, row)
            near[3], acc = lax.optimization_barrier((near[3], acc))
            spread(3)
            settle_far(1)
            acc, total = flow(1, acc, total)
            settle_far(2)
            far[3], acc = lax.optimization_barrier((far[3], acc))
            if last:
                held, _ = lax.optimization_barrier((held, far[2]))
                back = lax.all_to_all(held, "bus", split_axis=0, concat_axis=0, tiled=True)
            acc, total = flow(2, acc, total)
            settle_far(3)
            line_price, line_half, total = flow(3, acc, total, limit, line_price)
            balance = total
        else:
            if last:
                back = lax.all_to_all(held, "bus", split_axis=0, concat_axis=0, tiled=True)
            every = lax.all_gather(block, "bus", axis=0, tiled=False)
            balance = jnp.sum(every[:, buses:].astype(F32), axis=(0, 1)).reshape(1, hours)
            flow = jnp.dot(ptdf, every[:, :buses].reshape(all_buses, hours), preferred_element_type=F32)
            shifted = line_price + sigma_step * flow
            line_price = shifted - sigma_step * jnp.clip(shifted / sigma_step, -limit, limit)
            line_half = line_price.astype(BF16)
        balance_row = balance_row + sigma_step * balance / all_buses
    dispatch = unpack(slot, back, dispatch, gen_max.reshape(gens, 1), availability)
    return (dispatch, balance_row.reshape(hours), line_price)


def solution(mesh):
    return jax.shard_map(
        local,
        mesh=mesh,
        in_specs=(
            P("bus", None),
            P("bus"),
            P("bus"),
            P("bus"),
            P("bus", None),
            P("bus"),
            P(("cases", "bus"), None),
            P(("cases", "bus"), None),
            P(("cases", "bus"), None),
            P("cases"),
            P(("cases", "bus"), None),
        ),
        out_specs=(P(("cases", "bus"), None), P("cases"), P(("cases", "bus"), None)),
        check_vma=False,
    )
```

```python
import functools

import jax
import jax.numpy as jnp
from jax import lax
from jax.experimental import pallas as pl
from jax.experimental.pallas import tpu as pltpu
from jax.sharding import PartitionSpec as P

ITERS = 2

tau_step = 0.2
sigma_step = 0.15

GROUP = 4
LIMIT = 16 << 20
COST = 3
META = 16
HBM_SPEC = pl.BlockSpec(memory_space=pltpu.MemorySpace.HBM)
VMEM_SPEC = pl.BlockSpec(memory_space=pltpu.VMEM)
SMEM_SPEC = pl.BlockSpec(memory_space=pltpu.SMEM)
F32 = jnp.float32
BF16 = jnp.bfloat16
NT = (((1,), (1,)), ((), ()))
NN = (((1,), (0,)), ((), ()))


def dot(a, b, dims=NN):
    return lax.dot_general(a, b, dims, preferred_element_type=F32)


def halves(x):
    hi = x.astype(BF16)
    lo = (x - hi.astype(F32)).astype(BF16)
    return hi, lo


def thirds(x):
    hi = x.astype(BF16)
    rest = x - hi.astype(F32)
    mid = rest.astype(BF16)
    low = (rest - mid.astype(F32)).astype(BF16)
    return hi, mid, low


def as_row(ref):
    return jnp.concatenate([ref[i : i + 1, :] for i in range(ref.shape[0])], axis=1)


def pack_kernel(
    cap, devices, place_ref, owner_ref, local_ref, cost_ref, dispatch_ref, max_ref, avail_ref,
    out_ref, near_ref, slot_ref, pay_ref, meta_ref,
):
    step = pl.program_id(0)
    gens, hours = dispatch_ref.shape
    group = out_ref.shape[0]

    @pl.when(step == 0)
    def _():
        owner = owner_ref[...]
        hits = (lax.broadcasted_iota(jnp.int32, (devices, gens), 0) == owner).astype(F32)
        before = (
            lax.broadcasted_iota(jnp.int32, (gens, gens), 0) < lax.broadcasted_iota(jnp.int32, (gens, gens), 1)
        ).astype(F32)
        count = dot(hits.astype(BF16), before.astype(BF16))
        rank = jnp.sum(count * hits, axis=0, keepdims=True).astype(jnp.int32)
        slot_ref[...] = owner * cap + rank
        near_ref[...] = (owner ^ place_ref[0]) * cap + rank
        pay_ref[:, :hours] = dispatch_ref[...].astype(BF16)
        lanes = max_ref.shape[1]
        eye = (
            lax.broadcasted_iota(jnp.int32, (lanes, lanes), 0) == lax.broadcasted_iota(jnp.int32, (lanes, lanes), 1)
        ).astype(F32)
        for i in range(gens // lanes):
            rows = slice(i * lanes, (i + 1) * lanes)
            most = jnp.sum(eye * max_ref[i : i + 1, :], axis=1, keepdims=True)
            pay_ref[rows, hours:] = (most * avail_ref[rows, :]).astype(BF16)
        local = as_row(local_ref)
        hi, mid, low = thirds(as_row(cost_ref))
        row = lax.broadcasted_iota(jnp.int32, (META, gens), 0)
        parts = [
            (lax.shift_right_logical(local, 7) + 1).astype(F32),
            (local & 127).astype(F32),
            hi.astype(F32),
            mid.astype(F32),
            low.astype(F32),
        ]
        meta = jnp.zeros((META, gens), F32)
        for i, part in enumerate(parts):
            meta = jnp.where(row == i, part, meta)
        meta_ref[...] = meta.astype(BF16)

    slot = slot_ref[...] - step * (group * cap)
    place = lax.broadcasted_iota(jnp.int32, (cap, gens), 0)
    picks = [(place == slot - i * cap).astype(F32).astype(BF16) for i in range(group)]
    moved = dot(jnp.concatenate(picks, axis=0), pay_ref[...]).astype(BF16)
    for i in range(group):
        out_ref[i, :cap, :] = moved[i * cap : (i + 1) * cap]
        out_ref[i, cap:, :] = jnp.zeros((META, 2 * hours), BF16)
        out_ref[i, cap:, :cap] = dot(meta_ref[...], picks[i], NT).astype(BF16)


def pack(devices, cap, place, owner, local_bus, cost, dispatch, gen_max, availability):
    gens, hours = dispatch.shape
    full = lambda *shape: pl.BlockSpec(shape, lambda i: (0,) * len(shape))
    folded = (gens // 128, 128)
    return pl.pallas_call(
        functools.partial(pack_kernel, cap, devices),
        grid=(devices // GROUP,),
        out_shape=(
            jax.ShapeDtypeStruct((devices, cap + META, 2 * hours), BF16),
            jax.ShapeDtypeStruct((1, gens), jnp.int32),
        ),
        in_specs=[
            SMEM_SPEC,
            full(1, gens),
            full(*folded),
            full(*folded),
            full(gens, hours),
            full(*folded),
            full(gens, hours),
        ],
        out_specs=(pl.BlockSpec((GROUP, cap + META, 2 * hours), lambda i: (i, 0, 0)), full(1, gens)),
        scratch_shapes=[
            pltpu.VMEM((1, gens), jnp.int32),
            pltpu.VMEM((gens, 2 * hours), BF16),
            pltpu.VMEM((META, gens), BF16),
        ],
        compiler_params=pltpu.CompilerParams(vmem_limit_bytes=LIMIT),
        cost_estimate=pl.CostEstimate(flops=4 * devices * cap * gens * hours, bytes_accessed=3 << 20, transcendentals=0),
        name="pack_generators",
    )(
        place,
        owner.reshape(1, gens),
        local_bus.reshape(folded),
        cost.reshape(folded),
        dispatch,
        gen_max.reshape(folded),
        availability,
    )


def unpack_kernel(block, slot_ref, *refs):
    *back_refs, dispatch_ref, max_ref, avail_ref, out_ref, back_ref = refs
    peers, cap, _ = back_refs[0].shape
    for i, ref in enumerate(back_refs):
        for j in range(peers):
            start = (j * len(back_refs) + i) * cap
            back_ref[start : start + cap, :] = ref[j]
    gens = slot_ref.shape[1]
    slot = jnp.broadcast_to(slot_ref[...].astype(F32), (128, gens)).T[:, 0:1].astype(jnp.int32)
    at = lax.broadcasted_iota(jnp.int32, (gens, block), 1)
    change = None
    for start in range(0, back_ref.shape[0], block):
        pick = (at == slot - start).astype(F32).astype(BF16)
        part = dot(pick, back_ref[start : start + block, :])
        change = part if change is None else change + part
    dispatch = dispatch_ref[...]
    upper = max_ref[...] * avail_ref[...]
    sent = dispatch.astype(BF16).astype(F32)
    to_upper = (upper.astype(BF16).astype(F32) - sent).astype(BF16).astype(F32)
    moved = jnp.minimum(jnp.maximum(dispatch + change, 0.0), upper)
    moved = jnp.where(change == to_upper, upper, moved)
    out_ref[...] = jnp.where(change == -sent, 0.0, moved)


def unpack(slot, backs, dispatch, gen_max, availability):
    gens = slot.shape[1]
    peers, cap, hours = backs[0].shape
    slots = len(backs) * peers * cap
    block = next(size for size in (768, 256, 128, 16) if slots % size == 0)
    return pl.pallas_call(
        functools.partial(unpack_kernel, block),
        out_shape=jax.ShapeDtypeStruct((gens, hours), F32),
        scratch_shapes=[pltpu.VMEM((slots, hours), BF16)],
        compiler_params=pltpu.CompilerParams(vmem_limit_bytes=LIMIT),
        cost_estimate=pl.CostEstimate(flops=2 * slots * gens * hours, bytes_accessed=1 << 20, transcendentals=0),
        name="unpack_dispatch",
    )(slot, *backs, dispatch, gen_max, availability)


def update_kernel(cap, devices, first, last, parts, chunks, place_ref, *refs):
    price_refs, refs = refs[:parts], refs[parts:]
    recv_ref, balance_ref, demand_ref, *refs = refs
    if not first:
        prev_ref, *refs = refs
    copies = []
    if chunks:
        ptdf_ref, upd_ref, inj_ref, *held_refs, shadow_ref, acc_ref, extra_ref, sems = refs
        copies = column_copies(place_ref, ptdf_ref, chunks, held_refs, sems)
    else:
        upd_ref, inj_ref, shadow_ref, acc_ref, extra_ref = refs
    for copy in copies:
        copy.start()
    buses, hours = demand_ref.shape
    wide = 2 * hours
    pad = extra_ref.shape[0] // devices
    shadow = price_refs[0][...].astype(F32)
    for ref in price_refs[1:]:
        shadow = shadow + ref[...].astype(F32)
    hi, lo = halves(shadow)
    shadow_ref[:hours, :] = hi
    shadow_ref[hours:, :] = lo
    eye = (
        lax.broadcasted_iota(jnp.int32, (cap, wide), 0) == lax.broadcasted_iota(jnp.int32, (cap, wide), 1)
    ).astype(F32)
    buses_at = lax.broadcasted_iota(jnp.int32, (cap, buses), 1)
    at_row = lax.broadcasted_iota(jnp.int32, (buses, pad), 0)
    for start in range(0, devices, GROUP):
        peers = range(start, start + GROUP)
        meta = jnp.concatenate([recv_ref[peer, cap:, :] for peer in peers], axis=0)
        columns = dot(eye.astype(BF16), meta, NT)
        picks = []
        for i in range(GROUP):
            at = i * META
            bus_column = ((columns[:, at : at + 1] - 1.0) * 128.0 + columns[:, at + 1 : at + 2]).astype(jnp.int32)
            picks.append((buses_at == bus_column).astype(F32).astype(BF16))
        both = dot(jnp.concatenate(picks, axis=0), shadow_ref[...], NT)
        for i, peer in enumerate(peers):
            at = i * META
            cost = (columns[:, at + 2 : at + 3] + columns[:, at + 3 : at + 4]) + columns[:, at + 4 : at + 5]
            rows = slice(i * cap, (i + 1) * cap)
            price = both[rows, :hours] + both[rows, hours:] + balance_ref[...]
            sent = recv_ref[peer, :cap, :hours].astype(F32)
            dispatch = sent if first else prev_ref[peer]
            upper = recv_ref[peer, :cap, hours:].astype(F32)
            updated = jnp.minimum(jnp.maximum(dispatch - tau_step * (cost + price), 0.0), upper)
            if last:
                upd_ref[peer ^ place_ref[0]] = (updated - sent).astype(BF16)
            else:
                upd_ref[peer] = updated
            hi, lo = halves(2.0 * updated - dispatch)
            extra_ref[peer * pad : peer * pad + cap, :hours] = hi
            extra_ref[peer * pad : peer * pad + cap, hours:] = lo
            if pad > cap:
                extra_ref[peer * pad + cap : (peer + 1) * pad, :] = jnp.zeros((pad - cap, wide), BF16)
        picks = []
        for peer in peers:
            row = recv_ref[peer, cap:, :pad].astype(F32)
            bus_row = ((row[0:1] - 1.0) * 128.0 + row[1:2]).astype(jnp.int32)
            picks.append((at_row == bus_row).astype(F32).astype(BF16))
        sums = dot(jnp.concatenate(picks, axis=1), extra_ref[start * pad : (start + GROUP) * pad, :])
        acc_ref[...] = sums if start == 0 else acc_ref[...] + sums
    injection = acc_ref[:, :hours] + acc_ref[:, hours:] - demand_ref[...]
    inj_ref[:buses, :] = injection.astype(BF16)
    hi, mid, low = thirds(jnp.sum(injection, axis=0, keepdims=True))
    row = lax.broadcasted_iota(jnp.int32, (META, hours), 0)
    tail = jnp.where(row == 0, hi.astype(F32), 0.0)
    tail = jnp.where(row == 1, mid.astype(F32), tail)
    tail = jnp.where(row == 2, low.astype(F32), tail)
    inj_ref[buses:, :] = tail.astype(BF16)
    for copy in copies:
        copy.wait()


def update(cap, place, last, prices, balance_price, demand, recv, previous, ptdf, chunks):
    devices = recv.shape[0]
    buses, hours = demand.shape
    first = previous is None
    operands = [place, *prices, recv, balance_price, demand] + ([] if first else [previous])
    in_specs = [SMEM_SPEC] + [VMEM_SPEC] * (len(operands) - 1)
    out_shape = [
        jax.ShapeDtypeStruct((devices, cap, hours), BF16 if last else F32),
        jax.ShapeDtypeStruct((buses + META, hours), BF16),
    ]
    scratch = [
        pltpu.VMEM((2 * hours, buses), BF16),
        pltpu.VMEM((buses, 2 * hours), F32),
        pltpu.VMEM((devices * (-(-cap // 128) * 128), 2 * hours), BF16),
    ]
    if chunks:
        operands.append(in_hbm(ptdf))
        in_specs.append(HBM_SPEC)
        out_shape += [pltpu.VMEM((ptdf.shape[0], 4 * buses), BF16)] * len(chunks)
        scratch.append(pltpu.SemaphoreType.DMA((len(chunks), 4)))
    return pl.pallas_call(
        functools.partial(update_kernel, cap, devices, first, last, len(prices), chunks),
        in_specs=in_specs,
        out_specs=tuple([VMEM_SPEC] * len(out_shape)),
        out_shape=tuple(out_shape),
        scratch_shapes=scratch,
        compiler_params=pltpu.CompilerParams(vmem_limit_bytes=LIMIT),
        cost_estimate=pl.CostEstimate(flops=8 * devices * cap * buses * hours, bytes_accessed=4 << 20, transcendentals=0),
        name="update_generators",
    )(*operands)


def shadow_kernel(chunk, stream, turn, place_ref, line_ref, ptdf_ref, keep_ref, send_ref, *rest):
    buses = keep_ref.shape[2]
    columns = [slice(rel * buses, (rel + 1) * buses) for rel in range(4)]
    if stream:
        if turn:
            line_t_ref, held_ref, sems, line_held_ref = rest
            line_copy = pltpu.make_async_copy(line_ref, line_held_ref, sems.at[4])
            line_copy.start()
        else:
            held_ref, sems = rest
        copies = []
        for rel in range(4):
            start = pl.multiple_of((place_ref[0] ^ (4 * chunk + rel)) * buses, 128)
            copies.append(
                pltpu.make_async_copy(
                    ptdf_ref.at[:, pl.ds(start, buses)], held_ref.at[:, columns[rel]], sems.at[rel]
                )
            )
        for rel in (3, 2, 1, 0):
            copies[rel].start()
        if turn:
            line_copy.wait()
            line_t_ref[...] = line_held_ref[...].T.astype(BF16)
            line_ref = line_t_ref
    else:
        held_ref = ptdf_ref

    def part(rel):
        if stream:
            copies[rel].wait()
        return dot(line_ref[...], held_ref[:, columns[rel]])

    send_ref[1] = part(3).astype(BF16)
    keep_ref[1] = part(2)
    send_ref[0] = part(1).astype(BF16)
    keep_ref[0] = part(0)


def in_hbm(x):
    return pltpu.with_memory_space_constraint(x, pltpu.MemorySpace.HBM)


def chunk_cost(hours, lines, buses):
    return pl.CostEstimate(flops=COST * 8 * hours * lines * buses, bytes_accessed=8 * lines * buses, transcendentals=0)


def shadow_chunk(chunk, stream, place, line, ptdf, buses):
    turn = line.dtype == F32
    lines, hours = line.shape if turn else line.shape[::-1]
    out_shape = [
        jax.ShapeDtypeStruct((2, hours, buses), F32),
        jax.ShapeDtypeStruct((2, hours, buses), BF16),
    ]
    scratch = [pltpu.VMEM((lines, 4 * buses), BF16), pltpu.SemaphoreType.DMA((5,))] if stream else []
    if turn:
        out_shape.append(jax.ShapeDtypeStruct((hours, lines), BF16))
        scratch.append(pltpu.VMEM((lines, hours), F32))
    return pl.pallas_call(
        functools.partial(shadow_kernel, chunk, stream, turn),
        in_specs=[SMEM_SPEC, HBM_SPEC if turn else VMEM_SPEC, HBM_SPEC if stream else VMEM_SPEC],
        out_specs=tuple([VMEM_SPEC] * len(out_shape)),
        out_shape=tuple(out_shape),
        scratch_shapes=scratch,
        compiler_params=pltpu.CompilerParams(vmem_limit_bytes=LIMIT),
        cost_estimate=chunk_cost(hours, lines, buses),
        name="shadow_chunk",
    )(place, in_hbm(line) if turn else line, in_hbm(ptdf) if stream else ptdf)


def column_copies(place_ref, ptdf_ref, chunks, held_refs, sems):
    buses = held_refs[0].shape[1] // 4
    copies = []
    for i, chunk in enumerate(chunks):
        for rel in range(4):
            start = pl.multiple_of((place_ref[0] ^ (4 * chunk + rel)) * buses, 128)
            copies.append(
                pltpu.make_async_copy(
                    ptdf_ref.at[:, pl.ds(start, buses)],
                    held_refs[i].at[:, pl.ds(rel * buses, buses)],
                    sems.at[i, rel],
                )
            )
    return copies


def load_kernel(chunks, place_ref, ptdf_ref, token_ref, *rest):
    *held_refs, sems = rest
    copies = column_copies(place_ref, ptdf_ref, chunks, held_refs, sems)
    for copy in copies:
        copy.start()
    token_ref[0] = place_ref[0]
    for copy in copies:
        copy.wait()


def load_chunks(chunks, place, ptdf, buses):
    lines = ptdf.shape[0]
    count = len(chunks)
    token, *held = pl.pallas_call(
        functools.partial(load_kernel, chunks),
        in_specs=[SMEM_SPEC, HBM_SPEC],
        out_specs=tuple([SMEM_SPEC] + [VMEM_SPEC] * count),
        out_shape=tuple([jax.ShapeDtypeStruct((1,), jnp.int32)] + [pltpu.VMEM((lines, 4 * buses), BF16)] * count),
        scratch_shapes=[pltpu.SemaphoreType.DMA((count, 4))],
        compiler_params=pltpu.CompilerParams(vmem_limit_bytes=LIMIT),
        cost_estimate=pl.CostEstimate(flops=0, bytes_accessed=8 * count * lines * buses, transcendentals=0),
        name="load_chunks",
    )(place, in_hbm(ptdf))
    return token, held


def flow_kernel(start, end, ptdf_ref, b0, b1, b2, b3, acc_ref, sum_ref, *rest):
    if end:
        limit_ref, line_ref, out_ref, half_ref, sum_out, inj_ref = rest
    else:
        out_ref, sum_out, inj_ref = rest
    buses = inj_ref.shape[0] // 4
    total = jnp.zeros(sum_ref.shape, F32) if start else sum_ref[...]
    for rel, ref in enumerate((b0, b1, b2, b3)):
        inj_ref[rel * buses : (rel + 1) * buses, :] = ref[:buses, :]
        tail = ref[buses:, :].astype(F32)
        total = total + jnp.sum(tail, axis=0, keepdims=True)
    sum_out[...] = total
    tile = ptdf_ref.shape[0] // 4

    def body(i, carry):
        rows = pl.ds(pl.multiple_of(i * tile, tile), tile)
        flow = dot(ptdf_ref[rows, :], inj_ref[...])
        if not start:
            flow = flow + acc_ref[rows, :]
        if end:
            shifted = line_ref[rows, :] + sigma_step * flow
            limit = limit_ref[rows, :]
            line = shifted - sigma_step * jnp.minimum(jnp.maximum(shifted / sigma_step, -limit), limit)
            out_ref[rows, :] = line
        else:
            out_ref[rows, :] = flow
        return carry

    lax.fori_loop(0, 4, body, 0)
    if end:
        half_ref[...] = out_ref[...].T.astype(BF16)


def flow_chunk(ptdf, blocks, acc, total, limit=None, line=None):
    lines = ptdf.shape[0]
    rows, hours = blocks[0].shape
    buses = rows - META
    start, end = acc is None, limit is not None
    operands = [ptdf, *blocks, total if start else acc, total]
    out_shape = [jax.ShapeDtypeStruct((lines, hours), F32)]
    if end:
        operands += [limit, line]
        out_shape += [jax.ShapeDtypeStruct((hours, lines), BF16)]
    out_shape += [jax.ShapeDtypeStruct((1, hours), F32)]
    return pl.pallas_call(
        functools.partial(flow_kernel, start, end),
        in_specs=[VMEM_SPEC] * len(operands),
        out_shape=tuple(out_shape),
        scratch_shapes=[pltpu.VMEM((4 * buses, hours), BF16)],
        compiler_params=pltpu.CompilerParams(vmem_limit_bytes=LIMIT),
        cost_estimate=chunk_cost(hours, lines, buses),
        name="flow_chunk",
    )(*operands)


def swap(x, devices, mask):
    return lax.ppermute(x, "bus", [(i, i ^ mask) for i in range(devices)])


def local(
    ptdf,
    line_limit,
    gen_cost,
    gen_max,
    gen_owner,
    gen_local,
    availability,
    demand,
    dispatch,
    balance_price,
    line_price,
):
    devices = lax.axis_size("bus")
    place = lax.axis_index("bus").astype(jnp.int32).reshape(1)
    buses = demand.shape[0]
    all_buses = buses * devices
    gens, hours = dispatch.shape
    cap = -(-max(2, 3 * gens // devices) // 16) * 16
    staged = devices == 16 and buses % 128 == 0

    near_place = place if staged else jnp.zeros_like(place)
    outgoing, slot = pack(
        devices,
        cap,
        near_place,
        gen_owner,
        gen_local,
        gen_cost,
        dispatch,
        gen_max,
        availability,
    )
    limit = line_limit.reshape(-1, 1)
    balance_row = balance_price.reshape(1, hours)
    line_half = line_price if staged else line_price.astype(BF16)
    recv = lax.all_to_all(outgoing, "bus", split_axis=0, concat_axis=0, tiled=True)
    held, resident = None, {}
    for iteration in range(ITERS):
        last = iteration == ITERS - 1
        if staged:
            line_t = line_half
            keeps, gots, crossed, parts = {}, {}, {}, {}

            def across(chunk):
                both = (keeps[chunk][1] + gots[chunk][1].astype(F32)).astype(BF16)
                crossed[chunk] = swap(both, devices, 2)
                return both

            def settle(chunk):
                part = keeps[chunk][0] + gots[chunk][0].astype(F32) + crossed[chunk].astype(F32)
                if chunk == 2:
                    part = part + parts[3].astype(F32)
                if chunk:
                    part = part.astype(BF16)
                    parts[chunk] = swap(part, devices, 8 if chunk == 2 else 4)
                else:
                    parts[chunk] = part
                return part

            def product(chunk, line_t):
                columns = resident.get(chunk, ptdf)
                keeps[chunk], send, *turned = shadow_chunk(
                    chunk, chunk not in resident, place, line_t, columns, buses
                )
                gots[chunk] = swap(send, devices, 1)
                return turned[0] if turned else line_t

            line_t = product(3, line_t)
            if iteration == 0:
                line_t, _ = lax.optimization_barrier((line_t, outgoing))
            product(2, line_t)
            line_t, _ = lax.optimization_barrier((line_t, across(3)))
            product(1, line_t)
            line_t, _, _ = lax.optimization_barrier((line_t, across(2), settle(3)))
            product(0, line_t)
            gots[1], crossed[2] = lax.optimization_barrier((gots[1], crossed[2]))
            parts[3], _, _ = lax.optimization_barrier((parts[3], across(1), across(0)))
            crossed[1], _ = lax.optimization_barrier((crossed[1], settle(2)))
            settle(1)
            settle(0)
            prices = [parts[0], parts[1], parts[2]]
        else:
            shadow = lax.dot_general(ptdf, line_half, (((0,), (0,)), ((), ())), preferred_element_type=F32)
            prices = [lax.psum_scatter(shadow, "bus", scatter_dimension=0, tiled=True).T]
        chunks = (0, 1) if staged and not last else ()
        held, block, *loaded = update(
            cap, place if staged else near_place, last, prices, balance_row, demand, recv, held, ptdf, chunks
        )
        resident.update(zip(chunks, loaded))
        if staged:
            near, far, cross, far_cross = {0: block}, {}, {}, {}

            def spread(chunk):
                far[chunk] = swap(near[chunk], devices, 2)
                cross[chunk] = swap(near[chunk], devices, 1)

            def settle_far(chunk):
                far_cross[chunk] = swap(far[chunk], devices, 1)

            def blocks(chunk):
                return [near[chunk], cross[chunk], far[chunk], far_cross[chunk]]

            near[2] = swap(block, devices, 8)
            near[1] = swap(block, devices, 4)
            spread(0)
            stage = [near[1], near[2], far[0]]
            if not last:
                cross[0], here = lax.optimization_barrier((cross[0], place))
                place, (resident[2], resident[3]) = load_chunks((2, 3), here, ptdf, buses)
                stage.append(place)
            near[1], near[2], far[0], *rest = lax.optimization_barrier(stage)
            place = rest[0] if rest else place
            near[3] = swap(near[2], devices, 4)
            spread(1)
            spread(2)
            settle_far(0)
            acc, total = flow_chunk(resident[0], blocks(0), None, balance_row)
            near[3], acc = lax.optimization_barrier((near[3], acc))
            spread(3)
            if last:
                home, _ = lax.optimization_barrier((held, cross[0]))
                home = home.reshape(4, 4, *home.shape[1:])
                home = [home[0]] + [swap(home[chunk], devices, 4 * chunk) for chunk in (1, 2, 3)]
            settle_far(1)
            acc, total = flow_chunk(resident[1], blocks(1), acc, total)
            settle_far(2)
            if last:
                far[3], acc, *home = lax.optimization_barrier((far[3], acc, *home))
            else:
                far[3], acc = lax.optimization_barrier((far[3], acc))
            settle_far(3)
            acc, total = flow_chunk(resident[2], blocks(2), acc, total)
            if last:
                back = [jnp.stack([home[chunk][rel] for chunk in range(4)]) for rel in range(4)]
                back = [back[0]] + [swap(back[rel], devices, rel) for rel in (1, 2, 3)]
            line_price, line_half, total = flow_chunk(resident[3], blocks(3), acc, total, limit, line_price)
            balance = total
        else:
            if last:
                back = [lax.all_to_all(held, "bus", split_axis=0, concat_axis=0, tiled=True)]
            every = lax.all_gather(block, "bus", axis=0, tiled=False)
            balance = jnp.sum(every[:, buses:].astype(F32), axis=(0, 1)).reshape(1, hours)
            flow = jnp.dot(ptdf, every[:, :buses].reshape(all_buses, hours), preferred_element_type=F32)
            shifted = line_price + sigma_step * flow
            line_price = shifted - sigma_step * jnp.clip(shifted / sigma_step, -limit, limit)
            line_half = line_price.astype(BF16)
        balance_row = balance_row + sigma_step * balance / all_buses
    dispatch = unpack(slot, back, dispatch, gen_max.reshape(gens, 1), availability)
    return (dispatch, balance_row.reshape(hours), line_price)


def solution(mesh):
    return jax.shard_map(
        local,
        mesh=mesh,
        in_specs=(
            P("bus", None),
            P("bus"),
            P("bus"),
            P("bus"),
            P("bus", None),
            P("bus"),
            P(("cases", "bus"), None),
            P(("cases", "bus"), None),
            P(("cases", "bus"), None),
            P("cases"),
            P(("cases", "bus"), None),
        ),
        out_specs=(P(("cases", "bus"), None), P("cases"), P(("cases", "bus"), None)),
        check_vma=False,
    )
```

```python
import functools

import jax
import jax.numpy as jnp
from jax import lax
from jax.experimental import pallas as pl
from jax.experimental.pallas import tpu as pltpu
from jax.sharding import PartitionSpec as P

ITERS = 2

tau_step = 0.2
sigma_step = 0.15

GROUP = 4
LIMIT = 16 << 20
COST = 3
META = 16
HBM_SPEC = pl.BlockSpec(memory_space=pltpu.MemorySpace.HBM)
VMEM_SPEC = pl.BlockSpec(memory_space=pltpu.VMEM)
SMEM_SPEC = pl.BlockSpec(memory_space=pltpu.SMEM)
F32 = jnp.float32
BF16 = jnp.bfloat16
NT = (((1,), (1,)), ((), ()))
NN = (((1,), (0,)), ((), ()))


def dot(a, b, dims=NN):
    return lax.dot_general(a, b, dims, preferred_element_type=F32)


def halves(x):
    hi = x.astype(BF16)
    lo = (x - hi.astype(F32)).astype(BF16)
    return hi, lo


def thirds(x):
    hi = x.astype(BF16)
    rest = x - hi.astype(F32)
    mid = rest.astype(BF16)
    low = (rest - mid.astype(F32)).astype(BF16)
    return hi, mid, low


def as_row(ref):
    return jnp.concatenate([ref[i : i + 1, :] for i in range(ref.shape[0])], axis=1)


def pack_kernel(
    cap, devices, place_ref, owner_ref, local_ref, cost_ref, dispatch_ref, max_ref, avail_ref,
    out_ref, near_ref, slot_ref, pay_ref, meta_ref,
):
    step = pl.program_id(0)
    gens, hours = dispatch_ref.shape
    group = out_ref.shape[0]

    @pl.when(step == 0)
    def _():
        owner = owner_ref[...]
        hits = (lax.broadcasted_iota(jnp.int32, (devices, gens), 0) == owner).astype(F32)
        before = (
            lax.broadcasted_iota(jnp.int32, (gens, gens), 0) < lax.broadcasted_iota(jnp.int32, (gens, gens), 1)
        ).astype(F32)
        count = dot(hits.astype(BF16), before.astype(BF16))
        rank = jnp.sum(count * hits, axis=0, keepdims=True).astype(jnp.int32)
        slot_ref[...] = owner * cap + rank
        near_ref[...] = (owner ^ place_ref[0]) * cap + rank
        pay_ref[:, :hours] = dispatch_ref[...].astype(BF16)
        lanes = max_ref.shape[1]
        eye = (
            lax.broadcasted_iota(jnp.int32, (lanes, lanes), 0) == lax.broadcasted_iota(jnp.int32, (lanes, lanes), 1)
        ).astype(F32)
        for i in range(gens // lanes):
            rows = slice(i * lanes, (i + 1) * lanes)
            most = jnp.sum(eye * max_ref[i : i + 1, :], axis=1, keepdims=True)
            pay_ref[rows, hours:] = (most * avail_ref[rows, :]).astype(BF16)
        local = as_row(local_ref)
        hi, mid, low = thirds(as_row(cost_ref))
        row = lax.broadcasted_iota(jnp.int32, (META, gens), 0)
        parts = [
            (lax.shift_right_logical(local, 7) + 1).astype(F32),
            (local & 127).astype(F32),
            hi.astype(F32),
            mid.astype(F32),
            low.astype(F32),
        ]
        meta = jnp.zeros((META, gens), F32)
        for i, part in enumerate(parts):
            meta = jnp.where(row == i, part, meta)
        meta_ref[...] = meta.astype(BF16)

    slot = slot_ref[...] - step * (group * cap)
    place = lax.broadcasted_iota(jnp.int32, (cap, gens), 0)
    picks = [(place == slot - i * cap).astype(F32).astype(BF16) for i in range(group)]
    moved = dot(jnp.concatenate(picks, axis=0), pay_ref[...]).astype(BF16)
    for i in range(group):
        out_ref[i, :cap, :] = moved[i * cap : (i + 1) * cap]
        out_ref[i, cap:, :] = jnp.zeros((META, 2 * hours), BF16)
        out_ref[i, cap:, :cap] = dot(meta_ref[...], picks[i], NT).astype(BF16)


def pack(devices, cap, place, owner, local_bus, cost, dispatch, gen_max, availability):
    gens, hours = dispatch.shape
    full = lambda *shape: pl.BlockSpec(shape, lambda i: (0,) * len(shape))
    folded = (gens // 128, 128)
    return pl.pallas_call(
        functools.partial(pack_kernel, cap, devices),
        grid=(devices // GROUP,),
        out_shape=(
            jax.ShapeDtypeStruct((devices, cap + META, 2 * hours), BF16),
            jax.ShapeDtypeStruct((1, gens), jnp.int32),
        ),
        in_specs=[
            SMEM_SPEC,
            full(1, gens),
            full(*folded),
            full(*folded),
            full(gens, hours),
            full(*folded),
            full(gens, hours),
        ],
        out_specs=(pl.BlockSpec((GROUP, cap + META, 2 * hours), lambda i: (i, 0, 0)), full(1, gens)),
        scratch_shapes=[
            pltpu.VMEM((1, gens), jnp.int32),
            pltpu.VMEM((gens, 2 * hours), BF16),
            pltpu.VMEM((META, gens), BF16),
        ],
        compiler_params=pltpu.CompilerParams(vmem_limit_bytes=LIMIT),
        cost_estimate=pl.CostEstimate(flops=4 * devices * cap * gens * hours, bytes_accessed=3 << 20, transcendentals=0),
        name="pack_generators",
    )(
        place,
        owner.reshape(1, gens),
        local_bus.reshape(folded),
        cost.reshape(folded),
        dispatch,
        gen_max.reshape(folded),
        availability,
    )


def unpack_kernel(block, slot_ref, *refs):
    *back_refs, dispatch_ref, max_ref, avail_ref, out_ref, back_ref = refs
    peers, cap, _ = back_refs[0].shape
    for i, ref in enumerate(back_refs):
        for j in range(peers):
            start = (i * peers + j) * cap
            back_ref[start : start + cap, :] = ref[j]
    gens = slot_ref.shape[1]
    slot = jnp.broadcast_to(slot_ref[...].astype(F32), (128, gens)).T[:, 0:1].astype(jnp.int32)
    at = lax.broadcasted_iota(jnp.int32, (gens, block), 1)
    change = None
    for start in range(0, back_ref.shape[0], block):
        pick = (at == slot - start).astype(F32).astype(BF16)
        part = dot(pick, back_ref[start : start + block, :])
        change = part if change is None else change + part
    dispatch = dispatch_ref[...]
    upper = max_ref[...] * avail_ref[...]
    sent = dispatch.astype(BF16).astype(F32)
    to_upper = (upper.astype(BF16).astype(F32) - sent).astype(BF16).astype(F32)
    moved = jnp.minimum(jnp.maximum(dispatch + change, 0.0), upper)
    moved = jnp.where(change == to_upper, upper, moved)
    out_ref[...] = jnp.where(change == -sent, 0.0, moved)


def unpack(slot, backs, dispatch, gen_max, availability):
    gens = slot.shape[1]
    peers, cap, hours = backs[0].shape
    slots = len(backs) * peers * cap
    block = next(size for size in (768, 256, 128, 16) if slots % size == 0)
    return pl.pallas_call(
        functools.partial(unpack_kernel, block),
        out_shape=jax.ShapeDtypeStruct((gens, hours), F32),
        scratch_shapes=[pltpu.VMEM((slots, hours), BF16)],
        compiler_params=pltpu.CompilerParams(vmem_limit_bytes=LIMIT),
        cost_estimate=pl.CostEstimate(flops=2 * slots * gens * hours, bytes_accessed=1 << 20, transcendentals=0),
        name="unpack_dispatch",
    )(slot, *backs, dispatch, gen_max, availability)


def update_kernel(cap, devices, first, last, parts, chunks, place_ref, *refs):
    price_refs, refs = refs[:parts], refs[parts:]
    recv_ref, balance_ref, demand_ref, *refs = refs
    if not first:
        prev_ref, *refs = refs
    copies = []
    if chunks:
        ptdf_ref, upd_ref, inj_ref, *held_refs, shadow_ref, acc_ref, extra_ref, sems = refs
        copies = column_copies(place_ref, ptdf_ref, chunks, held_refs, sems)
    else:
        upd_ref, inj_ref, shadow_ref, acc_ref, extra_ref = refs
    for copy in copies:
        copy.start()
    buses, hours = demand_ref.shape
    wide = 2 * hours
    pad = extra_ref.shape[0] // devices
    shadow = price_refs[0][...].astype(F32)
    for ref in price_refs[1:]:
        shadow = shadow + ref[...].astype(F32)
    hi, lo = halves(shadow)
    shadow_ref[:hours, :] = hi
    shadow_ref[hours:, :] = lo
    eye = (
        lax.broadcasted_iota(jnp.int32, (cap, wide), 0) == lax.broadcasted_iota(jnp.int32, (cap, wide), 1)
    ).astype(F32)
    buses_at = lax.broadcasted_iota(jnp.int32, (cap, buses), 1)
    at_row = lax.broadcasted_iota(jnp.int32, (buses, pad), 0)
    for start in range(0, devices, GROUP):
        peers = range(start, start + GROUP)
        meta = jnp.concatenate([recv_ref[peer, cap:, :] for peer in peers], axis=0)
        columns = dot(eye.astype(BF16), meta, NT)
        picks = []
        for i in range(GROUP):
            at = i * META
            bus_column = ((columns[:, at : at + 1] - 1.0) * 128.0 + columns[:, at + 1 : at + 2]).astype(jnp.int32)
            picks.append((buses_at == bus_column).astype(F32).astype(BF16))
        both = dot(jnp.concatenate(picks, axis=0), shadow_ref[...], NT)
        for i, peer in enumerate(peers):
            at = i * META
            cost = (columns[:, at + 2 : at + 3] + columns[:, at + 3 : at + 4]) + columns[:, at + 4 : at + 5]
            rows = slice(i * cap, (i + 1) * cap)
            price = both[rows, :hours] + both[rows, hours:] + balance_ref[...]
            sent = recv_ref[peer, :cap, :hours].astype(F32)
            dispatch = sent if first else prev_ref[peer]
            upper = recv_ref[peer, :cap, hours:].astype(F32)
            updated = jnp.minimum(jnp.maximum(dispatch - tau_step * (cost + price), 0.0), upper)
            if last:
                upd_ref[peer ^ place_ref[0]] = (updated - sent).astype(BF16)
            else:
                upd_ref[peer] = updated
            hi, lo = halves(2.0 * updated - dispatch)
            extra_ref[peer * pad : peer * pad + cap, :hours] = hi
            extra_ref[peer * pad : peer * pad + cap, hours:] = lo
            if pad > cap:
                extra_ref[peer * pad + cap : (peer + 1) * pad, :] = jnp.zeros((pad - cap, wide), BF16)
        picks = []
        for peer in peers:
            row = recv_ref[peer, cap:, :pad].astype(F32)
            bus_row = ((row[0:1] - 1.0) * 128.0 + row[1:2]).astype(jnp.int32)
            picks.append((at_row == bus_row).astype(F32).astype(BF16))
        sums = dot(jnp.concatenate(picks, axis=1), extra_ref[start * pad : (start + GROUP) * pad, :])
        acc_ref[...] = sums if start == 0 else acc_ref[...] + sums
    injection = acc_ref[:, :hours] + acc_ref[:, hours:] - demand_ref[...]
    inj_ref[:buses, :] = injection.astype(BF16)
    hi, mid, low = thirds(jnp.sum(injection, axis=0, keepdims=True))
    row = lax.broadcasted_iota(jnp.int32, (META, hours), 0)
    tail = jnp.where(row == 0, hi.astype(F32), 0.0)
    tail = jnp.where(row == 1, mid.astype(F32), tail)
    tail = jnp.where(row == 2, low.astype(F32), tail)
    inj_ref[buses:, :] = tail.astype(BF16)
    for copy in copies:
        copy.wait()


def update(cap, place, last, prices, balance_price, demand, recv, previous, ptdf, chunks):
    devices = recv.shape[0]
    buses, hours = demand.shape
    first = previous is None
    operands = [place, *prices, recv, balance_price, demand] + ([] if first else [previous])
    in_specs = [SMEM_SPEC] + [VMEM_SPEC] * (len(operands) - 1)
    out_shape = [
        jax.ShapeDtypeStruct((devices, cap, hours), BF16 if last else F32),
        jax.ShapeDtypeStruct((buses + META, hours), BF16),
    ]
    scratch = [
        pltpu.VMEM((2 * hours, buses), BF16),
        pltpu.VMEM((buses, 2 * hours), F32),
        pltpu.VMEM((devices * (-(-cap // 128) * 128), 2 * hours), BF16),
    ]
    if chunks:
        operands.append(in_hbm(ptdf))
        in_specs.append(HBM_SPEC)
        out_shape += [pltpu.VMEM((ptdf.shape[0], 4 * buses), BF16)] * len(chunks)
        scratch.append(pltpu.SemaphoreType.DMA((len(chunks), 4)))
    return pl.pallas_call(
        functools.partial(update_kernel, cap, devices, first, last, len(prices), chunks),
        in_specs=in_specs,
        out_specs=tuple([VMEM_SPEC] * len(out_shape)),
        out_shape=tuple(out_shape),
        scratch_shapes=scratch,
        compiler_params=pltpu.CompilerParams(vmem_limit_bytes=LIMIT),
        cost_estimate=pl.CostEstimate(flops=8 * devices * cap * buses * hours, bytes_accessed=4 << 20, transcendentals=0),
        name="update_generators",
    )(*operands)


def shadow_kernel(chunk, stream, turn, place_ref, line_ref, ptdf_ref, keep_ref, send_ref, *rest):
    buses = keep_ref.shape[2]
    columns = [slice(rel * buses, (rel + 1) * buses) for rel in range(4)]
    if stream:
        if turn:
            line_t_ref, held_ref, sems, line_held_ref = rest
            line_copy = pltpu.make_async_copy(line_ref, line_held_ref, sems.at[4])
            line_copy.start()
        else:
            held_ref, sems = rest
        copies = []
        for rel in range(4):
            start = pl.multiple_of((place_ref[0] ^ (4 * chunk + rel)) * buses, 128)
            copies.append(
                pltpu.make_async_copy(
                    ptdf_ref.at[:, pl.ds(start, buses)], held_ref.at[:, columns[rel]], sems.at[rel]
                )
            )
        for rel in (3, 2, 1, 0):
            copies[rel].start()
        if turn:
            line_copy.wait()
            line_t_ref[...] = line_held_ref[...].T.astype(BF16)
            line_ref = line_t_ref
    else:
        held_ref = ptdf_ref

    def part(rel):
        if stream:
            copies[rel].wait()
        return dot(line_ref[...], held_ref[:, columns[rel]])

    send_ref[1] = part(3).astype(BF16)
    keep_ref[1] = part(2)
    send_ref[0] = part(1).astype(BF16)
    keep_ref[0] = part(0)


def in_hbm(x):
    return pltpu.with_memory_space_constraint(x, pltpu.MemorySpace.HBM)


def chunk_cost(hours, lines, buses):
    return pl.CostEstimate(flops=COST * 8 * hours * lines * buses, bytes_accessed=8 * lines * buses, transcendentals=0)


def shadow_chunk(chunk, stream, place, line, ptdf, buses):
    turn = line.dtype == F32
    lines, hours = line.shape if turn else line.shape[::-1]
    out_shape = [
        jax.ShapeDtypeStruct((2, hours, buses), F32),
        jax.ShapeDtypeStruct((2, hours, buses), BF16),
    ]
    scratch = [pltpu.VMEM((lines, 4 * buses), BF16), pltpu.SemaphoreType.DMA((5,))] if stream else []
    if turn:
        out_shape.append(jax.ShapeDtypeStruct((hours, lines), BF16))
        scratch.append(pltpu.VMEM((lines, hours), F32))
    return pl.pallas_call(
        functools.partial(shadow_kernel, chunk, stream, turn),
        in_specs=[SMEM_SPEC, HBM_SPEC if turn else VMEM_SPEC, HBM_SPEC if stream else VMEM_SPEC],
        out_specs=tuple([VMEM_SPEC] * len(out_shape)),
        out_shape=tuple(out_shape),
        scratch_shapes=scratch,
        compiler_params=pltpu.CompilerParams(vmem_limit_bytes=LIMIT),
        cost_estimate=chunk_cost(hours, lines, buses),
        name="shadow_chunk",
    )(place, in_hbm(line) if turn else line, in_hbm(ptdf) if stream else ptdf)


def column_copies(place_ref, ptdf_ref, chunks, held_refs, sems):
    buses = held_refs[0].shape[1] // 4
    copies = []
    for i, chunk in enumerate(chunks):
        for rel in range(4):
            start = pl.multiple_of((place_ref[0] ^ (4 * chunk + rel)) * buses, 128)
            copies.append(
                pltpu.make_async_copy(
                    ptdf_ref.at[:, pl.ds(start, buses)],
                    held_refs[i].at[:, pl.ds(rel * buses, buses)],
                    sems.at[i, rel],
                )
            )
    return copies


def load_kernel(chunks, place_ref, ptdf_ref, token_ref, *rest):
    *held_refs, sems = rest
    copies = column_copies(place_ref, ptdf_ref, chunks, held_refs, sems)
    for copy in copies:
        copy.start()
    token_ref[0] = place_ref[0]
    for copy in copies:
        copy.wait()


def load_chunks(chunks, place, ptdf, buses):
    lines = ptdf.shape[0]
    count = len(chunks)
    token, *held = pl.pallas_call(
        functools.partial(load_kernel, chunks),
        in_specs=[SMEM_SPEC, HBM_SPEC],
        out_specs=tuple([SMEM_SPEC] + [VMEM_SPEC] * count),
        out_shape=tuple([jax.ShapeDtypeStruct((1,), jnp.int32)] + [pltpu.VMEM((lines, 4 * buses), BF16)] * count),
        scratch_shapes=[pltpu.SemaphoreType.DMA((count, 4))],
        compiler_params=pltpu.CompilerParams(vmem_limit_bytes=LIMIT),
        cost_estimate=pl.CostEstimate(flops=0, bytes_accessed=8 * count * lines * buses, transcendentals=0),
        name="load_chunks",
    )(place, in_hbm(ptdf))
    return token, held


def flow_kernel(start, end, ptdf_ref, b0, b1, b2, b3, acc_ref, sum_ref, *rest):
    if end:
        limit_ref, line_ref, out_ref, half_ref, sum_out, inj_ref = rest
    else:
        out_ref, sum_out, inj_ref = rest
    buses = inj_ref.shape[0] // 4
    total = jnp.zeros(sum_ref.shape, F32) if start else sum_ref[...]
    for rel, ref in enumerate((b0, b1, b2, b3)):
        inj_ref[rel * buses : (rel + 1) * buses, :] = ref[:buses, :]
        tail = ref[buses:, :].astype(F32)
        total = total + jnp.sum(tail, axis=0, keepdims=True)
    sum_out[...] = total
    tile = ptdf_ref.shape[0] // 4

    def body(i, carry):
        rows = pl.ds(pl.multiple_of(i * tile, tile), tile)
        flow = dot(ptdf_ref[rows, :], inj_ref[...])
        if not start:
            flow = flow + acc_ref[rows, :]
        if end:
            shifted = line_ref[rows, :] + sigma_step * flow
            limit = limit_ref[rows, :]
            line = shifted - sigma_step * jnp.minimum(jnp.maximum(shifted / sigma_step, -limit), limit)
            out_ref[rows, :] = line
        else:
            out_ref[rows, :] = flow
        return carry

    lax.fori_loop(0, 4, body, 0)
    if end:
        half_ref[...] = out_ref[...].T.astype(BF16)


def flow_chunk(ptdf, blocks, acc, total, limit=None, line=None):
    lines = ptdf.shape[0]
    rows, hours = blocks[0].shape
    buses = rows - META
    start, end = acc is None, limit is not None
    operands = [ptdf, *blocks, total if start else acc, total]
    out_shape = [jax.ShapeDtypeStruct((lines, hours), F32)]
    if end:
        operands += [limit, line]
        out_shape += [jax.ShapeDtypeStruct((hours, lines), BF16)]
    out_shape += [jax.ShapeDtypeStruct((1, hours), F32)]
    return pl.pallas_call(
        functools.partial(flow_kernel, start, end),
        in_specs=[VMEM_SPEC] * len(operands),
        out_shape=tuple(out_shape),
        scratch_shapes=[pltpu.VMEM((4 * buses, hours), BF16)],
        compiler_params=pltpu.CompilerParams(vmem_limit_bytes=LIMIT),
        cost_estimate=chunk_cost(hours, lines, buses),
        name="flow_chunk",
    )(*operands)


def swap(x, devices, mask):
    return lax.ppermute(x, "bus", [(i, i ^ mask) for i in range(devices)])


def local(
    ptdf,
    line_limit,
    gen_cost,
    gen_max,
    gen_owner,
    gen_local,
    availability,
    demand,
    dispatch,
    balance_price,
    line_price,
):
    devices = lax.axis_size("bus")
    place = lax.axis_index("bus").astype(jnp.int32).reshape(1)
    buses = demand.shape[0]
    all_buses = buses * devices
    gens, hours = dispatch.shape
    cap = -(-max(2, 3 * gens // devices) // 16) * 16
    staged = devices == 16 and buses % 128 == 0

    near_place = place if staged else jnp.zeros_like(place)
    outgoing, slot = pack(
        devices,
        cap,
        near_place,
        gen_owner,
        gen_local,
        gen_cost,
        dispatch,
        gen_max,
        availability,
    )
    limit = line_limit.reshape(-1, 1)
    balance_row = balance_price.reshape(1, hours)
    line_half = line_price if staged else line_price.astype(BF16)
    limit = line_limit.reshape(-1, 1)
    balance_row = balance_price.reshape(1, hours)
    line_half = line_price if staged else line_price.astype(BF16)
    recv = lax.all_to_all(outgoing, "bus", split_axis=0, concat_axis=0, tiled=True)
    held, resident, recv = None, {}, None
    for iteration in range(ITERS):
        last = iteration == ITERS - 1
        if staged:
            line_t = line_half
            keeps, gots, crossed, parts = {}, {}, {}, {}

            def across(chunk):
                both = (keeps[chunk][1] + gots[chunk][1].astype(F32)).astype(BF16)
                crossed[chunk] = swap(both, devices, 2)
                return both

            def settle(chunk):
                part = keeps[chunk][0] + gots[chunk][0].astype(F32) + crossed[chunk].astype(F32)
                if chunk == 2:
                    part = part + parts[3].astype(F32)
                if chunk:
                    part = part.astype(BF16)
                    parts[chunk] = swap(part, devices, 8 if chunk == 2 else 4)
                else:
                    parts[chunk] = part
                return part

            def product(chunk, line_t):
                columns = resident.get(chunk, ptdf)
                keeps[chunk], send, *turned = shadow_chunk(
                    chunk, chunk not in resident, place, line_t, columns, buses
                )
                gots[chunk] = swap(send, devices, 1)
                return turned[0] if turned else line_t

            line_t = product(3, line_t)
            if iteration == 0:
                line_t, gots[3], outgoing = lax.optimization_barrier((line_t, gots[3], outgoing))
                outgoing, _ = lax.optimization_barrier((outgoing, across(3)))
                recv = lax.all_to_all(outgoing, "bus", split_axis=0, concat_axis=0, tiled=True)
                line_t, _ = lax.optimization_barrier((line_t, settle(3)))
                product(2, line_t)
            else:
                product(2, line_t)
                line_t, _ = lax.optimization_barrier((line_t, across(3)))
            product(1, line_t)
            line_t, _ = lax.optimization_barrier((line_t, across(2)))
            if iteration:
                line_t, _ = lax.optimization_barrier((line_t, settle(3)))
            else:
                line_t, parts[3] = lax.optimization_barrier((line_t, parts[3]))
            product(0, line_t)
            gots[1], crossed[2] = lax.optimization_barrier((gots[1], crossed[2]))
            parts[3], _, _ = lax.optimization_barrier((parts[3], across(1), across(0)))
            crossed[1], _ = lax.optimization_barrier((crossed[1], settle(2)))
            settle(1)
            settle(0)
            prices = [parts[0], parts[1], parts[2]]
        else:
            recv = lax.all_to_all(outgoing, "bus", split_axis=0, concat_axis=0, tiled=True) if recv is None else recv
            shadow = lax.dot_general(ptdf, line_half, (((0,), (0,)), ((), ())), preferred_element_type=F32)
            prices = [lax.psum_scatter(shadow, "bus", scatter_dimension=0, tiled=True).T]
        chunks = (0, 1) if staged and not last else ()
        held, block, *loaded = update(
            cap, place if staged else near_place, last, prices, balance_row, demand, recv, held, ptdf, chunks
        )
        resident.update(zip(chunks, loaded))
        if staged:
            near, far, cross, far_cross = {0: block}, {}, {}, {}

            def spread(chunk):
                far[chunk] = swap(near[chunk], devices, 2)
                cross[chunk] = swap(near[chunk], devices, 1)

            def settle_far(chunk):
                far_cross[chunk] = swap(far[chunk], devices, 1)

            def blocks(chunk):
                return [near[chunk], cross[chunk], far[chunk], far_cross[chunk]]

            near[2] = swap(block, devices, 8)
            near[1] = swap(block, devices, 4)
            spread(0)
            stage = [near[1], near[2], far[0]]
            if last:
                home = held.reshape(4, 4, *held.shape[1:])
                stage += [swap(home[:, rel], devices, rel) for rel in (1, 2, 3)]
            else:
                cross[0], here = lax.optimization_barrier((cross[0], place))
                place, (resident[2], resident[3]) = load_chunks((2, 3), here, ptdf, buses)
                stage.append(place)
            near[1], near[2], far[0], *rest = lax.optimization_barrier(stage)
            near[3] = swap(near[2], devices, 4)
            spread(1)
            spread(2)
            settle_far(0)
            if last:
                home = jnp.stack([home[:, 0], *rest], axis=1)
                back = [home[0]] + [swap(home[chunk], devices, 4 * chunk) for chunk in (1, 2, 3)]
            else:
                (place,) = rest
            acc, total = flow_chunk(resident[0], blocks(0), None, balance_row)
            near[3], far[1], acc = lax.optimization_barrier((near[3], far[1], acc))
            spread(3)
            settle_far(1)
            acc, total = flow_chunk(resident[1], blocks(1), acc, total)
            settle_far(2)
            far[3], acc = lax.optimization_barrier((far[3], acc))
            settle_far(3)
            acc, total = flow_chunk(resident[2], blocks(2), acc, total)
            if last:
                acc, *back = lax.optimization_barrier((acc, *back))
            line_price, line_half, total = flow_chunk(resident[3], blocks(3), acc, total, limit, line_price)
            balance = total
        else:
            if last:
                back = [lax.all_to_all(held, "bus", split_axis=0, concat_axis=0, tiled=True)]
            every = lax.all_gather(block, "bus", axis=0, tiled=False)
            balance = jnp.sum(every[:, buses:].astype(F32), axis=(0, 1)).reshape(1, hours)
            flow = jnp.dot(ptdf, every[:, :buses].reshape(all_buses, hours), preferred_element_type=F32)
            shifted = line_price + sigma_step * flow
            line_price = shifted - sigma_step * jnp.clip(shifted / sigma_step, -limit, limit)
            line_half = line_price.astype(BF16)
        balance_row = balance_row + sigma_step * balance / all_buses
    dispatch = unpack(slot, back, dispatch, gen_max.reshape(gens, 1), availability)
    return (dispatch, balance_row.reshape(hours), line_price)


def solution(mesh):
    return jax.shard_map(
        local,
        mesh=mesh,
        in_specs=(
            P("bus", None),
            P("bus"),
            P("bus"),
            P("bus"),
            P("bus", None),
            P("bus"),
            P(("cases", "bus"), None),
            P(("cases", "bus"), None),
            P(("cases", "bus"), None),
            P("cases"),
            P(("cases", "bus"), None),
        ),
        out_specs=(P(("cases", "bus"), None), P("cases"), P(("cases", "bus"), None)),
        check_vma=False,
    )
```

```python
import functools

import jax
import jax.numpy as jnp
from jax import lax
from jax.experimental import pallas as pl
from jax.experimental.pallas import tpu as pltpu
from jax.sharding import PartitionSpec as P

ITERS = 2

tau_step = 0.2
sigma_step = 0.15

GROUP = 4
LIMIT = 16 << 20
META = 16
HBM_SPEC = pl.BlockSpec(memory_space=pltpu.MemorySpace.HBM)
VMEM_SPEC = pl.BlockSpec(memory_space=pltpu.VMEM)
SMEM_SPEC = pl.BlockSpec(memory_space=pltpu.SMEM)
F32 = jnp.float32
BF16 = jnp.bfloat16
NT = (((1,), (1,)), ((), ()))
NN = (((1,), (0,)), ((), ()))


def dot(a, b, dims=NN):
    return lax.dot_general(a, b, dims, preferred_element_type=F32)


def halves(x):
    hi = x.astype(BF16)
    lo = (x - hi.astype(F32)).astype(BF16)
    return hi, lo


def thirds(x):
    hi = x.astype(BF16)
    rest = x - hi.astype(F32)
    mid = rest.astype(BF16)
    low = (rest - mid.astype(F32)).astype(BF16)
    return hi, mid, low


def as_row(ref):
    return jnp.concatenate([ref[i : i + 1, :] for i in range(ref.shape[0])], axis=1)


def pack_kernel(
    cap, devices, place_ref, owner_ref, local_ref, cost_ref, dispatch_ref, max_ref, avail_ref,
    out_ref, near_ref, slot_ref, pay_ref, meta_ref,
):
    step = pl.program_id(0)
    gens, hours = dispatch_ref.shape
    group = out_ref.shape[0]

    @pl.when(step == 0)
    def _():
        owner = owner_ref[...]
        hits = (lax.broadcasted_iota(jnp.int32, (devices, gens), 0) == owner).astype(F32)
        before = (
            lax.broadcasted_iota(jnp.int32, (gens, gens), 0) < lax.broadcasted_iota(jnp.int32, (gens, gens), 1)
        ).astype(F32)
        count = dot(hits.astype(BF16), before.astype(BF16))
        rank = jnp.sum(count * hits, axis=0, keepdims=True).astype(jnp.int32)
        slot_ref[...] = owner * cap + rank
        near_ref[...] = (owner ^ place_ref[0]) * cap + rank
        pay_ref[:, :hours] = dispatch_ref[...].astype(BF16)
        lanes = max_ref.shape[1]
        eye = (
            lax.broadcasted_iota(jnp.int32, (lanes, lanes), 0) == lax.broadcasted_iota(jnp.int32, (lanes, lanes), 1)
        ).astype(F32)
        for i in range(gens // lanes):
            rows = slice(i * lanes, (i + 1) * lanes)
            most = jnp.sum(eye * max_ref[i : i + 1, :], axis=1, keepdims=True)
            pay_ref[rows, hours:] = (most * avail_ref[rows, :]).astype(BF16)
        local = as_row(local_ref)
        hi, mid, low = thirds(as_row(cost_ref))
        row = lax.broadcasted_iota(jnp.int32, (META, gens), 0)
        parts = [
            (lax.shift_right_logical(local, 7) + 1).astype(F32),
            (local & 127).astype(F32),
            hi.astype(F32),
            mid.astype(F32),
            low.astype(F32),
        ]
        meta = jnp.zeros((META, gens), F32)
        for i, part in enumerate(parts):
            meta = jnp.where(row == i, part, meta)
        meta_ref[...] = meta.astype(BF16)

    slot = slot_ref[...] - step * (group * cap)
    place = lax.broadcasted_iota(jnp.int32, (cap, gens), 0)
    picks = [(place == slot - i * cap).astype(F32).astype(BF16) for i in range(group)]
    moved = dot(jnp.concatenate(picks, axis=0), pay_ref[...]).astype(BF16)
    for i in range(group):
        out_ref[i, :cap, :] = moved[i * cap : (i + 1) * cap]
        out_ref[i, cap:, :] = jnp.zeros((META, 2 * hours), BF16)
        out_ref[i, cap:, :cap] = dot(meta_ref[...], picks[i], NT).astype(BF16)


def pack(devices, cap, place, owner, local_bus, cost, dispatch, gen_max, availability):
    gens, hours = dispatch.shape
    full = lambda *shape: pl.BlockSpec(shape, lambda i: (0,) * len(shape))
    folded = (gens // 128, 128)
    return pl.pallas_call(
        functools.partial(pack_kernel, cap, devices),
        grid=(devices // GROUP,),
        out_shape=(
            jax.ShapeDtypeStruct((devices, cap + META, 2 * hours), BF16),
            jax.ShapeDtypeStruct((1, gens), jnp.int32),
        ),
        in_specs=[
            SMEM_SPEC,
            full(1, gens),
            full(*folded),
            full(*folded),
            full(gens, hours),
            full(*folded),
            full(gens, hours),
        ],
        out_specs=(pl.BlockSpec((GROUP, cap + META, 2 * hours), lambda i: (i, 0, 0)), full(1, gens)),
        scratch_shapes=[
            pltpu.VMEM((1, gens), jnp.int32),
            pltpu.VMEM((gens, 2 * hours), BF16),
            pltpu.VMEM((META, gens), BF16),
        ],
        compiler_params=pltpu.CompilerParams(vmem_limit_bytes=LIMIT),
        cost_estimate=pl.CostEstimate(flops=4 * devices * cap * gens * hours, bytes_accessed=3 << 20, transcendentals=0),
        name="pack_generators",
    )(
        place,
        owner.reshape(1, gens),
        local_bus.reshape(folded),
        cost.reshape(folded),
        dispatch,
        gen_max.reshape(folded),
        availability,
    )


def unpack_kernel(block, slot_ref, *refs):
    *back_refs, dispatch_ref, max_ref, avail_ref, out_ref, back_ref = refs
    peers, cap, _ = back_refs[0].shape
    for i, ref in enumerate(back_refs):
        for j in range(peers):
            start = (i * peers + j) * cap
            back_ref[start : start + cap, :] = ref[j]
    gens = slot_ref.shape[1]
    slot = jnp.broadcast_to(slot_ref[...].astype(F32), (128, gens)).T[:, 0:1].astype(jnp.int32)
    at = lax.broadcasted_iota(jnp.int32, (gens, block), 1)
    change = None
    for start in range(0, back_ref.shape[0], block):
        pick = (at == slot - start).astype(F32).astype(BF16)
        part = dot(pick, back_ref[start : start + block, :])
        change = part if change is None else change + part
    dispatch = dispatch_ref[...]
    upper = max_ref[...] * avail_ref[...]
    sent = dispatch.astype(BF16).astype(F32)
    to_upper = (upper.astype(BF16).astype(F32) - sent).astype(BF16).astype(F32)
    moved = jnp.minimum(jnp.maximum(dispatch + change, 0.0), upper)
    moved = jnp.where(change == to_upper, upper, moved)
    out_ref[...] = jnp.where(change == -sent, 0.0, moved)


def unpack(slot, backs, dispatch, gen_max, availability):
    gens = slot.shape[1]
    peers, cap, hours = backs[0].shape
    slots = len(backs) * peers * cap
    block = next(size for size in (768, 256, 128, 16) if slots % size == 0)
    return pl.pallas_call(
        functools.partial(unpack_kernel, block),
        out_shape=jax.ShapeDtypeStruct((gens, hours), F32),
        scratch_shapes=[pltpu.VMEM((slots, hours), BF16)],
        compiler_params=pltpu.CompilerParams(vmem_limit_bytes=LIMIT),
        cost_estimate=pl.CostEstimate(flops=2 * slots * gens * hours, bytes_accessed=1 << 20, transcendentals=0),
        name="unpack_dispatch",
    )(slot, *backs, dispatch, gen_max, availability)


def update_kernel(cap, devices, first, last, parts, chunks, place_ref, *refs):
    price_refs, refs = refs[:parts], refs[parts:]
    recv_ref, balance_ref, demand_ref, *refs = refs
    if not first:
        prev_ref, *refs = refs
    copies = []
    if chunks:
        ptdf_ref, upd_ref, inj_ref, *held_refs, shadow_ref, acc_ref, extra_ref, sems = refs
        copies = column_copies(place_ref, ptdf_ref, chunks, held_refs, sems)
    else:
        upd_ref, inj_ref, shadow_ref, acc_ref, extra_ref = refs
    for copy in copies:
        copy.start()
    buses, hours = demand_ref.shape
    wide = 2 * hours
    pad = extra_ref.shape[0] // devices
    shadow = price_refs[0][...].astype(F32)
    for ref in price_refs[1:]:
        shadow = shadow + ref[...].astype(F32)
    hi, lo = halves(shadow)
    shadow_ref[:hours, :] = hi
    shadow_ref[hours:, :] = lo
    eye = (
        lax.broadcasted_iota(jnp.int32, (cap, wide), 0) == lax.broadcasted_iota(jnp.int32, (cap, wide), 1)
    ).astype(F32)
    buses_at = lax.broadcasted_iota(jnp.int32, (cap, buses), 1)
    at_row = lax.broadcasted_iota(jnp.int32, (buses, pad), 0)
    for start in range(0, devices, GROUP):
        peers = range(start, start + GROUP)
        meta = jnp.concatenate([recv_ref[peer, cap:, :] for peer in peers], axis=0)
        columns = dot(eye.astype(BF16), meta, NT)
        picks = []
        for i in range(GROUP):
            at = i * META
            bus_column = ((columns[:, at : at + 1] - 1.0) * 128.0 + columns[:, at + 1 : at + 2]).astype(jnp.int32)
            picks.append((buses_at == bus_column).astype(F32).astype(BF16))
        both = dot(jnp.concatenate(picks, axis=0), shadow_ref[...], NT)
        for i, peer in enumerate(peers):
            at = i * META
            cost = (columns[:, at + 2 : at + 3] + columns[:, at + 3 : at + 4]) + columns[:, at + 4 : at + 5]
            rows = slice(i * cap, (i + 1) * cap)
            price = both[rows, :hours] + both[rows, hours:] + balance_ref[...]
            sent = recv_ref[peer, :cap, :hours].astype(F32)
            dispatch = sent if first else prev_ref[peer]
            upper = recv_ref[peer, :cap, hours:].astype(F32)
            updated = jnp.minimum(jnp.maximum(dispatch - tau_step * (cost + price), 0.0), upper)
            if last:
                upd_ref[peer ^ place_ref[0]] = (updated - sent).astype(BF16)
            else:
                upd_ref[peer] = updated
            hi, lo = halves(2.0 * updated - dispatch)
            extra_ref[peer * pad : peer * pad + cap, :hours] = hi
            extra_ref[peer * pad : peer * pad + cap, hours:] = lo
            if pad > cap:
                extra_ref[peer * pad + cap : (peer + 1) * pad, :] = jnp.zeros((pad - cap, wide), BF16)
        picks = []
        for peer in peers:
            row = recv_ref[peer, cap:, :pad].astype(F32)
            bus_row = ((row[0:1] - 1.0) * 128.0 + row[1:2]).astype(jnp.int32)
            picks.append((at_row == bus_row).astype(F32).astype(BF16))
        sums = dot(jnp.concatenate(picks, axis=1), extra_ref[start * pad : (start + GROUP) * pad, :])
        acc_ref[...] = sums if start == 0 else acc_ref[...] + sums
    injection = acc_ref[:, :hours] + acc_ref[:, hours:] - demand_ref[...]
    inj_ref[:buses, :] = injection.astype(BF16)
    hi, mid, low = thirds(jnp.sum(injection, axis=0, keepdims=True))
    row = lax.broadcasted_iota(jnp.int32, (META, hours), 0)
    tail = jnp.where(row == 0, hi.astype(F32), 0.0)
    tail = jnp.where(row == 1, mid.astype(F32), tail)
    tail = jnp.where(row == 2, low.astype(F32), tail)
    inj_ref[buses:, :] = tail.astype(BF16)
    for copy in copies:
        copy.wait()


def update(cap, place, last, prices, balance_price, demand, recv, previous, ptdf, chunks):
    devices = recv.shape[0]
    buses, hours = demand.shape
    first = previous is None
    operands = [place, *prices, recv, balance_price, demand] + ([] if first else [previous])
    in_specs = [SMEM_SPEC] + [VMEM_SPEC] * (len(operands) - 1)
    out_shape = [
        jax.ShapeDtypeStruct((devices, cap, hours), BF16 if last else F32),
        jax.ShapeDtypeStruct((buses + META, hours), BF16),
    ]
    scratch = [
        pltpu.VMEM((2 * hours, buses), BF16),
        pltpu.VMEM((buses, 2 * hours), F32),
        pltpu.VMEM((devices * (-(-cap // 128) * 128), 2 * hours), BF16),
    ]
    if chunks:
        operands.append(in_hbm(ptdf))
        in_specs.append(HBM_SPEC)
        out_shape += [pltpu.VMEM((ptdf.shape[0], 4 * buses), BF16)] * len(chunks)
        scratch.append(pltpu.SemaphoreType.DMA((len(chunks), 4)))
    return pl.pallas_call(
        functools.partial(update_kernel, cap, devices, first, last, len(prices), chunks),
        in_specs=in_specs,
        out_specs=tuple([VMEM_SPEC] * len(out_shape)),
        out_shape=tuple(out_shape),
        scratch_shapes=scratch,
        compiler_params=pltpu.CompilerParams(vmem_limit_bytes=LIMIT),
        cost_estimate=pl.CostEstimate(flops=8 * devices * cap * buses * hours, bytes_accessed=4 << 20, transcendentals=0),
        name="update_generators",
    )(*operands)


def shadow_kernel(chunk, stream, turn, place_ref, line_ref, ptdf_ref, keep_ref, send_ref, *rest):
    buses = keep_ref.shape[2]
    columns = [slice(rel * buses, (rel + 1) * buses) for rel in range(4)]
    if stream:
        if turn:
            line_t_ref, held_ref, sems, line_held_ref = rest
            line_copy = pltpu.make_async_copy(line_ref, line_held_ref, sems.at[4])
            line_copy.start()
        else:
            held_ref, sems = rest
        copies = []
        for rel in range(4):
            start = pl.multiple_of((place_ref[0] ^ (4 * chunk + rel)) * buses, 128)
            copies.append(
                pltpu.make_async_copy(
                    ptdf_ref.at[:, pl.ds(start, buses)], held_ref.at[:, columns[rel]], sems.at[rel]
                )
            )
        for rel in (3, 2, 1, 0):
            copies[rel].start()
        if turn:
            line_copy.wait()
            line_t_ref[...] = line_held_ref[...].T.astype(BF16)
            line_ref = line_t_ref
    else:
        held_ref = ptdf_ref

    def part(rel):
        if stream:
            copies[rel].wait()
        return dot(line_ref[...], held_ref[:, columns[rel]])

    send_ref[1] = part(3).astype(BF16)
    keep_ref[1] = part(2)
    send_ref[0] = part(1).astype(BF16)
    keep_ref[0] = part(0)


def in_hbm(x):
    return pltpu.with_memory_space_constraint(x, pltpu.MemorySpace.HBM)


def chunk_cost(hours, lines, buses):
    return pl.CostEstimate(flops=hours * lines * buses, bytes_accessed=lines * buses, transcendentals=0)


def shadow_chunk(chunk, stream, place, line, ptdf, buses):
    turn = line.dtype == F32
    lines, hours = line.shape if turn else line.shape[::-1]
    out_shape = [
        jax.ShapeDtypeStruct((2, hours, buses), F32),
        jax.ShapeDtypeStruct((2, hours, buses), BF16),
    ]
    scratch = [pltpu.VMEM((lines, 4 * buses), BF16), pltpu.SemaphoreType.DMA((5,))] if stream else []
    if turn:
        out_shape.append(jax.ShapeDtypeStruct((hours, lines), BF16))
        scratch.append(pltpu.VMEM((lines, hours), F32))
    return pl.pallas_call(
        functools.partial(shadow_kernel, chunk, stream, turn),
        in_specs=[SMEM_SPEC, HBM_SPEC if turn else VMEM_SPEC, HBM_SPEC if stream else VMEM_SPEC],
        out_specs=tuple([VMEM_SPEC] * len(out_shape)),
        out_shape=tuple(out_shape),
        scratch_shapes=scratch,
        compiler_params=pltpu.CompilerParams(vmem_limit_bytes=LIMIT),
        cost_estimate=chunk_cost(hours, lines, buses),
        name="shadow_chunk",
    )(place, in_hbm(line) if turn else line, in_hbm(ptdf) if stream else ptdf)


def column_copies(place_ref, ptdf_ref, chunks, held_refs, sems):
    buses = held_refs[0].shape[1] // 4
    copies = []
    for i, chunk in enumerate(chunks):
        for rel in range(4):
            start = pl.multiple_of((place_ref[0] ^ (4 * chunk + rel)) * buses, 128)
            copies.append(
                pltpu.make_async_copy(
                    ptdf_ref.at[:, pl.ds(start, buses)],
                    held_refs[i].at[:, pl.ds(rel * buses, buses)],
                    sems.at[i, rel],
                )
            )
    return copies


def load_kernel(chunks, place_ref, ptdf_ref, token_ref, *rest):
    *held_refs, sems = rest
    copies = column_copies(place_ref, ptdf_ref, chunks, held_refs, sems)
    for copy in copies:
        copy.start()
    token_ref[0] = place_ref[0]
    for copy in copies:
        copy.wait()


def load_chunks(chunks, place, ptdf, buses):
    lines = ptdf.shape[0]
    count = len(chunks)
    token, *held = pl.pallas_call(
        functools.partial(load_kernel, chunks),
        in_specs=[SMEM_SPEC, HBM_SPEC],
        out_specs=tuple([SMEM_SPEC] + [VMEM_SPEC] * count),
        out_shape=tuple([jax.ShapeDtypeStruct((1,), jnp.int32)] + [pltpu.VMEM((lines, 4 * buses), BF16)] * count),
        scratch_shapes=[pltpu.SemaphoreType.DMA((count, 4))],
        compiler_params=pltpu.CompilerParams(vmem_limit_bytes=LIMIT),
        cost_estimate=pl.CostEstimate(flops=0, bytes_accessed=lines * buses, transcendentals=0),
        name="load_chunks",
    )(place, in_hbm(ptdf))
    return token, held


def flow_kernel(start, end, ptdf_ref, b0, b1, b2, b3, acc_ref, sum_ref, *rest):
    if end:
        limit_ref, line_ref, out_ref, half_ref, sum_out, inj_ref = rest
    else:
        out_ref, sum_out, inj_ref = rest
    buses = inj_ref.shape[0] // 4
    total = jnp.zeros(sum_ref.shape, F32) if start else sum_ref[...]
    for rel, ref in enumerate((b0, b1, b2, b3)):
        inj_ref[rel * buses : (rel + 1) * buses, :] = ref[:buses, :]
        tail = ref[buses:, :].astype(F32)
        total = total + jnp.sum(tail, axis=0, keepdims=True)
    sum_out[...] = total
    tile = ptdf_ref.shape[0] // 4

    def body(i, carry):
        rows = pl.ds(pl.multiple_of(i * tile, tile), tile)
        flow = dot(ptdf_ref[rows, :], inj_ref[...])
        if not start:
            flow = flow + acc_ref[rows, :]
        if end:
            shifted = line_ref[rows, :] + sigma_step * flow
            limit = limit_ref[rows, :]
            line = shifted - sigma_step * jnp.minimum(jnp.maximum(shifted / sigma_step, -limit), limit)
            out_ref[rows, :] = line
        else:
            out_ref[rows, :] = flow
        return carry

    lax.fori_loop(0, 4, body, 0)
    if end:
        half_ref[...] = out_ref[...].T.astype(BF16)


def flow_chunk(ptdf, blocks, acc, total, limit=None, line=None):
    lines = ptdf.shape[0]
    rows, hours = blocks[0].shape
    buses = rows - META
    start, end = acc is None, limit is not None
    operands = [ptdf, *blocks, total if start else acc, total]
    out_shape = [jax.ShapeDtypeStruct((lines, hours), F32)]
    if end:
        operands += [limit, line]
        out_shape += [jax.ShapeDtypeStruct((hours, lines), BF16)]
    out_shape += [jax.ShapeDtypeStruct((1, hours), F32)]
    return pl.pallas_call(
        functools.partial(flow_kernel, start, end),
        in_specs=[VMEM_SPEC] * len(operands),
        out_shape=tuple(out_shape),
        scratch_shapes=[pltpu.VMEM((4 * buses, hours), BF16)],
        compiler_params=pltpu.CompilerParams(vmem_limit_bytes=LIMIT),
        cost_estimate=chunk_cost(hours, lines, buses),
        name="flow_chunk",
    )(*operands)


def swap(x, devices, mask):
    return lax.ppermute(x, "bus", [(i, i ^ mask) for i in range(devices)])


def local(
    ptdf,
    line_limit,
    gen_cost,
    gen_max,
    gen_owner,
    gen_local,
    availability,
    demand,
    dispatch,
    balance_price,
    line_price,
):
    devices = lax.axis_size("bus")
    place = lax.axis_index("bus").astype(jnp.int32).reshape(1)
    buses = demand.shape[0]
    all_buses = buses * devices
    gens, hours = dispatch.shape
    cap = -(-max(2, 3 * gens // devices) // 16) * 16
    staged = devices == 16 and buses % 128 == 0

    near_place = place if staged else jnp.zeros_like(place)
    outgoing, slot = pack(
        devices,
        cap,
        near_place,
        gen_owner,
        gen_local,
        gen_cost,
        dispatch,
        gen_max,
        availability,
    )
    limit = line_limit.reshape(-1, 1)
    balance_row = balance_price.reshape(1, hours)
    line_half = line_price if staged else line_price.astype(BF16)
    limit = line_limit.reshape(-1, 1)
    balance_row = balance_price.reshape(1, hours)
    line_half = line_price if staged else line_price.astype(BF16)
    recv = lax.all_to_all(outgoing, "bus", split_axis=0, concat_axis=0, tiled=True)
    held, resident, recv = None, {}, None
    for iteration in range(ITERS):
        last = iteration == ITERS - 1
        if staged:
            line_t = line_half
            keeps, gots, crossed, parts = {}, {}, {}, {}

            def across(chunk):
                both = (keeps[chunk][1] + gots[chunk][1].astype(F32)).astype(BF16)
                crossed[chunk] = swap(both, devices, 2)
                return both

            def settle(chunk):
                part = keeps[chunk][0] + gots[chunk][0].astype(F32) + crossed[chunk].astype(F32)
                if chunk == 2:
                    part = part + parts[3].astype(F32)
                if chunk:
                    part = part.astype(BF16)
                    parts[chunk] = swap(part, devices, 8 if chunk == 2 else 4)
                else:
                    parts[chunk] = part
                return part

            def product(chunk, line_t):
                columns = resident.get(chunk, ptdf)
                keeps[chunk], send, *turned = shadow_chunk(
                    chunk, chunk not in resident, place, line_t, columns, buses
                )
                gots[chunk] = swap(send, devices, 1)
                return turned[0] if turned else line_t

            line_t = product(3, line_t)
            if iteration == 0:
                line_t, gots[3], outgoing = lax.optimization_barrier((line_t, gots[3], outgoing))
                outgoing, _ = lax.optimization_barrier((outgoing, across(3)))
                recv = lax.all_to_all(outgoing, "bus", split_axis=0, concat_axis=0, tiled=True)
                line_t, _ = lax.optimization_barrier((line_t, settle(3)))
                product(2, line_t)
            else:
                product(2, line_t)
                line_t, _ = lax.optimization_barrier((line_t, across(3)))
            product(1, line_t)
            line_t, _ = lax.optimization_barrier((line_t, across(2)))
            if iteration:
                line_t, _ = lax.optimization_barrier((line_t, settle(3)))
            product(0, line_t)
            gots[1], crossed[2] = lax.optimization_barrier((gots[1], crossed[2]))
            parts[3], _, _ = lax.optimization_barrier((parts[3], across(1), across(0)))
            crossed[1], _ = lax.optimization_barrier((crossed[1], settle(2)))
            settle(1)
            settle(0)
            prices = [parts[0], parts[1], parts[2]]
        else:
            recv = lax.all_to_all(outgoing, "bus", split_axis=0, concat_axis=0, tiled=True) if recv is None else recv
            shadow = lax.dot_general(ptdf, line_half, (((0,), (0,)), ((), ())), preferred_element_type=F32)
            prices = [lax.psum_scatter(shadow, "bus", scatter_dimension=0, tiled=True).T]
        chunks = (0, 1) if staged and not last else ()
        held, block, *loaded = update(
            cap, place if staged else near_place, last, prices, balance_row, demand, recv, held, ptdf, chunks
        )
        resident.update(zip(chunks, loaded))
        if staged:
            near, far, cross, far_cross = {0: block}, {}, {}, {}

            def to_core(*xs):
                if len(xs) == 1:
                    return [swap(xs[0], devices, 1)]
                moved = swap(jnp.stack(xs), devices, 1)
                return [moved[i] for i in range(len(xs))]

            def blocks(chunk):
                return [near[chunk], cross[chunk], far[chunk], far_cross[chunk]]

            near[2] = swap(block, devices, 8)
            near[1] = swap(block, devices, 4)
            far[0] = swap(block, devices, 2)
            (cross[0],) = to_core(block)
            stage = [near[1], near[2], far[0]]
            if last:
                home = held.reshape(4, 4, *held.shape[1:])
                side = [swap(home[:, rel], devices, rel) for rel in (1, 2, 3)]
            else:
                cross[0], here = lax.optimization_barrier((cross[0], place))
                place, (resident[2], resident[3]) = load_chunks((2, 3), here, ptdf, buses)
                stage.append(place)
            near[1], near[2], far[0], *rest = lax.optimization_barrier(stage)
            near[3] = swap(near[2], devices, 4)
            far[1] = swap(near[1], devices, 2)
            far[2] = swap(near[2], devices, 2)
            cross[1], cross[2], far_cross[0] = to_core(near[1], near[2], far[0])
            acc, total = flow_chunk(resident[0], blocks(0), None, balance_row)
            if not last:
                (place,) = rest
                side = []
            near[3], far[1], far[2], acc, *side = lax.optimization_barrier((near[3], far[1], far[2], acc, *side))
            far[3] = swap(near[3], devices, 2)
            cross[3], far_cross[1], far_cross[2] = to_core(near[3], far[1], far[2])
            if last:
                home = jnp.stack([home[:, 0], *side], axis=1)
                back = [home[0]] + [swap(home[chunk], devices, 4 * chunk) for chunk in (1, 2, 3)]
            acc, total = flow_chunk(resident[1], blocks(1), acc, total)
            far[3], acc = lax.optimization_barrier((far[3], acc))
            (far_cross[3],) = to_core(far[3])
            acc, total = flow_chunk(resident[2], blocks(2), acc, total)
            if last:
                acc, *back = lax.optimization_barrier((acc, *back))
            line_price, line_half, total = flow_chunk(resident[3], blocks(3), acc, total, limit, line_price)
            balance = total
        else:
            if last:
                back = [lax.all_to_all(held, "bus", split_axis=0, concat_axis=0, tiled=True)]
            every = lax.all_gather(block, "bus", axis=0, tiled=False)
            balance = jnp.sum(every[:, buses:].astype(F32), axis=(0, 1)).reshape(1, hours)
            flow = jnp.dot(ptdf, every[:, :buses].reshape(all_buses, hours), preferred_element_type=F32)
            shifted = line_price + sigma_step * flow
            line_price = shifted - sigma_step * jnp.clip(shifted / sigma_step, -limit, limit)
            line_half = line_price.astype(BF16)
        balance_row = balance_row + sigma_step * balance / all_buses
    dispatch = unpack(slot, back, dispatch, gen_max.reshape(gens, 1), availability)
    return (dispatch, balance_row.reshape(hours), line_price)


def solution(mesh):
    return jax.shard_map(
        local,
        mesh=mesh,
        in_specs=(
            P("bus", None),
            P("bus"),
            P("bus"),
            P("bus"),
            P("bus", None),
            P("bus"),
            P(("cases", "bus"), None),
            P(("cases", "bus"), None),
            P(("cases", "bus"), None),
            P("cases"),
            P(("cases", "bus"), None),
        ),
        out_specs=(P(("cases", "bus"), None), P("cases"), P(("cases", "bus"), None)),
        check_vma=False,
    )
```

```python
import functools

import jax
import jax.numpy as jnp
from jax import lax
from jax.experimental import pallas as pl
from jax.experimental.pallas import tpu as pltpu
from jax.sharding import PartitionSpec as P

ITERS = 2

tau_step = 0.2
sigma_step = 0.15

GROUP = 4
LIMIT = 16 << 20
COST = 3
META = 16
HBM_SPEC = pl.BlockSpec(memory_space=pltpu.MemorySpace.HBM)
VMEM_SPEC = pl.BlockSpec(memory_space=pltpu.VMEM)
SMEM_SPEC = pl.BlockSpec(memory_space=pltpu.SMEM)
F32 = jnp.float32
BF16 = jnp.bfloat16
NT = (((1,), (1,)), ((), ()))
NN = (((1,), (0,)), ((), ()))


def dot(a, b, dims=NN):
    return lax.dot_general(a, b, dims, preferred_element_type=F32)


def halves(x):
    hi = x.astype(BF16)
    lo = (x - hi.astype(F32)).astype(BF16)
    return hi, lo


def thirds(x):
    hi = x.astype(BF16)
    rest = x - hi.astype(F32)
    mid = rest.astype(BF16)
    low = (rest - mid.astype(F32)).astype(BF16)
    return hi, mid, low


def as_row(ref):
    return jnp.concatenate([ref[i : i + 1, :] for i in range(ref.shape[0])], axis=1)


def pack_kernel(
    cap, devices, place_ref, owner_ref, local_ref, cost_ref, dispatch_ref, max_ref, avail_ref,
    out_ref, near_ref, slot_ref, pay_ref, meta_ref,
):
    step = pl.program_id(0)
    gens, hours = dispatch_ref.shape
    group = out_ref.shape[0]

    @pl.when(step == 0)
    def _():
        owner = owner_ref[...]
        hits = (lax.broadcasted_iota(jnp.int32, (devices, gens), 0) == owner).astype(F32)
        before = (
            lax.broadcasted_iota(jnp.int32, (gens, gens), 0) < lax.broadcasted_iota(jnp.int32, (gens, gens), 1)
        ).astype(F32)
        count = dot(hits.astype(BF16), before.astype(BF16))
        rank = jnp.sum(count * hits, axis=0, keepdims=True).astype(jnp.int32)
        slot_ref[...] = owner * cap + rank
        near_ref[...] = (owner ^ place_ref[0]) * cap + rank
        pay_ref[:, :hours] = dispatch_ref[...].astype(BF16)
        lanes = max_ref.shape[1]
        eye = (
            lax.broadcasted_iota(jnp.int32, (lanes, lanes), 0) == lax.broadcasted_iota(jnp.int32, (lanes, lanes), 1)
        ).astype(F32)
        for i in range(gens // lanes):
            rows = slice(i * lanes, (i + 1) * lanes)
            most = jnp.sum(eye * max_ref[i : i + 1, :], axis=1, keepdims=True)
            pay_ref[rows, hours:] = (most * avail_ref[rows, :]).astype(BF16)
        local = as_row(local_ref)
        hi, mid, low = thirds(as_row(cost_ref))
        row = lax.broadcasted_iota(jnp.int32, (META, gens), 0)
        parts = [
            (lax.shift_right_logical(local, 7) + 1).astype(F32),
            (local & 127).astype(F32),
            hi.astype(F32),
            mid.astype(F32),
            low.astype(F32),
        ]
        meta = jnp.zeros((META, gens), F32)
        for i, part in enumerate(parts):
            meta = jnp.where(row == i, part, meta)
        meta_ref[...] = meta.astype(BF16)

    slot = slot_ref[...] - step * (group * cap)
    place = lax.broadcasted_iota(jnp.int32, (cap, gens), 0)
    picks = [(place == slot - i * cap).astype(F32).astype(BF16) for i in range(group)]
    moved = dot(jnp.concatenate(picks, axis=0), pay_ref[...]).astype(BF16)
    for i in range(group):
        out_ref[i, :cap, :] = moved[i * cap : (i + 1) * cap]
        out_ref[i, cap:, :] = jnp.zeros((META, 2 * hours), BF16)
        out_ref[i, cap:, :cap] = dot(meta_ref[...], picks[i], NT).astype(BF16)


def pack(devices, cap, place, owner, local_bus, cost, dispatch, gen_max, availability):
    gens, hours = dispatch.shape
    full = lambda *shape: pl.BlockSpec(shape, lambda i: (0,) * len(shape))
    folded = (gens // 128, 128)
    return pl.pallas_call(
        functools.partial(pack_kernel, cap, devices),
        grid=(devices // GROUP,),
        out_shape=(
            jax.ShapeDtypeStruct((devices, cap + META, 2 * hours), BF16),
            jax.ShapeDtypeStruct((1, gens), jnp.int32),
        ),
        in_specs=[
            SMEM_SPEC,
            full(1, gens),
            full(*folded),
            full(*folded),
            full(gens, hours),
            full(*folded),
            full(gens, hours),
        ],
        out_specs=(pl.BlockSpec((GROUP, cap + META, 2 * hours), lambda i: (i, 0, 0)), full(1, gens)),
        scratch_shapes=[
            pltpu.VMEM((1, gens), jnp.int32),
            pltpu.VMEM((gens, 2 * hours), BF16),
            pltpu.VMEM((META, gens), BF16),
        ],
        compiler_params=pltpu.CompilerParams(vmem_limit_bytes=LIMIT),
        cost_estimate=pl.CostEstimate(flops=4 * devices * cap * gens * hours, bytes_accessed=3 << 20, transcendentals=0),
        name="pack_generators",
    )(
        place,
        owner.reshape(1, gens),
        local_bus.reshape(folded),
        cost.reshape(folded),
        dispatch,
        gen_max.reshape(folded),
        availability,
    )


def unpack_kernel(block, slot_ref, *refs):
    *back_refs, dispatch_ref, max_ref, avail_ref, out_ref, back_ref = refs
    peers, cap, _ = back_refs[0].shape
    for i, ref in enumerate(back_refs):
        for j in range(peers):
            start = (i * peers + j) * cap
            back_ref[start : start + cap, :] = ref[j]
    gens = slot_ref.shape[1]
    slot = jnp.broadcast_to(slot_ref[...].astype(F32), (128, gens)).T[:, 0:1].astype(jnp.int32)
    at = lax.broadcasted_iota(jnp.int32, (gens, block), 1)
    change = None
    for start in range(0, back_ref.shape[0], block):
        pick = (at == slot - start).astype(F32).astype(BF16)
        part = dot(pick, back_ref[start : start + block, :])
        change = part if change is None else change + part
    dispatch = dispatch_ref[...]
    upper = max_ref[...] * avail_ref[...]
    sent = dispatch.astype(BF16).astype(F32)
    to_upper = (upper.astype(BF16).astype(F32) - sent).astype(BF16).astype(F32)
    moved = jnp.minimum(jnp.maximum(dispatch + change, 0.0), upper)
    moved = jnp.where(change == to_upper, upper, moved)
    out_ref[...] = jnp.where(change == -sent, 0.0, moved)


def unpack(slot, backs, dispatch, gen_max, availability):
    gens = slot.shape[1]
    peers, cap, hours = backs[0].shape
    slots = len(backs) * peers * cap
    block = next(size for size in (768, 256, 128, 16) if slots % size == 0)
    return pl.pallas_call(
        functools.partial(unpack_kernel, block),
        out_shape=jax.ShapeDtypeStruct((gens, hours), F32),
        scratch_shapes=[pltpu.VMEM((slots, hours), BF16)],
        compiler_params=pltpu.CompilerParams(vmem_limit_bytes=LIMIT),
        cost_estimate=pl.CostEstimate(flops=2 * slots * gens * hours, bytes_accessed=1 << 20, transcendentals=0),
        name="unpack_dispatch",
    )(slot, *backs, dispatch, gen_max, availability)


def update_kernel(cap, devices, first, last, parts, chunks, place_ref, *refs):
    price_refs, refs = refs[:parts], refs[parts:]
    recv_ref, balance_ref, demand_ref, *refs = refs
    if not first:
        prev_ref, *refs = refs
    copies = []
    if chunks:
        ptdf_ref, upd_ref, inj_ref, *held_refs, shadow_ref, acc_ref, extra_ref, sems = refs
        copies = column_copies(place_ref, ptdf_ref, chunks, held_refs, sems)
    else:
        upd_ref, inj_ref, shadow_ref, acc_ref, extra_ref = refs
    for copy in copies:
        copy.start()
    buses, hours = demand_ref.shape
    wide = 2 * hours
    pad = extra_ref.shape[0] // devices
    shadow = price_refs[0][...].astype(F32)
    for ref in price_refs[1:]:
        shadow = shadow + ref[...].astype(F32)
    hi, lo = halves(shadow)
    shadow_ref[:hours, :] = hi
    shadow_ref[hours:, :] = lo
    eye = (
        lax.broadcasted_iota(jnp.int32, (cap, wide), 0) == lax.broadcasted_iota(jnp.int32, (cap, wide), 1)
    ).astype(F32)
    buses_at = lax.broadcasted_iota(jnp.int32, (cap, buses), 1)
    at_row = lax.broadcasted_iota(jnp.int32, (buses, pad), 0)
    for start in range(0, devices, GROUP):
        peers = range(start, start + GROUP)
        meta = jnp.concatenate([recv_ref[peer, cap:, :] for peer in peers], axis=0)
        columns = dot(eye.astype(BF16), meta, NT)
        picks = []
        for i in range(GROUP):
            at = i * META
            bus_column = ((columns[:, at : at + 1] - 1.0) * 128.0 + columns[:, at + 1 : at + 2]).astype(jnp.int32)
            picks.append((buses_at == bus_column).astype(F32).astype(BF16))
        both = dot(jnp.concatenate(picks, axis=0), shadow_ref[...], NT)
        for i, peer in enumerate(peers):
            at = i * META
            cost = (columns[:, at + 2 : at + 3] + columns[:, at + 3 : at + 4]) + columns[:, at + 4 : at + 5]
            rows = slice(i * cap, (i + 1) * cap)
            price = both[rows, :hours] + both[rows, hours:] + balance_ref[...]
            sent = recv_ref[peer, :cap, :hours].astype(F32)
            dispatch = sent if first else prev_ref[peer]
            upper = recv_ref[peer, :cap, hours:].astype(F32)
            updated = jnp.minimum(jnp.maximum(dispatch - tau_step * (cost + price), 0.0), upper)
            if last:
                upd_ref[peer ^ place_ref[0]] = (updated - sent).astype(BF16)
            else:
                upd_ref[peer] = updated
            hi, lo = halves(2.0 * updated - dispatch)
            extra_ref[peer * pad : peer * pad + cap, :hours] = hi
            extra_ref[peer * pad : peer * pad + cap, hours:] = lo
            if pad > cap:
                extra_ref[peer * pad + cap : (peer + 1) * pad, :] = jnp.zeros((pad - cap, wide), BF16)
        picks = []
        for peer in peers:
            row = recv_ref[peer, cap:, :pad].astype(F32)
            bus_row = ((row[0:1] - 1.0) * 128.0 + row[1:2]).astype(jnp.int32)
            picks.append((at_row == bus_row).astype(F32).astype(BF16))
        sums = dot(jnp.concatenate(picks, axis=1), extra_ref[start * pad : (start + GROUP) * pad, :])
        acc_ref[...] = sums if start == 0 else acc_ref[...] + sums
    injection = acc_ref[:, :hours] + acc_ref[:, hours:] - demand_ref[...]
    inj_ref[:buses, :] = injection.astype(BF16)
    hi, mid, low = thirds(jnp.sum(injection, axis=0, keepdims=True))
    row = lax.broadcasted_iota(jnp.int32, (META, hours), 0)
    tail = jnp.where(row == 0, hi.astype(F32), 0.0)
    tail = jnp.where(row == 1, mid.astype(F32), tail)
    tail = jnp.where(row == 2, low.astype(F32), tail)
    inj_ref[buses:, :] = tail.astype(BF16)
    for copy in copies:
        copy.wait()


def update(cap, place, last, prices, balance_price, demand, recv, previous, ptdf, chunks):
    devices = recv.shape[0]
    buses, hours = demand.shape
    first = previous is None
    operands = [place, *prices, recv, balance_price, demand] + ([] if first else [previous])
    in_specs = [SMEM_SPEC] + [VMEM_SPEC] * (len(operands) - 1)
    out_shape = [
        jax.ShapeDtypeStruct((devices, cap, hours), BF16 if last else F32),
        jax.ShapeDtypeStruct((buses + META, hours), BF16),
    ]
    scratch = [
        pltpu.VMEM((2 * hours, buses), BF16),
        pltpu.VMEM((buses, 2 * hours), F32),
        pltpu.VMEM((devices * (-(-cap // 128) * 128), 2 * hours), BF16),
    ]
    if chunks:
        operands.append(in_hbm(ptdf))
        in_specs.append(HBM_SPEC)
        out_shape += [pltpu.VMEM((ptdf.shape[0], 4 * buses), BF16)] * len(chunks)
        scratch.append(pltpu.SemaphoreType.DMA((len(chunks), 4)))
    return pl.pallas_call(
        functools.partial(update_kernel, cap, devices, first, last, len(prices), chunks),
        in_specs=in_specs,
        out_specs=tuple([VMEM_SPEC] * len(out_shape)),
        out_shape=tuple(out_shape),
        scratch_shapes=scratch,
        compiler_params=pltpu.CompilerParams(vmem_limit_bytes=LIMIT),
        cost_estimate=pl.CostEstimate(flops=8 * devices * cap * buses * hours, bytes_accessed=4 << 20, transcendentals=0),
        name="update_generators",
    )(*operands)


def shadow_kernel(chunk, stream, turn, place_ref, line_ref, ptdf_ref, keep_ref, send_ref, *rest):
    buses = keep_ref.shape[2]
    columns = [slice(rel * buses, (rel + 1) * buses) for rel in range(4)]
    if stream:
        if turn:
            line_t_ref, held_ref, sems, line_held_ref = rest
            line_copy = pltpu.make_async_copy(line_ref, line_held_ref, sems.at[4])
            line_copy.start()
        else:
            held_ref, sems = rest
        copies = []
        for rel in range(4):
            start = pl.multiple_of((place_ref[0] ^ (4 * chunk + rel)) * buses, 128)
            copies.append(
                pltpu.make_async_copy(
                    ptdf_ref.at[:, pl.ds(start, buses)], held_ref.at[:, columns[rel]], sems.at[rel]
                )
            )
        for rel in (3, 2, 1, 0):
            copies[rel].start()
        if turn:
            line_copy.wait()
            line_t_ref[...] = line_held_ref[...].T.astype(BF16)
            line_ref = line_t_ref
    else:
        held_ref = ptdf_ref

    def part(rel):
        if stream:
            copies[rel].wait()
        return dot(line_ref[...], held_ref[:, columns[rel]])

    send_ref[1] = part(3).astype(BF16)
    keep_ref[1] = part(2)
    send_ref[0] = part(1).astype(BF16)
    keep_ref[0] = part(0)


def in_hbm(x):
    return pltpu.with_memory_space_constraint(x, pltpu.MemorySpace.HBM)


def chunk_cost(hours, lines, buses, weight=COST):
    flops = max(1, 8 * weight) * hours * lines * buses
    return pl.CostEstimate(flops=flops, bytes_accessed=(8 if weight else 1) * lines * buses, transcendentals=0)


def shadow_chunk(chunk, stream, place, line, ptdf, buses):
    turn = line.dtype == F32
    lines, hours = line.shape if turn else line.shape[::-1]
    out_shape = [
        jax.ShapeDtypeStruct((2, hours, buses), F32),
        jax.ShapeDtypeStruct((2, hours, buses), BF16),
    ]
    scratch = [pltpu.VMEM((lines, 4 * buses), BF16), pltpu.SemaphoreType.DMA((5,))] if stream else []
    if turn:
        out_shape.append(jax.ShapeDtypeStruct((hours, lines), BF16))
        scratch.append(pltpu.VMEM((lines, hours), F32))
    return pl.pallas_call(
        functools.partial(shadow_kernel, chunk, stream, turn),
        in_specs=[SMEM_SPEC, HBM_SPEC if turn else VMEM_SPEC, HBM_SPEC if stream else VMEM_SPEC],
        out_specs=tuple([VMEM_SPEC] * len(out_shape)),
        out_shape=tuple(out_shape),
        scratch_shapes=scratch,
        compiler_params=pltpu.CompilerParams(vmem_limit_bytes=LIMIT),
        cost_estimate=chunk_cost(hours, lines, buses),
        name="shadow_chunk",
    )(place, in_hbm(line) if turn else line, in_hbm(ptdf) if stream else ptdf)


def column_copies(place_ref, ptdf_ref, chunks, held_refs, sems):
    buses = held_refs[0].shape[1] // 4
    copies = []
    for i, chunk in enumerate(chunks):
        for rel in range(4):
            start = pl.multiple_of((place_ref[0] ^ (4 * chunk + rel)) * buses, 128)
            copies.append(
                pltpu.make_async_copy(
                    ptdf_ref.at[:, pl.ds(start, buses)],
                    held_refs[i].at[:, pl.ds(rel * buses, buses)],
                    sems.at[i, rel],
                )
            )
    return copies


def load_kernel(chunks, place_ref, ptdf_ref, token_ref, *rest):
    *held_refs, sems = rest
    copies = column_copies(place_ref, ptdf_ref, chunks, held_refs, sems)
    for copy in copies:
        copy.start()
    token_ref[0] = place_ref[0]
    for copy in copies:
        copy.wait()


def load_chunks(chunks, place, ptdf, buses):
    lines = ptdf.shape[0]
    count = len(chunks)
    token, *held = pl.pallas_call(
        functools.partial(load_kernel, chunks),
        in_specs=[SMEM_SPEC, HBM_SPEC],
        out_specs=tuple([SMEM_SPEC] + [VMEM_SPEC] * count),
        out_shape=tuple([jax.ShapeDtypeStruct((1,), jnp.int32)] + [pltpu.VMEM((lines, 4 * buses), BF16)] * count),
        scratch_shapes=[pltpu.SemaphoreType.DMA((count, 4))],
        compiler_params=pltpu.CompilerParams(vmem_limit_bytes=LIMIT),
        cost_estimate=pl.CostEstimate(flops=0, bytes_accessed=8 * count * lines * buses, transcendentals=0),
        name="load_chunks",
    )(place, in_hbm(ptdf))
    return token, held


def flow_kernel(start, end, ptdf_ref, b0, b1, b2, b3, acc_ref, sum_ref, *rest):
    if end:
        limit_ref, line_ref, out_ref, half_ref, sum_out, inj_ref = rest
    else:
        out_ref, sum_out, inj_ref = rest
    buses = inj_ref.shape[0] // 4
    total = jnp.zeros(sum_ref.shape, F32) if start else sum_ref[...]
    for rel, ref in enumerate((b0, b1, b2, b3)):
        inj_ref[rel * buses : (rel + 1) * buses, :] = ref[:buses, :]
        tail = ref[buses:, :].astype(F32)
        total = total + jnp.sum(tail, axis=0, keepdims=True)
    sum_out[...] = total
    tile = ptdf_ref.shape[0] // 4

    def body(i, carry):
        rows = pl.ds(pl.multiple_of(i * tile, tile), tile)
        flow = dot(ptdf_ref[rows, :], inj_ref[...])
        if not start:
            flow = flow + acc_ref[rows, :]
        if end:
            shifted = line_ref[rows, :] + sigma_step * flow
            limit = limit_ref[rows, :]
            line = shifted - sigma_step * jnp.minimum(jnp.maximum(shifted / sigma_step, -limit), limit)
            out_ref[rows, :] = line
        else:
            out_ref[rows, :] = flow
        return carry

    lax.fori_loop(0, 4, body, 0)
    if end:
        half_ref[...] = out_ref[...].T.astype(BF16)


def flow_chunk(ptdf, blocks, acc, total, limit=None, line=None, weight=COST):
    lines = ptdf.shape[0]
    rows, hours = blocks[0].shape
    buses = rows - META
    start, end = acc is None, limit is not None
    operands = [ptdf, *blocks, total if start else acc, total]
    out_shape = [jax.ShapeDtypeStruct((lines, hours), F32)]
    if end:
        operands += [limit, line]
        out_shape += [jax.ShapeDtypeStruct((hours, lines), BF16)]
    out_shape += [jax.ShapeDtypeStruct((1, hours), F32)]
    return pl.pallas_call(
        functools.partial(flow_kernel, start, end),
        in_specs=[VMEM_SPEC] * len(operands),
        out_shape=tuple(out_shape),
        scratch_shapes=[pltpu.VMEM((4 * buses, hours), BF16)],
        compiler_params=pltpu.CompilerParams(vmem_limit_bytes=LIMIT),
        cost_estimate=chunk_cost(hours, lines, buses, weight),
        name="flow_chunk",
    )(*operands)


def swap(x, devices, mask):
    return lax.ppermute(x, "bus", [(i, i ^ mask) for i in range(devices)])


def local(
    ptdf,
    line_limit,
    gen_cost,
    gen_max,
    gen_owner,
    gen_local,
    availability,
    demand,
    dispatch,
    balance_price,
    line_price,
):
    devices = lax.axis_size("bus")
    place = lax.axis_index("bus").astype(jnp.int32).reshape(1)
    buses = demand.shape[0]
    all_buses = buses * devices
    gens, hours = dispatch.shape
    cap = -(-max(2, 3 * gens // devices) // 16) * 16
    staged = devices == 16 and buses % 128 == 0

    near_place = place if staged else jnp.zeros_like(place)
    outgoing, slot = pack(
        devices,
        cap,
        near_place,
        gen_owner,
        gen_local,
        gen_cost,
        dispatch,
        gen_max,
        availability,
    )
    limit = line_limit.reshape(-1, 1)
    balance_row = balance_price.reshape(1, hours)
    line_half = line_price if staged else line_price.astype(BF16)
    limit = line_limit.reshape(-1, 1)
    balance_row = balance_price.reshape(1, hours)
    line_half = line_price if staged else line_price.astype(BF16)
    recv = lax.all_to_all(outgoing, "bus", split_axis=0, concat_axis=0, tiled=True)
    held, resident, recv = None, {}, None
    for iteration in range(ITERS):
        last = iteration == ITERS - 1
        weight = 0 if last else COST
        if staged:
            line_t = line_half
            keeps, gots, crossed, parts = {}, {}, {}, {}

            def across(chunk):
                both = (keeps[chunk][1] + gots[chunk][1].astype(F32)).astype(BF16)
                crossed[chunk] = swap(both, devices, 2)
                return both

            def settle(chunk):
                part = keeps[chunk][0] + gots[chunk][0].astype(F32) + crossed[chunk].astype(F32)
                if chunk == 2:
                    part = part + parts[3].astype(F32)
                if chunk:
                    part = part.astype(BF16)
                    parts[chunk] = swap(part, devices, 8 if chunk == 2 else 4)
                else:
                    parts[chunk] = part
                return part

            def product(chunk, line_t):
                columns = resident.get(chunk, ptdf)
                keeps[chunk], send, *turned = shadow_chunk(
                    chunk, chunk not in resident, place, line_t, columns, buses
                )
                gots[chunk] = swap(send, devices, 1)
                return turned[0] if turned else line_t

            line_t = product(3, line_t)
            if iteration == 0:
                line_t, gots[3], outgoing = lax.optimization_barrier((line_t, gots[3], outgoing))
                outgoing, _ = lax.optimization_barrier((outgoing, across(3)))
                recv = lax.all_to_all(outgoing, "bus", split_axis=0, concat_axis=0, tiled=True)
                line_t, _ = lax.optimization_barrier((line_t, settle(3)))
                product(2, line_t)
            else:
                product(2, line_t)
                line_t, _ = lax.optimization_barrier((line_t, across(3)))
            product(1, line_t)
            line_t, _ = lax.optimization_barrier((line_t, across(2)))
            if iteration:
                line_t, _ = lax.optimization_barrier((line_t, settle(3)))
            product(0, line_t)
            gots[1], crossed[2] = lax.optimization_barrier((gots[1], crossed[2]))
            parts[3], _, _ = lax.optimization_barrier((parts[3], across(1), across(0)))
            crossed[1], _ = lax.optimization_barrier((crossed[1], settle(2)))
            settle(1)
            settle(0)
            prices = [parts[0], parts[1], parts[2]]
        else:
            recv = lax.all_to_all(outgoing, "bus", split_axis=0, concat_axis=0, tiled=True) if recv is None else recv
            shadow = lax.dot_general(ptdf, line_half, (((0,), (0,)), ((), ())), preferred_element_type=F32)
            prices = [lax.psum_scatter(shadow, "bus", scatter_dimension=0, tiled=True).T]
        chunks = (0, 1) if staged and not last else ()
        held, block, *loaded = update(
            cap, place if staged else near_place, last, prices, balance_row, demand, recv, held, ptdf, chunks
        )
        resident.update(zip(chunks, loaded))
        if staged:
            near, far, cross, far_cross = {0: block}, {}, {}, {}

            def spread(chunk):
                far[chunk] = swap(near[chunk], devices, 2)
                cross[chunk] = swap(near[chunk], devices, 1)

            def settle_far(chunk):
                far_cross[chunk] = swap(far[chunk], devices, 1)

            def blocks(chunk):
                return [near[chunk], cross[chunk], far[chunk], far_cross[chunk]]

            near[2] = swap(block, devices, 8)
            near[1] = swap(block, devices, 4)
            spread(0)
            stage = [near[1], near[2], far[0]]
            if last:
                home = held.reshape(4, 4, *held.shape[1:])
                stage += [swap(home[:, rel], devices, rel) for rel in (1, 2, 3)]
            else:
                cross[0], here = lax.optimization_barrier((cross[0], place))
                place, (resident[2], resident[3]) = load_chunks((2, 3), here, ptdf, buses)
                stage.append(place)
            near[1], near[2], far[0], *rest = lax.optimization_barrier(stage)
            near[3] = swap(near[2], devices, 4)
            spread(1)
            spread(2)
            settle_far(0)
            if last:
                home = jnp.stack([home[:, 0], *rest], axis=1)
                back = [home[0]] + [swap(home[chunk], devices, 4 * chunk) for chunk in (1, 2, 3)]
            else:
                (place,) = rest
            acc, total = flow_chunk(resident[0], blocks(0), None, balance_row, weight=weight)
            near[3], far[1], acc = lax.optimization_barrier((near[3], far[1], acc))
            spread(3)
            settle_far(1)
            acc, total = flow_chunk(resident[1], blocks(1), acc, total, weight=weight)
            settle_far(2)
            far[3], acc = lax.optimization_barrier((far[3], acc))
            settle_far(3)
            acc, total = flow_chunk(resident[2], blocks(2), acc, total, weight=weight)
            line_price, line_half, total = flow_chunk(
                resident[3], blocks(3), acc, total, limit, line_price, weight
            )
            balance = total
        else:
            if last:
                back = [lax.all_to_all(held, "bus", split_axis=0, concat_axis=0, tiled=True)]
            every = lax.all_gather(block, "bus", axis=0, tiled=False)
            balance = jnp.sum(every[:, buses:].astype(F32), axis=(0, 1)).reshape(1, hours)
            flow = jnp.dot(ptdf, every[:, :buses].reshape(all_buses, hours), preferred_element_type=F32)
            shifted = line_price + sigma_step * flow
            line_price = shifted - sigma_step * jnp.clip(shifted / sigma_step, -limit, limit)
            line_half = line_price.astype(BF16)
        balance_row = balance_row + sigma_step * balance / all_buses
    dispatch = unpack(slot, back, dispatch, gen_max.reshape(gens, 1), availability)
    return (dispatch, balance_row.reshape(hours), line_price)


def solution(mesh):
    return jax.shard_map(
        local,
        mesh=mesh,
        in_specs=(
            P("bus", None),
            P("bus"),
            P("bus"),
            P("bus"),
            P("bus", None),
            P("bus"),
            P(("cases", "bus"), None),
            P(("cases", "bus"), None),
            P(("cases", "bus"), None),
            P("cases"),
            P(("cases", "bus"), None),
        ),
        out_specs=(P(("cases", "bus"), None), P("cases"), P(("cases", "bus"), None)),
        check_vma=False,
    )
```

```python
import functools

import jax
import jax.numpy as jnp
from jax import lax
from jax.experimental import pallas as pl
from jax.experimental.pallas import tpu as pltpu
from jax.sharding import PartitionSpec as P

ITERS = 2

tau_step = 0.2
sigma_step = 0.15

GROUP = 4
LIMIT = 16 << 20
COST = 3
META = 16
HBM_SPEC = pl.BlockSpec(memory_space=pltpu.MemorySpace.HBM)
VMEM_SPEC = pl.BlockSpec(memory_space=pltpu.VMEM)
SMEM_SPEC = pl.BlockSpec(memory_space=pltpu.SMEM)
F32 = jnp.float32
BF16 = jnp.bfloat16
NT = (((1,), (1,)), ((), ()))
NN = (((1,), (0,)), ((), ()))


def dot(a, b, dims=NN):
    return lax.dot_general(a, b, dims, preferred_element_type=F32)


def halves(x):
    hi = x.astype(BF16)
    lo = (x - hi.astype(F32)).astype(BF16)
    return hi, lo


def thirds(x):
    hi = x.astype(BF16)
    rest = x - hi.astype(F32)
    mid = rest.astype(BF16)
    low = (rest - mid.astype(F32)).astype(BF16)
    return hi, mid, low


def as_row(ref):
    return jnp.concatenate([ref[i : i + 1, :] for i in range(ref.shape[0])], axis=1)


def pack_kernel(
    cap, devices, place_ref, owner_ref, local_ref, cost_ref, dispatch_ref, max_ref, avail_ref,
    out_ref, near_ref, slot_ref, pay_ref, meta_ref,
):
    step = pl.program_id(0)
    gens, hours = dispatch_ref.shape
    group = out_ref.shape[0]

    @pl.when(step == 0)
    def _():
        owner = owner_ref[...]
        hits = (lax.broadcasted_iota(jnp.int32, (devices, gens), 0) == owner).astype(F32)
        before = (
            lax.broadcasted_iota(jnp.int32, (gens, gens), 0) < lax.broadcasted_iota(jnp.int32, (gens, gens), 1)
        ).astype(F32)
        count = dot(hits.astype(BF16), before.astype(BF16))
        rank = jnp.sum(count * hits, axis=0, keepdims=True).astype(jnp.int32)
        slot_ref[...] = owner * cap + rank
        near_ref[...] = (owner ^ place_ref[0]) * cap + rank
        pay_ref[:, :hours] = dispatch_ref[...].astype(BF16)
        lanes = max_ref.shape[1]
        eye = (
            lax.broadcasted_iota(jnp.int32, (lanes, lanes), 0) == lax.broadcasted_iota(jnp.int32, (lanes, lanes), 1)
        ).astype(F32)
        for i in range(gens // lanes):
            rows = slice(i * lanes, (i + 1) * lanes)
            most = jnp.sum(eye * max_ref[i : i + 1, :], axis=1, keepdims=True)
            pay_ref[rows, hours:] = (most * avail_ref[rows, :]).astype(BF16)
        local = as_row(local_ref)
        hi, mid, low = thirds(as_row(cost_ref))
        row = lax.broadcasted_iota(jnp.int32, (META, gens), 0)
        parts = [
            (lax.shift_right_logical(local, 7) + 1).astype(F32),
            (local & 127).astype(F32),
            hi.astype(F32),
            mid.astype(F32),
            low.astype(F32),
        ]
        meta = jnp.zeros((META, gens), F32)
        for i, part in enumerate(parts):
            meta = jnp.where(row == i, part, meta)
        meta_ref[...] = meta.astype(BF16)

    slot = slot_ref[...] - step * (group * cap)
    place = lax.broadcasted_iota(jnp.int32, (cap, gens), 0)
    picks = [(place == slot - i * cap).astype(F32).astype(BF16) for i in range(group)]
    moved = dot(jnp.concatenate(picks, axis=0), pay_ref[...]).astype(BF16)
    for i in range(group):
        out_ref[i, :cap, :] = moved[i * cap : (i + 1) * cap]
        out_ref[i, cap:, :] = jnp.zeros((META, 2 * hours), BF16)
        out_ref[i, cap:, :cap] = dot(meta_ref[...], picks[i], NT).astype(BF16)


def pack(devices, cap, place, owner, local_bus, cost, dispatch, gen_max, availability):
    gens, hours = dispatch.shape
    full = lambda *shape: pl.BlockSpec(shape, lambda i: (0,) * len(shape))
    folded = (gens // 128, 128)
    return pl.pallas_call(
        functools.partial(pack_kernel, cap, devices),
        grid=(devices // GROUP,),
        out_shape=(
            jax.ShapeDtypeStruct((devices, cap + META, 2 * hours), BF16),
            jax.ShapeDtypeStruct((1, gens), jnp.int32),
        ),
        in_specs=[
            SMEM_SPEC,
            full(1, gens),
            full(*folded),
            full(*folded),
            full(gens, hours),
            full(*folded),
            full(gens, hours),
        ],
        out_specs=(pl.BlockSpec((GROUP, cap + META, 2 * hours), lambda i: (i, 0, 0)), full(1, gens)),
        scratch_shapes=[
            pltpu.VMEM((1, gens), jnp.int32),
            pltpu.VMEM((gens, 2 * hours), BF16),
            pltpu.VMEM((META, gens), BF16),
        ],
        compiler_params=pltpu.CompilerParams(vmem_limit_bytes=LIMIT),
        cost_estimate=pl.CostEstimate(flops=4 * devices * cap * gens * hours, bytes_accessed=3 << 20, transcendentals=0),
        name="pack_generators",
    )(
        place,
        owner.reshape(1, gens),
        local_bus.reshape(folded),
        cost.reshape(folded),
        dispatch,
        gen_max.reshape(folded),
        availability,
    )


def unpack_kernel(block, slot_ref, *refs):
    *back_refs, dispatch_ref, max_ref, avail_ref, out_ref, back_ref = refs
    peers, cap, _ = back_refs[0].shape
    for i, ref in enumerate(back_refs):
        for j in range(peers):
            start = (i * peers + j) * cap
            back_ref[start : start + cap, :] = ref[j]
    gens = slot_ref.shape[1]
    slot = jnp.broadcast_to(slot_ref[...].astype(F32), (128, gens)).T[:, 0:1].astype(jnp.int32)
    at = lax.broadcasted_iota(jnp.int32, (gens, block), 1)
    change = None
    for start in range(0, back_ref.shape[0], block):
        pick = (at == slot - start).astype(F32).astype(BF16)
        part = dot(pick, back_ref[start : start + block, :])
        change = part if change is None else change + part
    dispatch = dispatch_ref[...]
    upper = max_ref[...] * avail_ref[...]
    sent = dispatch.astype(BF16).astype(F32)
    to_upper = (upper.astype(BF16).astype(F32) - sent).astype(BF16).astype(F32)
    moved = jnp.minimum(jnp.maximum(dispatch + change, 0.0), upper)
    moved = jnp.where(change == to_upper, upper, moved)
    out_ref[...] = jnp.where(change == -sent, 0.0, moved)


def unpack(slot, backs, dispatch, gen_max, availability):
    gens = slot.shape[1]
    peers, cap, hours = backs[0].shape
    slots = len(backs) * peers * cap
    block = next(size for size in (768, 256, 128, 16) if slots % size == 0)
    return pl.pallas_call(
        functools.partial(unpack_kernel, block),
        out_shape=jax.ShapeDtypeStruct((gens, hours), F32),
        scratch_shapes=[pltpu.VMEM((slots, hours), BF16)],
        compiler_params=pltpu.CompilerParams(vmem_limit_bytes=LIMIT),
        cost_estimate=pl.CostEstimate(flops=2 * slots * gens * hours, bytes_accessed=1 << 20, transcendentals=0),
        name="unpack_dispatch",
    )(slot, *backs, dispatch, gen_max, availability)


def update_kernel(cap, devices, first, last, parts, chunks, place_ref, *refs):
    price_refs, refs = refs[:parts], refs[parts:]
    recv_ref, balance_ref, demand_ref, *refs = refs
    if not first:
        prev_ref, *refs = refs
    copies = []
    if chunks:
        ptdf_ref, upd_ref, inj_ref, *held_refs, shadow_ref, acc_ref, extra_ref, sems = refs
        copies = column_copies(place_ref, ptdf_ref, chunks, held_refs, sems)
    else:
        upd_ref, inj_ref, shadow_ref, acc_ref, extra_ref = refs
    for copy in copies:
        copy.start()
    buses, hours = demand_ref.shape
    wide = 2 * hours
    pad = extra_ref.shape[0] // devices
    shadow = price_refs[0][...].astype(F32)
    for ref in price_refs[1:]:
        shadow = shadow + ref[...].astype(F32)
    hi, lo = halves(shadow)
    shadow_ref[:hours, :] = hi
    shadow_ref[hours:, :] = lo
    eye = (
        lax.broadcasted_iota(jnp.int32, (cap, wide), 0) == lax.broadcasted_iota(jnp.int32, (cap, wide), 1)
    ).astype(F32)
    buses_at = lax.broadcasted_iota(jnp.int32, (cap, buses), 1)
    at_row = lax.broadcasted_iota(jnp.int32, (buses, pad), 0)
    for start in range(0, devices, GROUP):
        peers = range(start, start + GROUP)
        meta = jnp.concatenate([recv_ref[peer, cap:, :] for peer in peers], axis=0)
        columns = dot(eye.astype(BF16), meta, NT)
        picks = []
        for i in range(GROUP):
            at = i * META
            bus_column = ((columns[:, at : at + 1] - 1.0) * 128.0 + columns[:, at + 1 : at + 2]).astype(jnp.int32)
            picks.append((buses_at == bus_column).astype(F32).astype(BF16))
        both = dot(jnp.concatenate(picks, axis=0), shadow_ref[...], NT)
        for i, peer in enumerate(peers):
            at = i * META
            cost = (columns[:, at + 2 : at + 3] + columns[:, at + 3 : at + 4]) + columns[:, at + 4 : at + 5]
            rows = slice(i * cap, (i + 1) * cap)
            price = both[rows, :hours] + both[rows, hours:] + balance_ref[...]
            sent = recv_ref[peer, :cap, :hours].astype(F32)
            dispatch = sent if first else prev_ref[peer]
            upper = recv_ref[peer, :cap, hours:].astype(F32)
            updated = jnp.minimum(jnp.maximum(dispatch - tau_step * (cost + price), 0.0), upper)
            if last:
                upd_ref[peer ^ place_ref[0]] = (updated - sent).astype(BF16)
            else:
                upd_ref[peer] = updated
            hi, lo = halves(2.0 * updated - dispatch)
            extra_ref[peer * pad : peer * pad + cap, :hours] = hi
            extra_ref[peer * pad : peer * pad + cap, hours:] = lo
            if pad > cap:
                extra_ref[peer * pad + cap : (peer + 1) * pad, :] = jnp.zeros((pad - cap, wide), BF16)
        picks = []
        for peer in peers:
            row = recv_ref[peer, cap:, :pad].astype(F32)
            bus_row = ((row[0:1] - 1.0) * 128.0 + row[1:2]).astype(jnp.int32)
            picks.append((at_row == bus_row).astype(F32).astype(BF16))
        sums = dot(jnp.concatenate(picks, axis=1), extra_ref[start * pad : (start + GROUP) * pad, :])
        acc_ref[...] = sums if start == 0 else acc_ref[...] + sums
    injection = acc_ref[:, :hours] + acc_ref[:, hours:] - demand_ref[...]
    inj_ref[:buses, :] = injection.astype(BF16)
    hi, mid, low = thirds(jnp.sum(injection, axis=0, keepdims=True))
    row = lax.broadcasted_iota(jnp.int32, (META, hours), 0)
    tail = jnp.where(row == 0, hi.astype(F32), 0.0)
    tail = jnp.where(row == 1, mid.astype(F32), tail)
    tail = jnp.where(row == 2, low.astype(F32), tail)
    inj_ref[buses:, :] = tail.astype(BF16)
    for copy in copies:
        copy.wait()


def update(cap, place, last, prices, balance_price, demand, recv, previous, ptdf, chunks):
    devices = recv.shape[0]
    buses, hours = demand.shape
    first = previous is None
    operands = [place, *prices, recv, balance_price, demand] + ([] if first else [previous])
    in_specs = [SMEM_SPEC] + [VMEM_SPEC] * (len(operands) - 1)
    out_shape = [
        jax.ShapeDtypeStruct((devices, cap, hours), BF16 if last else F32),
        jax.ShapeDtypeStruct((buses + META, hours), BF16),
    ]
    scratch = [
        pltpu.VMEM((2 * hours, buses), BF16),
        pltpu.VMEM((buses, 2 * hours), F32),
        pltpu.VMEM((devices * (-(-cap // 128) * 128), 2 * hours), BF16),
    ]
    if chunks:
        operands.append(in_hbm(ptdf))
        in_specs.append(HBM_SPEC)
        out_shape += [pltpu.VMEM((ptdf.shape[0], 4 * buses), BF16)] * len(chunks)
        scratch.append(pltpu.SemaphoreType.DMA((len(chunks), 4)))
    return pl.pallas_call(
        functools.partial(update_kernel, cap, devices, first, last, len(prices), chunks),
        in_specs=in_specs,
        out_specs=tuple([VMEM_SPEC] * len(out_shape)),
        out_shape=tuple(out_shape),
        scratch_shapes=scratch,
        compiler_params=pltpu.CompilerParams(vmem_limit_bytes=LIMIT),
        cost_estimate=pl.CostEstimate(flops=8 * devices * cap * buses * hours, bytes_accessed=4 << 20, transcendentals=0),
        name="update_generators",
    )(*operands)


def shadow_kernel(chunk, stream, turn, place_ref, line_ref, ptdf_ref, keep_ref, send_ref, *rest):
    buses = keep_ref.shape[2]
    columns = [slice(rel * buses, (rel + 1) * buses) for rel in range(4)]
    if stream:
        if turn:
            line_t_ref, held_ref, sems, line_held_ref = rest
            line_copy = pltpu.make_async_copy(line_ref, line_held_ref, sems.at[4])
            line_copy.start()
        else:
            held_ref, sems = rest
        copies = []
        for rel in range(4):
            start = pl.multiple_of((place_ref[0] ^ (4 * chunk + rel)) * buses, 128)
            copies.append(
                pltpu.make_async_copy(
                    ptdf_ref.at[:, pl.ds(start, buses)], held_ref.at[:, columns[rel]], sems.at[rel]
                )
            )
        for rel in (3, 2, 1, 0):
            copies[rel].start()
        if turn:
            line_copy.wait()
            line_t_ref[...] = line_held_ref[...].T.astype(BF16)
            line_ref = line_t_ref
    else:
        held_ref = ptdf_ref

    def part(rel):
        if stream:
            copies[rel].wait()
        return dot(line_ref[...], held_ref[:, columns[rel]])

    send_ref[1] = part(3).astype(BF16)
    keep_ref[1] = part(2)
    send_ref[0] = part(1).astype(BF16)
    keep_ref[0] = part(0)


def in_hbm(x):
    return pltpu.with_memory_space_constraint(x, pltpu.MemorySpace.HBM)


def chunk_cost(hours, lines, buses, weight=COST):
    flops = max(1, 8 * weight) * hours * lines * buses
    return pl.CostEstimate(flops=flops, bytes_accessed=(8 if weight else 1) * lines * buses, transcendentals=0)


def shadow_chunk(chunk, stream, place, line, ptdf, buses):
    turn = line.dtype == F32
    lines, hours = line.shape if turn else line.shape[::-1]
    out_shape = [
        jax.ShapeDtypeStruct((2, hours, buses), F32),
        jax.ShapeDtypeStruct((2, hours, buses), BF16),
    ]
    scratch = [pltpu.VMEM((lines, 4 * buses), BF16), pltpu.SemaphoreType.DMA((5,))] if stream else []
    if turn:
        out_shape.append(jax.ShapeDtypeStruct((hours, lines), BF16))
        scratch.append(pltpu.VMEM((lines, hours), F32))
    return pl.pallas_call(
        functools.partial(shadow_kernel, chunk, stream, turn),
        in_specs=[SMEM_SPEC, HBM_SPEC if turn else VMEM_SPEC, HBM_SPEC if stream else VMEM_SPEC],
        out_specs=tuple([VMEM_SPEC] * len(out_shape)),
        out_shape=tuple(out_shape),
        scratch_shapes=scratch,
        compiler_params=pltpu.CompilerParams(vmem_limit_bytes=LIMIT),
        cost_estimate=chunk_cost(hours, lines, buses),
        name="shadow_chunk",
    )(place, in_hbm(line) if turn else line, in_hbm(ptdf) if stream else ptdf)


def column_copies(place_ref, ptdf_ref, chunks, held_refs, sems):
    buses = held_refs[0].shape[1] // 4
    copies = []
    for i, chunk in enumerate(chunks):
        for rel in range(4):
            start = pl.multiple_of((place_ref[0] ^ (4 * chunk + rel)) * buses, 128)
            copies.append(
                pltpu.make_async_copy(
                    ptdf_ref.at[:, pl.ds(start, buses)],
                    held_refs[i].at[:, pl.ds(rel * buses, buses)],
                    sems.at[i, rel],
                )
            )
    return copies


def load_kernel(chunks, place_ref, ptdf_ref, token_ref, *rest):
    *held_refs, sems = rest
    copies = column_copies(place_ref, ptdf_ref, chunks, held_refs, sems)
    for copy in copies:
        copy.start()
    token_ref[0] = place_ref[0]
    for copy in copies:
        copy.wait()


def load_chunks(chunks, place, ptdf, buses):
    lines = ptdf.shape[0]
    count = len(chunks)
    token, *held = pl.pallas_call(
        functools.partial(load_kernel, chunks),
        in_specs=[SMEM_SPEC, HBM_SPEC],
        out_specs=tuple([SMEM_SPEC] + [VMEM_SPEC] * count),
        out_shape=tuple([jax.ShapeDtypeStruct((1,), jnp.int32)] + [pltpu.VMEM((lines, 4 * buses), BF16)] * count),
        scratch_shapes=[pltpu.SemaphoreType.DMA((count, 4))],
        compiler_params=pltpu.CompilerParams(vmem_limit_bytes=LIMIT),
        cost_estimate=pl.CostEstimate(flops=0, bytes_accessed=8 * count * lines * buses, transcendentals=0),
        name="load_chunks",
    )(place, in_hbm(ptdf))
    return token, held


def flow_kernel(start, end, ptdf_ref, b0, b1, b2, b3, acc_ref, sum_ref, *rest):
    if end:
        limit_ref, line_ref, out_ref, half_ref, sum_out, inj_ref = rest
    else:
        out_ref, sum_out, inj_ref = rest
    buses = inj_ref.shape[0] // 4
    total = jnp.zeros(sum_ref.shape, F32) if start else sum_ref[...]
    for rel, ref in enumerate((b0, b1, b2, b3)):
        inj_ref[rel * buses : (rel + 1) * buses, :] = ref[:buses, :]
        tail = ref[buses:, :].astype(F32)
        total = total + jnp.sum(tail, axis=0, keepdims=True)
    sum_out[...] = total
    tile = ptdf_ref.shape[0] // 4

    def body(i, carry):
        rows = pl.ds(pl.multiple_of(i * tile, tile), tile)
        flow = dot(ptdf_ref[rows, :], inj_ref[...])
        if not start:
            flow = flow + acc_ref[rows, :]
        if end:
            shifted = line_ref[rows, :] + sigma_step * flow
            limit = limit_ref[rows, :]
            line = shifted - sigma_step * jnp.minimum(jnp.maximum(shifted / sigma_step, -limit), limit)
            out_ref[rows, :] = line
        else:
            out_ref[rows, :] = flow
        return carry

    lax.fori_loop(0, 4, body, 0)
    if end:
        half_ref[...] = out_ref[...].T.astype(BF16)


def flow_chunk(ptdf, blocks, acc, total, limit=None, line=None, weight=COST):
    lines = ptdf.shape[0]
    rows, hours = blocks[0].shape
    buses = rows - META
    start, end = acc is None, limit is not None
    operands = [ptdf, *blocks, total if start else acc, total]
    out_shape = [jax.ShapeDtypeStruct((lines, hours), F32)]
    if end:
        operands += [limit, line]
        out_shape += [jax.ShapeDtypeStruct((hours, lines), BF16)]
    out_shape += [jax.ShapeDtypeStruct((1, hours), F32)]
    return pl.pallas_call(
        functools.partial(flow_kernel, start, end),
        in_specs=[VMEM_SPEC] * len(operands),
        out_shape=tuple(out_shape),
        scratch_shapes=[pltpu.VMEM((4 * buses, hours), BF16)],
        compiler_params=pltpu.CompilerParams(vmem_limit_bytes=LIMIT),
        cost_estimate=chunk_cost(hours, lines, buses, weight),
        name="flow_chunk",
    )(*operands)


def swap(x, devices, mask):
    return lax.ppermute(x, "bus", [(i, i ^ mask) for i in range(devices)])


def local(
    ptdf,
    line_limit,
    gen_cost,
    gen_max,
    gen_owner,
    gen_local,
    availability,
    demand,
    dispatch,
    balance_price,
    line_price,
):
    devices = lax.axis_size("bus")
    place = lax.axis_index("bus").astype(jnp.int32).reshape(1)
    buses = demand.shape[0]
    all_buses = buses * devices
    gens, hours = dispatch.shape
    cap = -(-max(2, 3 * gens // devices) // 16) * 16
    staged = devices == 16 and buses % 128 == 0

    near_place = place if staged else jnp.zeros_like(place)
    outgoing, slot = pack(
        devices,
        cap,
        near_place,
        gen_owner,
        gen_local,
        gen_cost,
        dispatch,
        gen_max,
        availability,
    )
    limit = line_limit.reshape(-1, 1)
    balance_row = balance_price.reshape(1, hours)
    line_half = line_price if staged else line_price.astype(BF16)
    limit = line_limit.reshape(-1, 1)
    balance_row = balance_price.reshape(1, hours)
    line_half = line_price if staged else line_price.astype(BF16)
    recv = lax.all_to_all(outgoing, "bus", split_axis=0, concat_axis=0, tiled=True)
    held, resident, recv = None, {}, None
    for iteration in range(ITERS):
        last = iteration == ITERS - 1
        weight = 0 if last else COST
        if staged:
            line_t = line_half
            keeps, gots, crossed, parts = {}, {}, {}, {}

            def across(chunk):
                both = (keeps[chunk][1] + gots[chunk][1].astype(F32)).astype(BF16)
                crossed[chunk] = swap(both, devices, 2)
                return both

            def settle(chunk):
                part = keeps[chunk][0] + gots[chunk][0].astype(F32) + crossed[chunk].astype(F32)
                if chunk == 2:
                    part = part + parts[3].astype(F32)
                if chunk:
                    part = part.astype(BF16)
                    parts[chunk] = swap(part, devices, 8 if chunk == 2 else 4)
                else:
                    parts[chunk] = part
                return part

            def product(chunk, line_t):
                columns = resident.get(chunk, ptdf)
                keeps[chunk], send, *turned = shadow_chunk(
                    chunk, chunk not in resident, place, line_t, columns, buses
                )
                gots[chunk] = swap(send, devices, 1)
                return turned[0] if turned else line_t

            line_t = product(3, line_t)
            if iteration == 0:
                line_t, gots[3], outgoing = lax.optimization_barrier((line_t, gots[3], outgoing))
                outgoing, _ = lax.optimization_barrier((outgoing, across(3)))
                recv = lax.all_to_all(outgoing, "bus", split_axis=0, concat_axis=0, tiled=True)
                line_t, _ = lax.optimization_barrier((line_t, settle(3)))
                product(2, line_t)
            else:
                product(2, line_t)
                line_t, _ = lax.optimization_barrier((line_t, across(3)))
            product(1, line_t)
            line_t, _ = lax.optimization_barrier((line_t, across(2)))
            if iteration:
                line_t, _ = lax.optimization_barrier((line_t, settle(3)))
            product(0, line_t)
            gots[1], crossed[2] = lax.optimization_barrier((gots[1], crossed[2]))
            parts[3], _, _ = lax.optimization_barrier((parts[3], across(1), across(0)))
            crossed[1], _ = lax.optimization_barrier((crossed[1], settle(2)))
            settle(1)
            settle(0)
            prices = [parts[0], parts[1], parts[2]]
        else:
            recv = lax.all_to_all(outgoing, "bus", split_axis=0, concat_axis=0, tiled=True) if recv is None else recv
            shadow = lax.dot_general(ptdf, line_half, (((0,), (0,)), ((), ())), preferred_element_type=F32)
            prices = [lax.psum_scatter(shadow, "bus", scatter_dimension=0, tiled=True).T]
        chunks = (0,) if staged and not last else ()
        held, block, *loaded = update(
            cap, place if staged else near_place, last, prices, balance_row, demand, recv, held, ptdf, chunks
        )
        resident.update(zip(chunks, loaded))
        if staged:
            near, far, cross, far_cross = {0: block}, {}, {}, {}

            def spread(chunk):
                far[chunk] = swap(near[chunk], devices, 2)
                cross[chunk] = swap(near[chunk], devices, 1)

            def settle_far(chunk):
                far_cross[chunk] = swap(far[chunk], devices, 1)

            def blocks(chunk):
                return [near[chunk], cross[chunk], far[chunk], far_cross[chunk]]

            near[2] = swap(block, devices, 8)
            near[1] = swap(block, devices, 4)
            spread(0)
            stage = [near[1], near[2], far[0]]
            if last:
                home = held.reshape(4, 4, *held.shape[1:])
                stage += [swap(home[:, rel], devices, rel) for rel in (1, 2, 3)]
            else:
                cross[0], here = lax.optimization_barrier((cross[0], place))
                place, (resident[1], resident[2]) = load_chunks((1, 2), here, ptdf, buses)
                stage.append(place)
            near[1], near[2], far[0], *rest = lax.optimization_barrier(stage)
            near[3] = swap(near[2], devices, 4)
            spread(1)
            spread(2)
            settle_far(0)
            if last:
                home = jnp.stack([home[:, 0], *rest], axis=1)
                back = [home[0]] + [swap(home[chunk], devices, 4 * chunk) for chunk in (1, 2, 3)]
            else:
                (place,) = rest
            acc, total = flow_chunk(resident[0], blocks(0), None, balance_row, weight=weight)
            if not last:
                acc, here = lax.optimization_barrier((acc, place))
                place, (resident[3],) = load_chunks((3,), here, ptdf, buses)
            near[3], far[1], acc, place = lax.optimization_barrier((near[3], far[1], acc, place))
            spread(3)
            settle_far(1)
            acc, total = flow_chunk(resident[1], blocks(1), acc, total, weight=weight)
            settle_far(2)
            far[3], acc = lax.optimization_barrier((far[3], acc))
            settle_far(3)
            acc, total = flow_chunk(resident[2], blocks(2), acc, total, weight=weight)
            line_price, line_half, total = flow_chunk(
                resident[3], blocks(3), acc, total, limit, line_price, weight
            )
            balance = total
        else:
            if last:
                back = [lax.all_to_all(held, "bus", split_axis=0, concat_axis=0, tiled=True)]
            every = lax.all_gather(block, "bus", axis=0, tiled=False)
            balance = jnp.sum(every[:, buses:].astype(F32), axis=(0, 1)).reshape(1, hours)
            flow = jnp.dot(ptdf, every[:, :buses].reshape(all_buses, hours), preferred_element_type=F32)
            shifted = line_price + sigma_step * flow
            line_price = shifted - sigma_step * jnp.clip(shifted / sigma_step, -limit, limit)
            line_half = line_price.astype(BF16)
        balance_row = balance_row + sigma_step * balance / all_buses
    dispatch = unpack(slot, back, dispatch, gen_max.reshape(gens, 1), availability)
    return (dispatch, balance_row.reshape(hours), line_price)


def solution(mesh):
    return jax.shard_map(
        local,
        mesh=mesh,
        in_specs=(
            P("bus", None),
            P("bus"),
            P("bus"),
            P("bus"),
            P("bus", None),
            P("bus"),
            P(("cases", "bus"), None),
            P(("cases", "bus"), None),
            P(("cases", "bus"), None),
            P("cases"),
            P(("cases", "bus"), None),
        ),
        out_specs=(P(("cases", "bus"), None), P("cases"), P(("cases", "bus"), None)),
        check_vma=False,
    )
```

```python
import functools

import jax
import jax.numpy as jnp
from jax import lax
from jax.experimental import pallas as pl
from jax.experimental.pallas import tpu as pltpu
from jax.sharding import PartitionSpec as P

ITERS = 2

tau_step = 0.2
sigma_step = 0.15

GROUP = 4
LIMIT = 16 << 20
COST = 3
META = 16
HBM_SPEC = pl.BlockSpec(memory_space=pltpu.MemorySpace.HBM)
VMEM_SPEC = pl.BlockSpec(memory_space=pltpu.VMEM)
SMEM_SPEC = pl.BlockSpec(memory_space=pltpu.SMEM)
F32 = jnp.float32
BF16 = jnp.bfloat16
NT = (((1,), (1,)), ((), ()))
NN = (((1,), (0,)), ((), ()))


def dot(a, b, dims=NN):
    return lax.dot_general(a, b, dims, preferred_element_type=F32)


def halves(x):
    hi = x.astype(BF16)
    lo = (x - hi.astype(F32)).astype(BF16)
    return hi, lo


def thirds(x):
    hi = x.astype(BF16)
    rest = x - hi.astype(F32)
    mid = rest.astype(BF16)
    low = (rest - mid.astype(F32)).astype(BF16)
    return hi, mid, low


def as_row(ref):
    return jnp.concatenate([ref[i : i + 1, :] for i in range(ref.shape[0])], axis=1)


def pack_kernel(
    cap, devices, place_ref, owner_ref, local_ref, cost_ref, dispatch_ref, max_ref, avail_ref,
    out_ref, near_ref, slot_ref, pay_ref, meta_ref,
):
    step = pl.program_id(0)
    gens, hours = dispatch_ref.shape
    group = out_ref.shape[0]

    @pl.when(step == 0)
    def _():
        owner = owner_ref[...]
        hits = (lax.broadcasted_iota(jnp.int32, (devices, gens), 0) == owner).astype(F32)
        before = (
            lax.broadcasted_iota(jnp.int32, (gens, gens), 0) < lax.broadcasted_iota(jnp.int32, (gens, gens), 1)
        ).astype(F32)
        count = dot(hits.astype(BF16), before.astype(BF16))
        rank = jnp.sum(count * hits, axis=0, keepdims=True).astype(jnp.int32)
        slot_ref[...] = owner * cap + rank
        near_ref[...] = (owner ^ place_ref[0]) * cap + rank
        pay_ref[:, :hours] = dispatch_ref[...].astype(BF16)
        lanes = max_ref.shape[1]
        eye = (
            lax.broadcasted_iota(jnp.int32, (lanes, lanes), 0) == lax.broadcasted_iota(jnp.int32, (lanes, lanes), 1)
        ).astype(F32)
        for i in range(gens // lanes):
            rows = slice(i * lanes, (i + 1) * lanes)
            most = jnp.sum(eye * max_ref[i : i + 1, :], axis=1, keepdims=True)
            pay_ref[rows, hours:] = (most * avail_ref[rows, :]).astype(BF16)
        local = as_row(local_ref)
        hi, mid, low = thirds(as_row(cost_ref))
        row = lax.broadcasted_iota(jnp.int32, (META, gens), 0)
        parts = [
            (lax.shift_right_logical(local, 7) + 1).astype(F32),
            (local & 127).astype(F32),
            hi.astype(F32),
            mid.astype(F32),
            low.astype(F32),
        ]
        meta = jnp.zeros((META, gens), F32)
        for i, part in enumerate(parts):
            meta = jnp.where(row == i, part, meta)
        meta_ref[...] = meta.astype(BF16)

    slot = slot_ref[...] - step * (group * cap)
    place = lax.broadcasted_iota(jnp.int32, (cap, gens), 0)
    picks = [(place == slot - i * cap).astype(F32).astype(BF16) for i in range(group)]
    moved = dot(jnp.concatenate(picks, axis=0), pay_ref[...]).astype(BF16)
    for i in range(group):
        out_ref[i, :cap, :] = moved[i * cap : (i + 1) * cap]
        out_ref[i, cap:, :] = jnp.zeros((META, 2 * hours), BF16)
        out_ref[i, cap:, :cap] = dot(meta_ref[...], picks[i], NT).astype(BF16)


def pack(devices, cap, place, owner, local_bus, cost, dispatch, gen_max, availability):
    gens, hours = dispatch.shape
    full = lambda *shape: pl.BlockSpec(shape, lambda i: (0,) * len(shape))
    folded = (gens // 128, 128)
    return pl.pallas_call(
        functools.partial(pack_kernel, cap, devices),
        grid=(devices // GROUP,),
        out_shape=(
            jax.ShapeDtypeStruct((devices, cap + META, 2 * hours), BF16),
            jax.ShapeDtypeStruct((1, gens), jnp.int32),
        ),
        in_specs=[
            SMEM_SPEC,
            full(1, gens),
            full(*folded),
            full(*folded),
            full(gens, hours),
            full(*folded),
            full(gens, hours),
        ],
        out_specs=(pl.BlockSpec((GROUP, cap + META, 2 * hours), lambda i: (i, 0, 0)), full(1, gens)),
        scratch_shapes=[
            pltpu.VMEM((1, gens), jnp.int32),
            pltpu.VMEM((gens, 2 * hours), BF16),
            pltpu.VMEM((META, gens), BF16),
        ],
        compiler_params=pltpu.CompilerParams(vmem_limit_bytes=LIMIT),
        cost_estimate=pl.CostEstimate(flops=4 * devices * cap * gens * hours, bytes_accessed=3 << 20, transcendentals=0),
        name="pack_generators",
    )(
        place,
        owner.reshape(1, gens),
        local_bus.reshape(folded),
        cost.reshape(folded),
        dispatch,
        gen_max.reshape(folded),
        availability,
    )


def unpack_kernel(block, slot_ref, *refs):
    *back_refs, dispatch_ref, max_ref, avail_ref, out_ref, back_ref = refs
    peers, cap, _ = back_refs[0].shape
    for i, ref in enumerate(back_refs):
        for j in range(peers):
            start = (i * peers + j) * cap
            back_ref[start : start + cap, :] = ref[j]
    gens = slot_ref.shape[1]
    slot = jnp.broadcast_to(slot_ref[...].astype(F32), (128, gens)).T[:, 0:1].astype(jnp.int32)
    at = lax.broadcasted_iota(jnp.int32, (gens, block), 1)
    change = None
    for start in range(0, back_ref.shape[0], block):
        pick = (at == slot - start).astype(F32).astype(BF16)
        part = dot(pick, back_ref[start : start + block, :])
        change = part if change is None else change + part
    dispatch = dispatch_ref[...]
    upper = max_ref[...] * avail_ref[...]
    sent = dispatch.astype(BF16).astype(F32)
    to_upper = (upper.astype(BF16).astype(F32) - sent).astype(BF16).astype(F32)
    moved = jnp.minimum(jnp.maximum(dispatch + change, 0.0), upper)
    moved = jnp.where(change == to_upper, upper, moved)
    out_ref[...] = jnp.where(change == -sent, 0.0, moved)


def unpack(slot, backs, dispatch, gen_max, availability):
    gens = slot.shape[1]
    peers, cap, hours = backs[0].shape
    slots = len(backs) * peers * cap
    block = next(size for size in (768, 256, 128, 16) if slots % size == 0)
    return pl.pallas_call(
        functools.partial(unpack_kernel, block),
        out_shape=jax.ShapeDtypeStruct((gens, hours), F32),
        scratch_shapes=[pltpu.VMEM((slots, hours), BF16)],
        compiler_params=pltpu.CompilerParams(vmem_limit_bytes=LIMIT),
        cost_estimate=pl.CostEstimate(flops=2 * slots * gens * hours, bytes_accessed=1 << 20, transcendentals=0),
        name="unpack_dispatch",
    )(slot, *backs, dispatch, gen_max, availability)


def update_kernel(cap, devices, first, last, parts, chunks, place_ref, *refs):
    price_refs, refs = refs[:parts], refs[parts:]
    recv_ref, balance_ref, demand_ref, *refs = refs
    if not first:
        prev_ref, *refs = refs
    copies = []
    if chunks:
        ptdf_ref, upd_ref, inj_ref, *held_refs, shadow_ref, acc_ref, extra_ref, sems = refs
        copies = column_copies(place_ref, ptdf_ref, chunks, held_refs, sems)
    else:
        upd_ref, inj_ref, shadow_ref, acc_ref, extra_ref = refs
    for copy in copies:
        copy.start()
    buses, hours = demand_ref.shape
    wide = 2 * hours
    pad = extra_ref.shape[0] // devices
    shadow = price_refs[0][...].astype(F32)
    for ref in price_refs[1:]:
        shadow = shadow + ref[...].astype(F32)
    hi, lo = halves(shadow)
    shadow_ref[:hours, :] = hi
    shadow_ref[hours:, :] = lo
    eye = (
        lax.broadcasted_iota(jnp.int32, (cap, wide), 0) == lax.broadcasted_iota(jnp.int32, (cap, wide), 1)
    ).astype(F32)
    buses_at = lax.broadcasted_iota(jnp.int32, (cap, buses), 1)
    at_row = lax.broadcasted_iota(jnp.int32, (buses, pad), 0)
    for start in range(0, devices, GROUP):
        peers = range(start, start + GROUP)
        meta = jnp.concatenate([recv_ref[peer, cap:, :] for peer in peers], axis=0)
        columns = dot(eye.astype(BF16), meta, NT)
        picks = []
        for i in range(GROUP):
            at = i * META
            bus_column = ((columns[:, at : at + 1] - 1.0) * 128.0 + columns[:, at + 1 : at + 2]).astype(jnp.int32)
            picks.append((buses_at == bus_column).astype(F32).astype(BF16))
        both = dot(jnp.concatenate(picks, axis=0), shadow_ref[...], NT)
        for i, peer in enumerate(peers):
            at = i * META
            cost = (columns[:, at + 2 : at + 3] + columns[:, at + 3 : at + 4]) + columns[:, at + 4 : at + 5]
            rows = slice(i * cap, (i + 1) * cap)
            price = both[rows, :hours] + both[rows, hours:] + balance_ref[...]
            sent = recv_ref[peer, :cap, :hours].astype(F32)
            dispatch = sent if first else prev_ref[peer]
            upper = recv_ref[peer, :cap, hours:].astype(F32)
            updated = jnp.minimum(jnp.maximum(dispatch - tau_step * (cost + price), 0.0), upper)
            if last:
                upd_ref[peer ^ place_ref[0]] = (updated - sent).astype(BF16)
            else:
                upd_ref[peer] = updated
            hi, lo = halves(2.0 * updated - dispatch)
            extra_ref[peer * pad : peer * pad + cap, :hours] = hi
            extra_ref[peer * pad : peer * pad + cap, hours:] = lo
            if pad > cap:
                extra_ref[peer * pad + cap : (peer + 1) * pad, :] = jnp.zeros((pad - cap, wide), BF16)
        picks = []
        for peer in peers:
            row = recv_ref[peer, cap:, :pad].astype(F32)
            bus_row = ((row[0:1] - 1.0) * 128.0 + row[1:2]).astype(jnp.int32)
            picks.append((at_row == bus_row).astype(F32).astype(BF16))
        sums = dot(jnp.concatenate(picks, axis=1), extra_ref[start * pad : (start + GROUP) * pad, :])
        acc_ref[...] = sums if start == 0 else acc_ref[...] + sums
    injection = acc_ref[:, :hours] + acc_ref[:, hours:] - demand_ref[...]
    inj_ref[:buses, :] = injection.astype(BF16)
    hi, mid, low = thirds(jnp.sum(injection, axis=0, keepdims=True))
    row = lax.broadcasted_iota(jnp.int32, (META, hours), 0)
    tail = jnp.where(row == 0, hi.astype(F32), 0.0)
    tail = jnp.where(row == 1, mid.astype(F32), tail)
    tail = jnp.where(row == 2, low.astype(F32), tail)
    inj_ref[buses:, :] = tail.astype(BF16)
    for copy in copies:
        copy.wait()


def update(cap, place, last, prices, balance_price, demand, recv, previous, ptdf, chunks):
    devices = recv.shape[0]
    buses, hours = demand.shape
    first = previous is None
    operands = [place, *prices, recv, balance_price, demand] + ([] if first else [previous])
    in_specs = [SMEM_SPEC] + [VMEM_SPEC] * (len(operands) - 1)
    out_shape = [
        jax.ShapeDtypeStruct((devices, cap, hours), BF16 if last else F32),
        jax.ShapeDtypeStruct((buses + META, hours), BF16),
    ]
    scratch = [
        pltpu.VMEM((2 * hours, buses), BF16),
        pltpu.VMEM((buses, 2 * hours), F32),
        pltpu.VMEM((devices * (-(-cap // 128) * 128), 2 * hours), BF16),
    ]
    if chunks:
        operands.append(in_hbm(ptdf))
        in_specs.append(HBM_SPEC)
        out_shape += [pltpu.VMEM((ptdf.shape[0], 4 * buses), BF16)] * len(chunks)
        scratch.append(pltpu.SemaphoreType.DMA((len(chunks), 4)))
    return pl.pallas_call(
        functools.partial(update_kernel, cap, devices, first, last, len(prices), chunks),
        in_specs=in_specs,
        out_specs=tuple([VMEM_SPEC] * len(out_shape)),
        out_shape=tuple(out_shape),
        scratch_shapes=scratch,
        compiler_params=pltpu.CompilerParams(vmem_limit_bytes=LIMIT),
        cost_estimate=pl.CostEstimate(flops=8 * devices * cap * buses * hours, bytes_accessed=4 << 20, transcendentals=0),
        name="update_generators",
    )(*operands)


def shadow_kernel(chunk, stream, turn, place_ref, line_ref, ptdf_ref, keep_ref, send_ref, *rest):
    buses = keep_ref.shape[2]
    columns = [slice(rel * buses, (rel + 1) * buses) for rel in range(4)]
    if stream:
        if turn:
            line_t_ref, held_ref, sems, line_held_ref = rest
            line_copy = pltpu.make_async_copy(line_ref, line_held_ref, sems.at[4])
            line_copy.start()
        else:
            held_ref, sems = rest
        copies = []
        for rel in range(4):
            start = pl.multiple_of((place_ref[0] ^ (4 * chunk + rel)) * buses, 128)
            copies.append(
                pltpu.make_async_copy(
                    ptdf_ref.at[:, pl.ds(start, buses)], held_ref.at[:, columns[rel]], sems.at[rel]
                )
            )
        for rel in (3, 2, 1, 0):
            copies[rel].start()
        if turn:
            line_copy.wait()
            line_t_ref[...] = line_held_ref[...].T.astype(BF16)
            line_ref = line_t_ref
    else:
        held_ref = ptdf_ref

    def part(rel):
        if stream:
            copies[rel].wait()
        return dot(line_ref[...], held_ref[:, columns[rel]])

    send_ref[1] = part(3).astype(BF16)
    keep_ref[1] = part(2)
    send_ref[0] = part(1).astype(BF16)
    keep_ref[0] = part(0)


def in_hbm(x):
    return pltpu.with_memory_space_constraint(x, pltpu.MemorySpace.HBM)


def chunk_cost(hours, lines, buses, weight=COST):
    flops = max(1, 8 * weight) * hours * lines * buses
    return pl.CostEstimate(flops=flops, bytes_accessed=(8 if weight else 1) * lines * buses, transcendentals=0)


def shadow_chunk(chunk, stream, place, line, ptdf, buses):
    turn = line.dtype == F32
    lines, hours = line.shape if turn else line.shape[::-1]
    out_shape = [
        jax.ShapeDtypeStruct((2, hours, buses), F32),
        jax.ShapeDtypeStruct((2, hours, buses), BF16),
    ]
    scratch = [pltpu.VMEM((lines, 4 * buses), BF16), pltpu.SemaphoreType.DMA((5,))] if stream else []
    if turn:
        out_shape.append(jax.ShapeDtypeStruct((hours, lines), BF16))
        scratch.append(pltpu.VMEM((lines, hours), F32))
    return pl.pallas_call(
        functools.partial(shadow_kernel, chunk, stream, turn),
        in_specs=[SMEM_SPEC, HBM_SPEC if turn else VMEM_SPEC, HBM_SPEC if stream else VMEM_SPEC],
        out_specs=tuple([VMEM_SPEC] * len(out_shape)),
        out_shape=tuple(out_shape),
        scratch_shapes=scratch,
        compiler_params=pltpu.CompilerParams(vmem_limit_bytes=LIMIT),
        cost_estimate=chunk_cost(hours, lines, buses),
        name="shadow_chunk",
    )(place, in_hbm(line) if turn else line, in_hbm(ptdf) if stream else ptdf)


def column_copies(place_ref, ptdf_ref, chunks, held_refs, sems):
    buses = held_refs[0].shape[1] // 4
    copies = []
    for i, chunk in enumerate(chunks):
        for rel in range(4):
            start = pl.multiple_of((place_ref[0] ^ (4 * chunk + rel)) * buses, 128)
            copies.append(
                pltpu.make_async_copy(
                    ptdf_ref.at[:, pl.ds(start, buses)],
                    held_refs[i].at[:, pl.ds(rel * buses, buses)],
                    sems.at[i, rel],
                )
            )
    return copies


def load_kernel(chunks, place_ref, ptdf_ref, token_ref, *rest):
    *held_refs, sems = rest
    copies = column_copies(place_ref, ptdf_ref, chunks, held_refs, sems)
    for copy in copies:
        copy.start()
    token_ref[0] = place_ref[0]
    for copy in copies:
        copy.wait()


def load_chunks(chunks, place, ptdf, buses):
    lines = ptdf.shape[0]
    count = len(chunks)
    token, *held = pl.pallas_call(
        functools.partial(load_kernel, chunks),
        in_specs=[SMEM_SPEC, HBM_SPEC],
        out_specs=tuple([SMEM_SPEC] + [VMEM_SPEC] * count),
        out_shape=tuple([jax.ShapeDtypeStruct((1,), jnp.int32)] + [pltpu.VMEM((lines, 4 * buses), BF16)] * count),
        scratch_shapes=[pltpu.SemaphoreType.DMA((count, 4))],
        compiler_params=pltpu.CompilerParams(vmem_limit_bytes=LIMIT),
        cost_estimate=pl.CostEstimate(flops=0, bytes_accessed=8 * count * lines * buses, transcendentals=0),
        name="load_chunks",
    )(place, in_hbm(ptdf))
    return token, held


def flow_kernel(start, end, ptdf_ref, b0, b1, b2, b3, acc_ref, sum_ref, *rest):
    if end:
        limit_ref, line_ref, out_ref, half_ref, sum_out, inj_ref = rest
    else:
        out_ref, sum_out, inj_ref = rest
    buses = inj_ref.shape[0] // 4
    total = jnp.zeros(sum_ref.shape, F32) if start else sum_ref[...]
    for rel, ref in enumerate((b0, b1, b2, b3)):
        inj_ref[rel * buses : (rel + 1) * buses, :] = ref[:buses, :]
        tail = ref[buses:, :].astype(F32)
        total = total + jnp.sum(tail, axis=0, keepdims=True)
    sum_out[...] = total
    tile = ptdf_ref.shape[0] // 4

    def body(i, carry):
        rows = pl.ds(pl.multiple_of(i * tile, tile), tile)
        flow = dot(ptdf_ref[rows, :], inj_ref[...])
        if not start:
            flow = flow + acc_ref[rows, :]
        if end:
            shifted = line_ref[rows, :] + sigma_step * flow
            limit = limit_ref[rows, :]
            line = shifted - sigma_step * jnp.minimum(jnp.maximum(shifted / sigma_step, -limit), limit)
            out_ref[rows, :] = line
        else:
            out_ref[rows, :] = flow
        return carry

    lax.fori_loop(0, 4, body, 0)
    if end:
        half_ref[...] = out_ref[...].T.astype(BF16)


def flow_chunk(ptdf, blocks, acc, total, limit=None, line=None, weight=COST):
    lines = ptdf.shape[0]
    rows, hours = blocks[0].shape
    buses = rows - META
    start, end = acc is None, limit is not None
    operands = [ptdf, *blocks, total if start else acc, total]
    out_shape = [jax.ShapeDtypeStruct((lines, hours), F32)]
    if end:
        operands += [limit, line]
        out_shape += [jax.ShapeDtypeStruct((hours, lines), BF16)]
    out_shape += [jax.ShapeDtypeStruct((1, hours), F32)]
    return pl.pallas_call(
        functools.partial(flow_kernel, start, end),
        in_specs=[VMEM_SPEC] * len(operands),
        out_shape=tuple(out_shape),
        scratch_shapes=[pltpu.VMEM((4 * buses, hours), BF16)],
        compiler_params=pltpu.CompilerParams(vmem_limit_bytes=LIMIT),
        cost_estimate=chunk_cost(hours, lines, buses, weight),
        name="flow_chunk",
    )(*operands)


def swap(x, devices, mask):
    return lax.ppermute(x, "bus", [(i, i ^ mask) for i in range(devices)])


def local(
    ptdf,
    line_limit,
    gen_cost,
    gen_max,
    gen_owner,
    gen_local,
    availability,
    demand,
    dispatch,
    balance_price,
    line_price,
):
    devices = lax.axis_size("bus")
    place = lax.axis_index("bus").astype(jnp.int32).reshape(1)
    buses = demand.shape[0]
    all_buses = buses * devices
    gens, hours = dispatch.shape
    cap = -(-max(2, 3 * gens // devices) // 16) * 16
    staged = devices == 16 and buses % 128 == 0

    near_place = place if staged else jnp.zeros_like(place)
    outgoing, slot = pack(
        devices,
        cap,
        near_place,
        gen_owner,
        gen_local,
        gen_cost,
        dispatch,
        gen_max,
        availability,
    )
    limit = line_limit.reshape(-1, 1)
    balance_row = balance_price.reshape(1, hours)
    line_half = line_price if staged else line_price.astype(BF16)
    limit = line_limit.reshape(-1, 1)
    balance_row = balance_price.reshape(1, hours)
    line_half = line_price if staged else line_price.astype(BF16)
    recv = lax.all_to_all(outgoing, "bus", split_axis=0, concat_axis=0, tiled=True)
    held, resident, recv = None, {}, None
    for iteration in range(ITERS):
        last = iteration == ITERS - 1
        weight = 0 if last else COST
        if staged:
            line_t = line_half
            keeps, gots, crossed, parts = {}, {}, {}, {}

            def across(chunk):
                both = (keeps[chunk][1] + gots[chunk][1].astype(F32)).astype(BF16)
                crossed[chunk] = swap(both, devices, 2)
                return both

            def settle(chunk):
                part = keeps[chunk][0] + gots[chunk][0].astype(F32) + crossed[chunk].astype(F32)
                if chunk == 2:
                    part = part + parts[3].astype(F32)
                if chunk:
                    part = part.astype(BF16)
                    parts[chunk] = swap(part, devices, 8 if chunk == 2 else 4)
                else:
                    parts[chunk] = part
                return part

            def product(chunk, line_t):
                columns = resident.get(chunk, ptdf)
                keeps[chunk], send, *turned = shadow_chunk(
                    chunk, chunk not in resident, place, line_t, columns, buses
                )
                gots[chunk] = swap(send, devices, 1)
                return turned[0] if turned else line_t

            line_t = product(3, line_t)
            if iteration == 0:
                line_t, gots[3], outgoing = lax.optimization_barrier((line_t, gots[3], outgoing))
                outgoing, _ = lax.optimization_barrier((outgoing, across(3)))
                recv = lax.all_to_all(outgoing, "bus", split_axis=0, concat_axis=0, tiled=True)
                line_t, _ = lax.optimization_barrier((line_t, settle(3)))
                product(2, line_t)
            else:
                product(2, line_t)
                line_t, _ = lax.optimization_barrier((line_t, across(3)))
            product(1, line_t)
            line_t, _ = lax.optimization_barrier((line_t, across(2)))
            if iteration:
                line_t, _ = lax.optimization_barrier((line_t, settle(3)))
            product(0, line_t)
            gots[1], crossed[2] = lax.optimization_barrier((gots[1], crossed[2]))
            parts[3], _, _ = lax.optimization_barrier((parts[3], across(1), across(0)))
            crossed[1], _ = lax.optimization_barrier((crossed[1], settle(2)))
            settle(1)
            settle(0)
            prices = [parts[0], parts[1], parts[2]]
        else:
            recv = lax.all_to_all(outgoing, "bus", split_axis=0, concat_axis=0, tiled=True) if recv is None else recv
            shadow = lax.dot_general(ptdf, line_half, (((0,), (0,)), ((), ())), preferred_element_type=F32)
            prices = [lax.psum_scatter(shadow, "bus", scatter_dimension=0, tiled=True).T]
        chunks = (0,) if staged and not last else ()
        held, block, *loaded = update(
            cap, place if staged else near_place, last, prices, balance_row, demand, recv, held, ptdf, chunks
        )
        resident.update(zip(chunks, loaded))
        if staged:
            near, far, cross, far_cross = {0: block}, {}, {}, {}

            def spread(chunk):
                far[chunk] = swap(near[chunk], devices, 2)
                cross[chunk] = swap(near[chunk], devices, 1)

            def settle_far(chunk):
                far_cross[chunk] = swap(far[chunk], devices, 1)

            def blocks(chunk):
                return [near[chunk], cross[chunk], far[chunk], far_cross[chunk]]

            near[2] = swap(block, devices, 8)
            near[1] = swap(block, devices, 4)
            spread(0)
            stage = [near[1], near[2], far[0]]
            if last:
                home = held.reshape(4, 4, *held.shape[1:])
                stage += [swap(home[:, rel], devices, rel) for rel in (1, 2, 3)]
            else:
                cross[0], here = lax.optimization_barrier((cross[0], place))
                place, (resident[1], resident[2]) = load_chunks((1, 2), here, ptdf, buses)
                stage.append(place)
            near[1], near[2], far[0], *rest = lax.optimization_barrier(stage)
            near[3] = swap(near[2], devices, 4)
            spread(1)
            spread(2)
            settle_far(0)
            if last:
                home = jnp.stack([home[:, 0], *rest], axis=1)
                back = [home[0]] + [swap(home[chunk], devices, 4 * chunk) for chunk in (1, 2, 3)]
            else:
                (place,) = rest
            acc, total = flow_chunk(resident[0], blocks(0), None, balance_row, weight=weight)
            if not last:
                acc, here = lax.optimization_barrier((acc, place))
                place, (resident[3],) = load_chunks((3,), here, ptdf, buses)
            near[3], far[1], acc, place = lax.optimization_barrier((near[3], far[1], acc, place))
            spread(3)
            settle_far(1)
            if last:
                acc, *back = lax.optimization_barrier((acc, *back))
            acc, total = flow_chunk(resident[1], blocks(1), acc, total, weight=weight)
            settle_far(2)
            far[3], acc = lax.optimization_barrier((far[3], acc))
            settle_far(3)
            acc, total = flow_chunk(resident[2], blocks(2), acc, total, weight=weight)
            line_price, line_half, total = flow_chunk(
                resident[3], blocks(3), acc, total, limit, line_price, weight
            )
            if last:
                line_price, *back = lax.optimization_barrier((line_price, *back))
            balance = total
        else:
            if last:
                back = [lax.all_to_all(held, "bus", split_axis=0, concat_axis=0, tiled=True)]
            every = lax.all_gather(block, "bus", axis=0, tiled=False)
            balance = jnp.sum(every[:, buses:].astype(F32), axis=(0, 1)).reshape(1, hours)
            flow = jnp.dot(ptdf, every[:, :buses].reshape(all_buses, hours), preferred_element_type=F32)
            shifted = line_price + sigma_step * flow
            line_price = shifted - sigma_step * jnp.clip(shifted / sigma_step, -limit, limit)
            line_half = line_price.astype(BF16)
        balance_row = balance_row + sigma_step * balance / all_buses
    dispatch = unpack(slot, back, dispatch, gen_max.reshape(gens, 1), availability)
    return (dispatch, balance_row.reshape(hours), line_price)


def solution(mesh):
    return jax.shard_map(
        local,
        mesh=mesh,
        in_specs=(
            P("bus", None),
            P("bus"),
            P("bus"),
            P("bus"),
            P("bus", None),
            P("bus"),
            P(("cases", "bus"), None),
            P(("cases", "bus"), None),
            P(("cases", "bus"), None),
            P("cases"),
            P(("cases", "bus"), None),
        ),
        out_specs=(P(("cases", "bus"), None), P("cases"), P(("cases", "bus"), None)),
        check_vma=False,
    )
```

```python
import functools

import jax
import jax.numpy as jnp
from jax import lax
from jax.experimental import pallas as pl
from jax.experimental.pallas import tpu as pltpu
from jax.sharding import PartitionSpec as P

ITERS = 2

tau_step = 0.2
sigma_step = 0.15

GROUP = 4
LIMIT = 16 << 20
COST = 3
META = 16
HBM_SPEC = pl.BlockSpec(memory_space=pltpu.MemorySpace.HBM)
VMEM_SPEC = pl.BlockSpec(memory_space=pltpu.VMEM)
SMEM_SPEC = pl.BlockSpec(memory_space=pltpu.SMEM)
F32 = jnp.float32
BF16 = jnp.bfloat16
NT = (((1,), (1,)), ((), ()))
NN = (((1,), (0,)), ((), ()))


def dot(a, b, dims=NN):
    return lax.dot_general(a, b, dims, preferred_element_type=F32)


def halves(x):
    hi = x.astype(BF16)
    lo = (x - hi.astype(F32)).astype(BF16)
    return hi, lo


def thirds(x):
    hi = x.astype(BF16)
    rest = x - hi.astype(F32)
    mid = rest.astype(BF16)
    low = (rest - mid.astype(F32)).astype(BF16)
    return hi, mid, low


def as_row(ref):
    return jnp.concatenate([ref[i : i + 1, :] for i in range(ref.shape[0])], axis=1)


def pack_kernel(
    cap, devices, place_ref, owner_ref, local_ref, cost_ref, dispatch_ref, max_ref, avail_ref,
    out_ref, near_ref, slot_ref, pay_ref, meta_ref,
):
    step = pl.program_id(0)
    gens, hours = dispatch_ref.shape
    group = out_ref.shape[0]

    @pl.when(step == 0)
    def _():
        owner = owner_ref[...]
        hits = (lax.broadcasted_iota(jnp.int32, (devices, gens), 0) == owner).astype(F32)
        before = (
            lax.broadcasted_iota(jnp.int32, (gens, gens), 0) < lax.broadcasted_iota(jnp.int32, (gens, gens), 1)
        ).astype(F32)
        count = dot(hits.astype(BF16), before.astype(BF16))
        rank = jnp.sum(count * hits, axis=0, keepdims=True).astype(jnp.int32)
        slot_ref[...] = owner * cap + rank
        near_ref[...] = (owner ^ place_ref[0]) * cap + rank
        pay_ref[:, :hours] = dispatch_ref[...].astype(BF16)
        lanes = max_ref.shape[1]
        eye = (
            lax.broadcasted_iota(jnp.int32, (lanes, lanes), 0) == lax.broadcasted_iota(jnp.int32, (lanes, lanes), 1)
        ).astype(F32)
        for i in range(gens // lanes):
            rows = slice(i * lanes, (i + 1) * lanes)
            most = jnp.sum(eye * max_ref[i : i + 1, :], axis=1, keepdims=True)
            pay_ref[rows, hours:] = (most * avail_ref[rows, :]).astype(BF16)
        local = as_row(local_ref)
        hi, mid, low = thirds(as_row(cost_ref))
        row = lax.broadcasted_iota(jnp.int32, (META, gens), 0)
        parts = [
            (lax.shift_right_logical(local, 7) + 1).astype(F32),
            (local & 127).astype(F32),
            hi.astype(F32),
            mid.astype(F32),
            low.astype(F32),
        ]
        meta = jnp.zeros((META, gens), F32)
        for i, part in enumerate(parts):
            meta = jnp.where(row == i, part, meta)
        meta_ref[...] = meta.astype(BF16)

    slot = slot_ref[...] - step * (group * cap)
    place = lax.broadcasted_iota(jnp.int32, (cap, gens), 0)
    picks = [(place == slot - i * cap).astype(F32).astype(BF16) for i in range(group)]
    moved = dot(jnp.concatenate(picks, axis=0), pay_ref[...]).astype(BF16)
    for i in range(group):
        out_ref[i, :cap, :] = moved[i * cap : (i + 1) * cap]
        out_ref[i, cap:, :] = jnp.zeros((META, 2 * hours), BF16)
        out_ref[i, cap:, :cap] = dot(meta_ref[...], picks[i], NT).astype(BF16)


def pack(devices, cap, place, owner, local_bus, cost, dispatch, gen_max, availability):
    gens, hours = dispatch.shape
    full = lambda *shape: pl.BlockSpec(shape, lambda i: (0,) * len(shape))
    folded = (gens // 128, 128)
    return pl.pallas_call(
        functools.partial(pack_kernel, cap, devices),
        grid=(devices // GROUP,),
        out_shape=(
            jax.ShapeDtypeStruct((devices, cap + META, 2 * hours), BF16),
            jax.ShapeDtypeStruct((1, gens), jnp.int32),
        ),
        in_specs=[
            SMEM_SPEC,
            full(1, gens),
            full(*folded),
            full(*folded),
            full(gens, hours),
            full(*folded),
            full(gens, hours),
        ],
        out_specs=(pl.BlockSpec((GROUP, cap + META, 2 * hours), lambda i: (i, 0, 0)), full(1, gens)),
        scratch_shapes=[
            pltpu.VMEM((1, gens), jnp.int32),
            pltpu.VMEM((gens, 2 * hours), BF16),
            pltpu.VMEM((META, gens), BF16),
        ],
        compiler_params=pltpu.CompilerParams(vmem_limit_bytes=LIMIT),
        cost_estimate=pl.CostEstimate(flops=4 * devices * cap * gens * hours, bytes_accessed=3 << 20, transcendentals=0),
        name="pack_generators",
    )(
        place,
        owner.reshape(1, gens),
        local_bus.reshape(folded),
        cost.reshape(folded),
        dispatch,
        gen_max.reshape(folded),
        availability,
    )


def unpack_kernel(block, slot_ref, *refs):
    *back_refs, dispatch_ref, max_ref, avail_ref, out_ref, back_ref = refs
    peers, cap, _ = back_refs[0].shape
    for i, ref in enumerate(back_refs):
        for j in range(peers):
            start = (i * peers + j) * cap
            back_ref[start : start + cap, :] = ref[j]
    gens = slot_ref.shape[1]
    slot = jnp.broadcast_to(slot_ref[...].astype(F32), (128, gens)).T[:, 0:1].astype(jnp.int32)
    at = lax.broadcasted_iota(jnp.int32, (gens, block), 1)
    change = None
    for start in range(0, back_ref.shape[0], block):
        pick = (at == slot - start).astype(F32).astype(BF16)
        part = dot(pick, back_ref[start : start + block, :])
        change = part if change is None else change + part
    dispatch = dispatch_ref[...]
    upper = max_ref[...] * avail_ref[...]
    sent = dispatch.astype(BF16).astype(F32)
    to_upper = (upper.astype(BF16).astype(F32) - sent).astype(BF16).astype(F32)
    moved = jnp.minimum(jnp.maximum(dispatch + change, 0.0), upper)
    moved = jnp.where(change == to_upper, upper, moved)
    out_ref[...] = jnp.where(change == -sent, 0.0, moved)


def unpack(slot, backs, dispatch, gen_max, availability):
    gens = slot.shape[1]
    peers, cap, hours = backs[0].shape
    slots = len(backs) * peers * cap
    block = next(size for size in (768, 256, 128, 16) if slots % size == 0)
    return pl.pallas_call(
        functools.partial(unpack_kernel, block),
        out_shape=jax.ShapeDtypeStruct((gens, hours), F32),
        scratch_shapes=[pltpu.VMEM((slots, hours), BF16)],
        compiler_params=pltpu.CompilerParams(vmem_limit_bytes=LIMIT),
        cost_estimate=pl.CostEstimate(flops=2 * slots * gens * hours, bytes_accessed=1 << 20, transcendentals=0),
        name="unpack_dispatch",
    )(slot, *backs, dispatch, gen_max, availability)


def update_kernel(cap, devices, first, last, parts, chunks, place_ref, *refs):
    price_refs, refs = refs[:parts], refs[parts:]
    recv_ref, balance_ref, demand_ref, *refs = refs
    if not first:
        prev_ref, *refs = refs
    copies = []
    if chunks:
        ptdf_ref, upd_ref, inj_ref, *held_refs, shadow_ref, acc_ref, extra_ref, sems = refs
        copies = column_copies(place_ref, ptdf_ref, chunks, held_refs, sems)
    else:
        upd_ref, inj_ref, shadow_ref, acc_ref, extra_ref = refs
    for copy in copies:
        copy.start()
    buses, hours = demand_ref.shape
    wide = 2 * hours
    pad = extra_ref.shape[0] // devices
    shadow = price_refs[0][...].astype(F32)
    for ref in price_refs[1:]:
        shadow = shadow + ref[...].astype(F32)
    hi, lo = halves(shadow)
    shadow_ref[:hours, :] = hi
    shadow_ref[hours:, :] = lo
    eye = (
        lax.broadcasted_iota(jnp.int32, (cap, wide), 0) == lax.broadcasted_iota(jnp.int32, (cap, wide), 1)
    ).astype(F32)
    buses_at = lax.broadcasted_iota(jnp.int32, (cap, buses), 1)
    at_row = lax.broadcasted_iota(jnp.int32, (buses, pad), 0)
    for start in range(0, devices, GROUP):
        peers = range(start, start + GROUP)
        meta = jnp.concatenate([recv_ref[peer, cap:, :] for peer in peers], axis=0)
        columns = dot(eye.astype(BF16), meta, NT)
        picks = []
        for i in range(GROUP):
            at = i * META
            bus_column = ((columns[:, at : at + 1] - 1.0) * 128.0 + columns[:, at + 1 : at + 2]).astype(jnp.int32)
            picks.append((buses_at == bus_column).astype(F32).astype(BF16))
        both = dot(jnp.concatenate(picks, axis=0), shadow_ref[...], NT)
        for i, peer in enumerate(peers):
            at = i * META
            cost = (columns[:, at + 2 : at + 3] + columns[:, at + 3 : at + 4]) + columns[:, at + 4 : at + 5]
            rows = slice(i * cap, (i + 1) * cap)
            price = both[rows, :hours] + both[rows, hours:] + balance_ref[...]
            sent = recv_ref[peer, :cap, :hours].astype(F32)
            dispatch = sent if first else prev_ref[peer]
            upper = recv_ref[peer, :cap, hours:].astype(F32)
            updated = jnp.minimum(jnp.maximum(dispatch - tau_step * (cost + price), 0.0), upper)
            if last:
                upd_ref[peer ^ place_ref[0]] = (updated - sent).astype(BF16)
            else:
                upd_ref[peer] = updated
            hi, lo = halves(2.0 * updated - dispatch)
            extra_ref[peer * pad : peer * pad + cap, :hours] = hi
            extra_ref[peer * pad : peer * pad + cap, hours:] = lo
            if pad > cap:
                extra_ref[peer * pad + cap : (peer + 1) * pad, :] = jnp.zeros((pad - cap, wide), BF16)
        picks = []
        for peer in peers:
            row = recv_ref[peer, cap:, :pad].astype(F32)
            bus_row = ((row[0:1] - 1.0) * 128.0 + row[1:2]).astype(jnp.int32)
            picks.append((at_row == bus_row).astype(F32).astype(BF16))
        sums = dot(jnp.concatenate(picks, axis=1), extra_ref[start * pad : (start + GROUP) * pad, :])
        acc_ref[...] = sums if start == 0 else acc_ref[...] + sums
    injection = acc_ref[:, :hours] + acc_ref[:, hours:] - demand_ref[...]
    inj_ref[:buses, :] = injection.astype(BF16)
    hi, mid, low = thirds(jnp.sum(injection, axis=0, keepdims=True))
    row = lax.broadcasted_iota(jnp.int32, (META, hours), 0)
    tail = jnp.where(row == 0, hi.astype(F32), 0.0)
    tail = jnp.where(row == 1, mid.astype(F32), tail)
    tail = jnp.where(row == 2, low.astype(F32), tail)
    inj_ref[buses:, :] = tail.astype(BF16)
    for copy in copies:
        copy.wait()


def update(cap, place, last, prices, balance_price, demand, recv, previous, ptdf, chunks):
    devices = recv.shape[0]
    buses, hours = demand.shape
    first = previous is None
    operands = [place, *prices, recv, balance_price, demand] + ([] if first else [previous])
    in_specs = [SMEM_SPEC] + [VMEM_SPEC] * (len(operands) - 1)
    out_shape = [
        jax.ShapeDtypeStruct((devices, cap, hours), BF16 if last else F32),
        jax.ShapeDtypeStruct((buses + META, hours), BF16),
    ]
    scratch = [
        pltpu.VMEM((2 * hours, buses), BF16),
        pltpu.VMEM((buses, 2 * hours), F32),
        pltpu.VMEM((devices * (-(-cap // 128) * 128), 2 * hours), BF16),
    ]
    if chunks:
        operands.append(in_hbm(ptdf))
        in_specs.append(HBM_SPEC)
        out_shape += [pltpu.VMEM((ptdf.shape[0], 4 * buses), BF16)] * len(chunks)
        scratch.append(pltpu.SemaphoreType.DMA((len(chunks), 4)))
    return pl.pallas_call(
        functools.partial(update_kernel, cap, devices, first, last, len(prices), chunks),
        in_specs=in_specs,
        out_specs=tuple([VMEM_SPEC] * len(out_shape)),
        out_shape=tuple(out_shape),
        scratch_shapes=scratch,
        compiler_params=pltpu.CompilerParams(vmem_limit_bytes=LIMIT),
        cost_estimate=pl.CostEstimate(flops=8 * devices * cap * buses * hours, bytes_accessed=4 << 20, transcendentals=0),
        name="update_generators",
    )(*operands)


def shadow_kernel(chunk, stream, turn, place_ref, line_ref, ptdf_ref, keep_ref, send_ref, *rest):
    buses = keep_ref.shape[2]
    columns = [slice(rel * buses, (rel + 1) * buses) for rel in range(4)]
    if stream:
        if turn:
            line_t_ref, held_ref, sems, line_held_ref = rest
            line_copy = pltpu.make_async_copy(line_ref, line_held_ref, sems.at[4])
            line_copy.start()
        else:
            held_ref, sems = rest
        copies = []
        for rel in range(4):
            start = pl.multiple_of((place_ref[0] ^ (4 * chunk + rel)) * buses, 128)
            copies.append(
                pltpu.make_async_copy(
                    ptdf_ref.at[:, pl.ds(start, buses)], held_ref.at[:, columns[rel]], sems.at[rel]
                )
            )
        for rel in (3, 2, 1, 0):
            copies[rel].start()
        if turn:
            line_copy.wait()
            line_t_ref[...] = line_held_ref[...].T.astype(BF16)
            line_ref = line_t_ref
    else:
        held_ref = ptdf_ref

    def part(rel):
        if stream:
            copies[rel].wait()
        return dot(line_ref[...], held_ref[:, columns[rel]])

    send_ref[1] = part(3).astype(BF16)
    keep_ref[1] = part(2)
    send_ref[0] = part(1).astype(BF16)
    keep_ref[0] = part(0)


def in_hbm(x):
    return pltpu.with_memory_space_constraint(x, pltpu.MemorySpace.HBM)


def chunk_cost(hours, lines, buses, weight=COST):
    flops = max(1, 8 * weight) * hours * lines * buses
    return pl.CostEstimate(flops=flops, bytes_accessed=(8 if weight else 1) * lines * buses, transcendentals=0)


def shadow_chunk(chunk, stream, place, line, ptdf, buses):
    turn = line.dtype == F32
    lines, hours = line.shape if turn else line.shape[::-1]
    out_shape = [
        jax.ShapeDtypeStruct((2, hours, buses), F32),
        jax.ShapeDtypeStruct((2, hours, buses), BF16),
    ]
    scratch = [pltpu.VMEM((lines, 4 * buses), BF16), pltpu.SemaphoreType.DMA((5,))] if stream else []
    if turn:
        out_shape.append(jax.ShapeDtypeStruct((hours, lines), BF16))
        scratch.append(pltpu.VMEM((lines, hours), F32))
    return pl.pallas_call(
        functools.partial(shadow_kernel, chunk, stream, turn),
        in_specs=[SMEM_SPEC, HBM_SPEC if turn else VMEM_SPEC, HBM_SPEC if stream else VMEM_SPEC],
        out_specs=tuple([VMEM_SPEC] * len(out_shape)),
        out_shape=tuple(out_shape),
        scratch_shapes=scratch,
        compiler_params=pltpu.CompilerParams(vmem_limit_bytes=LIMIT),
        cost_estimate=chunk_cost(hours, lines, buses),
        name="shadow_chunk",
    )(place, in_hbm(line) if turn else line, in_hbm(ptdf) if stream else ptdf)


def column_copies(place_ref, ptdf_ref, chunks, held_refs, sems):
    buses = held_refs[0].shape[1] // 4
    copies = []
    for i, chunk in enumerate(chunks):
        for rel in range(4):
            start = pl.multiple_of((place_ref[0] ^ (4 * chunk + rel)) * buses, 128)
            copies.append(
                pltpu.make_async_copy(
                    ptdf_ref.at[:, pl.ds(start, buses)],
                    held_refs[i].at[:, pl.ds(rel * buses, buses)],
                    sems.at[i, rel],
                )
            )
    return copies


def load_kernel(chunks, place_ref, ptdf_ref, token_ref, *rest):
    *held_refs, sems = rest
    copies = column_copies(place_ref, ptdf_ref, chunks, held_refs, sems)
    for copy in copies:
        copy.start()
    token_ref[0] = place_ref[0]
    for copy in copies:
        copy.wait()


def load_chunks(chunks, place, ptdf, buses):
    lines = ptdf.shape[0]
    count = len(chunks)
    token, *held = pl.pallas_call(
        functools.partial(load_kernel, chunks),
        in_specs=[SMEM_SPEC, HBM_SPEC],
        out_specs=tuple([SMEM_SPEC] + [VMEM_SPEC] * count),
        out_shape=tuple([jax.ShapeDtypeStruct((1,), jnp.int32)] + [pltpu.VMEM((lines, 4 * buses), BF16)] * count),
        scratch_shapes=[pltpu.SemaphoreType.DMA((count, 4))],
        compiler_params=pltpu.CompilerParams(vmem_limit_bytes=LIMIT),
        cost_estimate=pl.CostEstimate(flops=0, bytes_accessed=8 * count * lines * buses, transcendentals=0),
        name="load_chunks",
    )(place, in_hbm(ptdf))
    return token, held


def flow_kernel(start, end, ptdf_ref, b0, b1, b2, b3, acc_ref, sum_ref, *rest):
    if end:
        limit_ref, line_ref, out_ref, half_ref, sum_out, inj_ref = rest
    else:
        out_ref, sum_out, inj_ref = rest
    buses = inj_ref.shape[0] // 4
    total = jnp.zeros(sum_ref.shape, F32) if start else sum_ref[...]
    for rel, ref in enumerate((b0, b1, b2, b3)):
        inj_ref[rel * buses : (rel + 1) * buses, :] = ref[:buses, :]
        tail = ref[buses:, :].astype(F32)
        total = total + jnp.sum(tail, axis=0, keepdims=True)
    sum_out[...] = total
    tile = ptdf_ref.shape[0] // 4

    def body(i, carry):
        rows = pl.ds(pl.multiple_of(i * tile, tile), tile)
        flow = dot(ptdf_ref[rows, :], inj_ref[...])
        if not start:
            flow = flow + acc_ref[rows, :]
        if end:
            shifted = line_ref[rows, :] + sigma_step * flow
            limit = limit_ref[rows, :]
            line = shifted - sigma_step * jnp.minimum(jnp.maximum(shifted / sigma_step, -limit), limit)
            out_ref[rows, :] = line
        else:
            out_ref[rows, :] = flow
        return carry

    lax.fori_loop(0, 4, body, 0)
    if end:
        half_ref[...] = out_ref[...].T.astype(BF16)


def flow_chunk(ptdf, blocks, acc, total, limit=None, line=None, weight=COST):
    lines = ptdf.shape[0]
    rows, hours = blocks[0].shape
    buses = rows - META
    start, end = acc is None, limit is not None
    operands = [ptdf, *blocks, total if start else acc, total]
    out_shape = [jax.ShapeDtypeStruct((lines, hours), F32)]
    if end:
        operands += [limit, line]
        out_shape += [jax.ShapeDtypeStruct((hours, lines), BF16)]
    out_shape += [jax.ShapeDtypeStruct((1, hours), F32)]
    return pl.pallas_call(
        functools.partial(flow_kernel, start, end),
        in_specs=[VMEM_SPEC] * len(operands),
        out_shape=tuple(out_shape),
        scratch_shapes=[pltpu.VMEM((4 * buses, hours), BF16)],
        compiler_params=pltpu.CompilerParams(vmem_limit_bytes=LIMIT),
        cost_estimate=chunk_cost(hours, lines, buses, weight),
        name="flow_chunk",
    )(*operands)


def swap(x, devices, mask):
    return lax.ppermute(x, "bus", [(i, i ^ mask) for i in range(devices)])


def local(
    ptdf,
    line_limit,
    gen_cost,
    gen_max,
    gen_owner,
    gen_local,
    availability,
    demand,
    dispatch,
    balance_price,
    line_price,
):
    devices = lax.axis_size("bus")
    place = lax.axis_index("bus").astype(jnp.int32).reshape(1)
    buses = demand.shape[0]
    all_buses = buses * devices
    gens, hours = dispatch.shape
    cap = -(-max(2, 3 * gens // devices) // 16) * 16
    staged = devices == 16 and buses % 128 == 0

    near_place = place if staged else jnp.zeros_like(place)
    outgoing, slot = pack(
        devices,
        cap,
        near_place,
        gen_owner,
        gen_local,
        gen_cost,
        dispatch,
        gen_max,
        availability,
    )
    limit = line_limit.reshape(-1, 1)
    balance_row = balance_price.reshape(1, hours)
    line_half = line_price if staged else line_price.astype(BF16)
    limit = line_limit.reshape(-1, 1)
    balance_row = balance_price.reshape(1, hours)
    line_half = line_price if staged else line_price.astype(BF16)
    recv = lax.all_to_all(outgoing, "bus", split_axis=0, concat_axis=0, tiled=True)
    held, resident, recv = None, {}, None
    for iteration in range(ITERS):
        last = iteration == ITERS - 1
        weight = 0 if last else COST
        if staged:
            line_t = line_half
            keeps, gots, crossed, parts = {}, {}, {}, {}

            def across(chunk):
                both = (keeps[chunk][1] + gots[chunk][1].astype(F32)).astype(BF16)
                crossed[chunk] = swap(both, devices, 2)
                return both

            def settle(chunk):
                part = keeps[chunk][0] + gots[chunk][0].astype(F32) + crossed[chunk].astype(F32)
                if chunk == 2:
                    part = part + parts[3].astype(F32)
                if chunk:
                    part = part.astype(BF16)
                    parts[chunk] = swap(part, devices, 8 if chunk == 2 else 4)
                else:
                    parts[chunk] = part
                return part

            def product(chunk, line_t):
                columns = resident.get(chunk, ptdf)
                keeps[chunk], send, *turned = shadow_chunk(
                    chunk, chunk not in resident, place, line_t, columns, buses
                )
                gots[chunk] = swap(send, devices, 1)
                return turned[0] if turned else line_t

            line_t = product(3, line_t)
            if iteration == 0:
                line_t, gots[3], outgoing = lax.optimization_barrier((line_t, gots[3], outgoing))
                outgoing, _ = lax.optimization_barrier((outgoing, across(3)))
                recv = lax.all_to_all(outgoing, "bus", split_axis=0, concat_axis=0, tiled=True)
                line_t, _ = lax.optimization_barrier((line_t, settle(3)))
                product(2, line_t)
            else:
                product(2, line_t)
                line_t, _ = lax.optimization_barrier((line_t, across(3)))
            product(1, line_t)
            line_t, _ = lax.optimization_barrier((line_t, across(2)))
            if iteration:
                line_t, _ = lax.optimization_barrier((line_t, settle(3)))
            product(0, line_t)
            gots[1], crossed[2] = lax.optimization_barrier((gots[1], crossed[2]))
            parts[3], _, _ = lax.optimization_barrier((parts[3], across(1), across(0)))
            crossed[1], _ = lax.optimization_barrier((crossed[1], settle(2)))
            settle(1)
            settle(0)
            prices = [parts[0], parts[1], parts[2]]
        else:
            recv = lax.all_to_all(outgoing, "bus", split_axis=0, concat_axis=0, tiled=True) if recv is None else recv
            shadow = lax.dot_general(ptdf, line_half, (((0,), (0,)), ((), ())), preferred_element_type=F32)
            prices = [lax.psum_scatter(shadow, "bus", scatter_dimension=0, tiled=True).T]
        chunks = (0,) if staged and not last else ()
        held, block, *loaded = update(
            cap, place if staged else near_place, last, prices, balance_row, demand, recv, held, ptdf, chunks
        )
        resident.update(zip(chunks, loaded))
        if staged:
            near, far, cross, far_cross = {0: block}, {}, {}, {}

            def spread(chunk):
                far[chunk] = swap(near[chunk], devices, 2)
                cross[chunk] = swap(near[chunk], devices, 1)

            def settle_far(chunk):
                far_cross[chunk] = swap(far[chunk], devices, 1)

            def blocks(chunk):
                return [near[chunk], cross[chunk], far[chunk], far_cross[chunk]]

            near[2] = swap(block, devices, 8)
            near[1] = swap(block, devices, 4)
            spread(0)
            stage = [near[1], near[2], far[0]]
            if last:
                home = held.reshape(4, 4, *held.shape[1:])
                stage += [swap(home[:, rel], devices, rel) for rel in (1, 2, 3)]
            else:
                cross[0], here = lax.optimization_barrier((cross[0], place))
                place, (resident[1], resident[2]) = load_chunks((1, 2), here, ptdf, buses)
                stage.append(place)
            near[1], near[2], far[0], *rest = lax.optimization_barrier(stage)
            near[3] = swap(near[2], devices, 4)
            spread(1)
            spread(2)
            settle_far(0)
            if last:
                home = jnp.stack([home[:, 0], *rest], axis=1)
                back = [home[0]] + [swap(home[chunk], devices, 4 * chunk) for chunk in (1, 2, 3)]
            else:
                (place,) = rest
            acc, total = flow_chunk(resident[0], blocks(0), None, balance_row, weight=weight)
            if not last:
                acc, here = lax.optimization_barrier((acc, place))
                place, (resident[3],) = load_chunks((3,), here, ptdf, buses)
            near[3], far[1], acc, place = lax.optimization_barrier((near[3], far[1], acc, place))
            spread(3)
            settle_far(1)
            if last:
                acc, *back = lax.optimization_barrier((acc, *back[::-1]))
                back = back[::-1]
            acc, total = flow_chunk(resident[1], blocks(1), acc, total, weight=weight)
            settle_far(2)
            far[3], acc = lax.optimization_barrier((far[3], acc))
            settle_far(3)
            acc, total = flow_chunk(resident[2], blocks(2), acc, total, weight=weight)
            line_price, line_half, total = flow_chunk(
                resident[3], blocks(3), acc, total, limit, line_price, weight
            )
            if last:
                line_price, *back = lax.optimization_barrier((line_price, *back))
            balance = total
        else:
            if last:
                back = [lax.all_to_all(held, "bus", split_axis=0, concat_axis=0, tiled=True)]
            every = lax.all_gather(block, "bus", axis=0, tiled=False)
            balance = jnp.sum(every[:, buses:].astype(F32), axis=(0, 1)).reshape(1, hours)
            flow = jnp.dot(ptdf, every[:, :buses].reshape(all_buses, hours), preferred_element_type=F32)
            shifted = line_price + sigma_step * flow
            line_price = shifted - sigma_step * jnp.clip(shifted / sigma_step, -limit, limit)
            line_half = line_price.astype(BF16)
        balance_row = balance_row + sigma_step * balance / all_buses
    dispatch = unpack(slot, back, dispatch, gen_max.reshape(gens, 1), availability)
    return (dispatch, balance_row.reshape(hours), line_price)


def solution(mesh):
    return jax.shard_map(
        local,
        mesh=mesh,
        in_specs=(
            P("bus", None),
            P("bus"),
            P("bus"),
            P("bus"),
            P("bus", None),
            P("bus"),
            P(("cases", "bus"), None),
            P(("cases", "bus"), None),
            P(("cases", "bus"), None),
            P("cases"),
            P(("cases", "bus"), None),
        ),
        out_specs=(P(("cases", "bus"), None), P("cases"), P(("cases", "bus"), None)),
        check_vma=False,
    )
```
